32 devices in a mesh: dp: 8 (over y, x, core), tensor: 4 (over z).
Axes of the slice: x: 2, y: 2, z: 4, core: 2. Of those that a mesh axis runs over, the one named last changes fastest.
Arguments:
- inputs: bfloat16 [1024, 8192], P('dp', 'tensor'), may hold values from -6 to 6
- out_grad: bfloat16 [1024, 8192], P('dp', 'tensor'), may hold values from -6 to 6
- weights: bfloat16 [3, 384, 128, 128], P(None, 'tensor'), may hold values from -0.1875 to 0.1875
- block_index: int32 [3, 384, 2], P(None, 'tensor'), may hold values from 0 to 63, as said below
- block_counts: int32 [4, 3], P('tensor'), may hold values from 38 to 96, as said below
- first_moment: float32 [3, 384, 128, 128], P(None, ('tensor', 'dp')), may hold values from -120 to 120
- second_moment: float32 [3, 384, 128, 128], P(None, ('tensor', 'dp')), may hold values from 100 to 10000
Outputs:
- outputs: bfloat16 [1024, 8192], P('dp', 'tensor')
- input_grad: bfloat16 [1024, 8192], P('dp', 'tensor')
- update: float32 [3, 384, 128, 128], P(None, ('tensor', 'dp'))
The draws below stay inside these ranges and needn't reach their ends.
Inputs may be any that keep to these rules, and one draw needn't show every extreme that they name: block_index[k, t * 96 + j, 0] is a feature block (below 64) and block_index[k, t * 96 + j, 1] a hidden block of tensor index t (below 14); the 96 slots of one matrix on one tensor index name distinct blocks. block_counts[t, k] live slots of matrix k on tensor index t; for each matrix some tensor index has exactly 96.
All inputs are finite; a program needn't handle non-finite values.
Results may differ from the reference program's by a relative error of at most 0.013.
Values may be sent and summed in bfloat16 or wider, within the bound.
No kernel may reach another device: no remote copies, remote signals or barrier semaphores. Data moves between devices by JAX's collectives and lax.ppermute only.
A program may use at most 128 MiB of HBM per device.

```python
import math
import jax
import jax.numpy as jnp
from jax import lax

D = 8192
BLK = 128
DBLK = 64
HB_DEV = 14
CAP = 96
TOK_DEV = 128
TOKENS = 1024
N_DP = 8
N_TENSOR = 4


def shuffled_blocks(device_key):
    position_count = DBLK * HB_DEV
    shuffled = jax.random.permutation(device_key, position_count)[:CAP]
    positions = (shuffled + (position_count - 1 - shuffled[0])) % position_count
    return jnp.stack([positions // HB_DEV, positions % HB_DEV], axis=-1).astype(jnp.int32)


def draw_block_index(key, part):
    device_keys = jax.random.split(jax.random.fold_in(key, 11), 3 * N_TENSOR)
    return jax.vmap(shuffled_blocks)(device_keys).reshape(3, N_TENSOR * CAP, 2)


def draw_block_counts(key, part):
    count_key = jax.random.fold_in(key, 23)
    counts_drawn = jax.random.randint(jax.random.fold_in(count_key, 1), (N_TENSOR, 3), CAP * 2 // 5, CAP + 1)
    fullest = jax.random.randint(jax.random.fold_in(count_key, 2), (3,), 0, N_TENSOR)
    fullest_rows = jnp.arange(N_TENSOR)[:, None] == fullest[None, :]
    return jnp.where(fullest_rows, CAP, counts_drawn).astype(jnp.int32)


def block_scale(rng, extent, pieces, least, largest):
    loudness, own = 1.0, jax.random.fold_in(rng, 6)
    for dim, shards_of in pieces:
        heights = jnp.exp(jax.random.uniform(jax.random.fold_in(own, dim), (shards_of,), jnp.float32, least / len(pieces), largest / len(pieces)))
        loudness = loudness * jnp.repeat(heights, extent[dim] // shards_of).reshape([-1 if axis == dim else 1 for axis in range(len(extent))])
    return loudness


def gaussian(stream_key, extent, scale, reach, shards=(), held_as=jnp.bfloat16):
    factor_of = block_scale(stream_key, extent, shards, -0.22, 0.18) if shards else 1.0
    result = jax.random.normal(stream_key, extent, jnp.float32) * scale * factor_of
    return jnp.minimum(jnp.maximum(result, -reach), reach).astype(held_as)


def setup_inputs(seed: int = 0) -> dict:
    splits = jax.random.split(jax.random.key(seed), 8)
    inputs = gaussian(splits[0], (TOKENS, D), 1.0, 6.0, ((0, 8), (1, 4)))
    out_grad = gaussian(splits[1], (TOKENS, D), 1.0, 6.0, ((0, 8), (1, 4)))
    weights = gaussian(splits[2], (3, N_TENSOR * CAP, BLK, BLK), (D // 8) ** -0.5, 0.1875, ((1, 4),))
    block_index = draw_block_index(jax.random.fold_in(splits[7], 71), 0)
    block_counts = draw_block_counts(jax.random.fold_in(splits[7], 71), 0)
    first_moment = gaussian(splits[5], (3, N_TENSOR * CAP, BLK, BLK), 20.0, 120.0, ((1, 32),), jnp.float32)
    second_moment = jnp.clip(jnp.exp(math.log(10000.0) - 4.6051702 * jax.random.uniform(splits[6], (3, N_TENSOR * CAP, BLK, BLK), jnp.float32) ** block_scale(splits[6], (3, N_TENSOR * CAP, BLK, BLK), ((1, 32),), -0.2, 0.2)), 100.0, 10000.0)
    return dict(inputs=inputs, out_grad=out_grad, weights=weights, block_index=block_index, block_counts=block_counts, first_moment=first_moment, second_moment=second_moment)


EPSILON = 1e-08

def reference(inputs, out_grad, weights, block_index, block_counts, first_moment, second_moment):
    input_blocks = inputs.reshape(TOKENS, DBLK, BLK)
    cotangent_blocks = out_grad.reshape(TOKENS, DBLK, BLK)
    device_weights = weights.reshape(3, N_TENSOR, CAP, BLK, BLK).transpose(1, 0, 2, 3, 4)
    device_index = block_index.reshape(3, N_TENSOR, CAP, 2).transpose(1, 0, 2, 3)
    first_prev = first_moment.reshape(3, N_TENSOR, CAP, BLK, BLK).transpose(1, 0, 2, 3, 4)
    second_prev = second_moment.reshape(3, N_TENSOR, CAP, BLK, BLK).transpose(1, 0, 2, 3, 4)
    slot_ids = jnp.arange(CAP, dtype=jnp.int32)
    hidden_ids = jnp.arange(HB_DEV, dtype=jnp.int32)
    feature_ids = jnp.arange(DBLK, dtype=jnp.int32)

    def replica_sum(left_rows, right_rows):
        left_rows = left_rows.reshape(N_DP, TOK_DEV, CAP, BLK)
        right_rows = right_rows.reshape(N_DP, TOK_DEV, CAP, BLK)
        replica_terms = jnp.einsum('rtsk,rtsn->rskn', left_rows, right_rows)
        replica_terms = lax.optimization_barrier(replica_terms.astype(jnp.bfloat16)).astype(jnp.float32)
        return lax.optimization_barrier(jnp.sum(replica_terms, axis=0))

    def per_device(running, device_items):
        out_sum, in_sum = running
        block_values, index_here, counts_here, first_here, second_here = device_items
        live_slots = (slot_ids[None, :] < counts_here[:, None]).astype(jnp.float32)
        hidden_select = (index_here[:, :, 1, None] == hidden_ids).astype(jnp.float32) * live_slots[:, :, None]
        feature_select = (index_here[:, :, 0, None] == feature_ids).astype(jnp.float32) * live_slots[:, :, None]
        values_wide = block_values.astype(jnp.float32)
        gate_inputs = input_blocks[:, index_here[0, :, 0], :].astype(jnp.float32)
        up_inputs = input_blocks[:, index_here[1, :, 0], :].astype(jnp.float32)
        gate_proj = jnp.einsum('tsn,sh->thn', jnp.einsum('tsk,skn->tsn', gate_inputs, values_wide[0]), hidden_select[0])
        up_proj = jnp.einsum('tsn,sh->thn', jnp.einsum('tsk,skn->tsn', up_inputs, values_wide[1]), hidden_select[1])
        sigmoid_gate = jax.nn.sigmoid(gate_proj)
        activated = gate_proj * sigmoid_gate
        hidden = (activated * up_proj).astype(jnp.bfloat16)
        down_inputs = hidden[:, index_here[2, :, 1], :].astype(jnp.float32)
        out_partial = jnp.einsum('tsn,sf->tfn', jnp.einsum('tsk,skn->tsn', down_inputs, values_wide[2]), feature_select[2])
        out_partial = out_partial.reshape(TOKENS, D)
        out_sum = out_sum + lax.optimization_barrier(out_partial.astype(jnp.bfloat16)).astype(jnp.float32)
        down_cotangents = cotangent_blocks[:, index_here[2, :, 0], :].astype(jnp.float32)
        hidden_grad = jnp.einsum('tsk,sh->thk', jnp.einsum('tsn,skn->tsk', down_cotangents, values_wide[2]), hidden_select[2])
        gate_grad_rows = (hidden_grad * up_proj * sigmoid_gate * (1.0 + gate_proj * (1.0 - sigmoid_gate))).astype(jnp.bfloat16)
        up_grad_rows = (hidden_grad * activated).astype(jnp.bfloat16)
        gate_back = gate_grad_rows[:, index_here[0, :, 1], :].astype(jnp.float32)
        up_back = up_grad_rows[:, index_here[1, :, 1], :].astype(jnp.float32)
        in_partial = jnp.einsum('tsk,sf->tfk', jnp.einsum('tsn,skn->tsk', gate_back, values_wide[0]), feature_select[0])
        in_partial = in_partial + jnp.einsum('tsk,sf->tfk', jnp.einsum('tsn,skn->tsk', up_back, values_wide[1]), feature_select[1])
        in_partial = in_partial.reshape(TOKENS, D)
        in_sum = in_sum + lax.optimization_barrier(in_partial.astype(jnp.bfloat16)).astype(jnp.float32)
        gradients = jnp.stack([replica_sum(gate_inputs, gate_back), replica_sum(up_inputs, up_back), replica_sum(down_inputs, down_cotangents)])
        gradients = gradients * live_slots[:, :, None, None]
        first_new = 0.9 * first_here + 0.1 * gradients
        second_new = 0.95 * second_here + 0.05 * gradients * gradients
        update = live_slots[:, :, None, None] * first_new / (jnp.sqrt(second_new) + EPSILON)
        return ((out_sum, in_sum), update)
    zero_sums = jnp.zeros((TOKENS, D), jnp.float32)
    results, updates = lax.scan(per_device, (zero_sums, zero_sums), (device_weights, device_index, block_counts, first_prev, second_prev))
    update = updates.transpose(1, 0, 2, 3, 4).reshape(3, N_TENSOR * CAP, BLK, BLK)
    return (results[0].astype(jnp.bfloat16), results[1].astype(jnp.bfloat16), update)
```

```python
import functools
import jax
import jax.numpy as jnp
from jax import lax
from jax.experimental import pallas as pl
from jax.experimental.pallas import tpu as pltpu
from jax.sharding import PartitionSpec as P

HB_DEV = 14
EPSILON = 1e-08
GROUP = 8
VMEM_LIMIT = 56 * 1024 * 1024


def group_of(capacity):
    return next(g for g in (GROUP, 4, 2, 1) if capacity % g == 0)


def feature_block(ref, block, size):
    per_shard = ref.shape[2] // size
    start = pl.multiple_of(lax.rem(block, per_shard) * size, size)
    return ref.at[lax.div(block, per_shard), :, pl.ds(start, size)]


def slot_pair(index_ref, matrix, slot, capacity):
    at = (matrix * capacity + slot) * 2
    return index_ref[at], index_ref[at + 1]


def each_group(count, group, body):
    def step(i, carry):
        body([i * group + u for u in range(group)])
        return carry

    lax.fori_loop(0, lax.div(count + (group - 1), group), step, 0)


def dot(a, b, contract):
    return lax.dot_general(a, b, ((contract[0], contract[1]), ((), ())), preferred_element_type=jnp.float32)


def forward_kernel(index_ref, count_ref, x_ref, w_ref, hidden_ref, act_ref, slope_ref, out_ref, gate, up, total):
    capacity, size = w_ref.shape[1], w_ref.shape[2]
    group = group_of(capacity)
    hidden_blocks = hidden_ref.shape[0]
    feature_blocks = x_ref.shape[0] * (x_ref.shape[2] // size)
    gate[...] = jnp.zeros_like(gate)
    up[...] = jnp.zeros_like(up)
    total[...] = jnp.zeros_like(total)
    for matrix, acc in ((0, gate), (1, up)):
        count = count_ref[matrix]

        def project(slots, matrix=matrix, acc=acc, count=count):
            products, targets = [], []
            for s in slots:
                f, h = slot_pair(index_ref, matrix, s, capacity)
                targets.append(jnp.where(s < count, h, hidden_blocks))
                products.append(dot(feature_block(x_ref, f, size)[...], w_ref[matrix, s], ((1,), (0,))))
            for h, p in zip(targets, products):
                acc[h] += p

        each_group(count, group, project)
    for h in range(hidden_blocks):
        g, u = gate[h], up[h]
        sig = 1.0 / (1.0 + jnp.exp(-g))
        act = g * sig
        act_ref[h] = act
        slope_ref[h] = u * sig * (1.0 + g * (1.0 - sig))
        hidden_ref[h] = (act * u).astype(hidden_ref.dtype)
    count = count_ref[2]

    def down(slots):
        products, targets = [], []
        for s in slots:
            f, h = slot_pair(index_ref, 2, s, capacity)
            targets.append(jnp.where(s < count, f, feature_blocks))
            products.append(dot(hidden_ref[h], w_ref[2, s], ((1,), (0,))))
        for f, p in zip(targets, products):
            total[f] += p

    each_group(count, group, down)
    for f in range(feature_blocks):
        feature_block(out_ref, f, size)[...] = total[f].astype(out_ref.dtype)


def rows_kernel(index_ref, count_ref, og_ref, w_ref, act_ref, slope_ref, gate_rows_ref, up_rows_ref, acc):
    capacity, size = w_ref.shape[1], w_ref.shape[2]
    group = group_of(capacity)
    hidden_blocks = act_ref.shape[0]
    acc[...] = jnp.zeros_like(acc)
    count = count_ref[2]

    def back(slots):
        products, targets = [], []
        for s in slots:
            f, h = slot_pair(index_ref, 2, s, capacity)
            targets.append(jnp.where(s < count, h, hidden_blocks))
            products.append(dot(feature_block(og_ref, f, size)[...], w_ref[2, s], ((1,), (1,))))
        for h, p in zip(targets, products):
            acc[h] += p

    each_group(count, group, back)
    for h in range(hidden_blocks):
        gate_rows_ref[h] = (acc[h] * slope_ref[h]).astype(gate_rows_ref.dtype)
        up_rows_ref[h] = (acc[h] * act_ref[h]).astype(up_rows_ref.dtype)


def grad_kernel(index_ref, count_ref, x_ref, og_ref, hidden_ref, gate_rows_ref, up_rows_ref, grad_ref):
    size = grad_ref.shape[2]
    share = grad_ref.shape[1]
    group = group_of(share)
    matrix, part = pl.program_id(0), pl.program_id(1)
    capacity = share * pl.num_programs(1)
    first = part * share
    live = jnp.clip(count_ref[matrix] - first, 0, share)

    def run(left, right):
        def body(slots):
            for s in slots:
                f, h = slot_pair(index_ref, matrix, first + s, capacity)
                grad_ref[0, s] = dot(left(f, h), right(f, h), ((0,), (0,))).astype(grad_ref.dtype)

        each_group(live, group, body)

    @pl.when(matrix == 0)
    def _():
        run(lambda f, h: feature_block(x_ref, f, size)[...], lambda f, h: gate_rows_ref[h])

    @pl.when(matrix == 1)
    def _():
        run(lambda f, h: feature_block(x_ref, f, size)[...], lambda f, h: up_rows_ref[h])

    @pl.when(matrix == 2)
    def _():
        run(lambda f, h: hidden_ref[h], lambda f, h: feature_block(og_ref, f, size)[...])


def input_kernel(index_ref, count_ref, gate_rows_ref, up_rows_ref, w_ref, out_ref, total):
    capacity, size = w_ref.shape[1], w_ref.shape[2]
    group = group_of(capacity)
    feature_blocks = out_ref.shape[0] * (out_ref.shape[2] // size)
    total[...] = jnp.zeros_like(total)
    for matrix, rows in ((0, gate_rows_ref), (1, up_rows_ref)):
        count = count_ref[matrix]

        def back(slots, matrix=matrix, rows=rows, count=count):
            products, targets = [], []
            for s in slots:
                f, h = slot_pair(index_ref, matrix, s, capacity)
                targets.append(jnp.where(s < count, f, feature_blocks))
                products.append(dot(rows[h], w_ref[matrix, s], ((1,), (1,))))
            for f, p in zip(targets, products):
                total[f] += p

        each_group(count, group, back)
    for f in range(feature_blocks):
        feature_block(out_ref, f, size)[...] = total[f].astype(out_ref.dtype)


SMEM = pl.BlockSpec(memory_space=pltpu.SMEM)
VMEM = pl.BlockSpec(memory_space=pltpu.VMEM)


def call(kernel, name, outs, scratch, *operands):
    return pl.pallas_call(
        kernel,
        name=name,
        out_shape=outs,
        in_specs=[SMEM, SMEM] + [VMEM] * (len(operands) - 2),
        out_specs=jax.tree.map(lambda _: VMEM, outs),
        scratch_shapes=scratch,
        compiler_params=pltpu.CompilerParams(vmem_limit_bytes=VMEM_LIMIT),
    )(*operands)


def forward(index, counts, x, w):
    shards, rows, width = x.shape
    size = w.shape[2]
    f32, bf16 = jnp.float32, jnp.bfloat16
    wide = jax.ShapeDtypeStruct((HB_DEV, rows, size), f32)
    outs = (
        jax.ShapeDtypeStruct((HB_DEV, rows, size), bf16),
        wide,
        wide,
        jax.ShapeDtypeStruct(x.shape, bf16),
    )
    acc = pltpu.VMEM((HB_DEV + 1, rows, size), f32)
    total = pltpu.VMEM((shards * width // size + 1, rows, size), f32)
    return call(forward_kernel, "forward", outs, [acc, acc, total], index, counts, x, w)


def row_grads(index, counts, og, w, act, slope):
    rows = og.shape[1]
    size = w.shape[2]
    out = jax.ShapeDtypeStruct((HB_DEV, rows, size), jnp.bfloat16)
    acc = pltpu.VMEM((HB_DEV + 1, rows, size), jnp.float32)
    return call(rows_kernel, "row_grads", (out, out), [acc], index, counts, og, w, act, slope)


def block_grads(index, counts, x, og, hidden, gate_rows, up_rows, capacity):
    size = hidden.shape[2]
    parts = next(p for p in (4, 3, 2, 1) if capacity % p == 0)
    return pl.pallas_call(
        grad_kernel,
        name="block_grads",
        grid=(3, parts),
        out_shape=jax.ShapeDtypeStruct((3, capacity, size, size), jnp.bfloat16),
        in_specs=[SMEM, SMEM] + [VMEM] * 5,
        out_specs=pl.BlockSpec((1, capacity // parts, size, size), lambda k, p: (k, p, 0, 0)),
        compiler_params=pltpu.CompilerParams(vmem_limit_bytes=VMEM_LIMIT),
    )(index, counts, x, og, hidden, gate_rows, up_rows)


def input_grads(index, counts, gate_rows, up_rows, w, like):
    rows, size = gate_rows.shape[1], w.shape[2]
    total = pltpu.VMEM((like.shape[0] * like.shape[2] // size + 1, rows, size), jnp.float32)
    return call(
        input_kernel, "input_grads", jax.ShapeDtypeStruct(like.shape, jnp.bfloat16), [total],
        index, counts, gate_rows, up_rows, w,
    )


def local(inputs, out_grad, weights, block_index, block_counts, first_moment, second_moment):
    capacity = weights.shape[1]
    index = block_index.reshape(-1)
    counts = block_counts[0]
    x = lax.all_gather(inputs, "tensor", axis=0)
    og = lax.all_gather(out_grad, "tensor", axis=0)
    hidden, act, slope, out_partial = forward(index, counts, x, weights)
    outputs = lax.psum_scatter(out_partial, "tensor", scatter_dimension=0)
    gate_rows, up_rows = row_grads(index, counts, og, weights, act, slope)
    grads = block_grads(index, counts, x, og, hidden, gate_rows, up_rows, capacity)
    shares = lax.psum_scatter(grads, "dp", scatter_dimension=1, tiled=True).astype(jnp.float32)
    input_partial = input_grads(index, counts, gate_rows, up_rows, weights, x)
    input_grad = lax.psum_scatter(input_partial, "tensor", scatter_dimension=0)
    share_rows = shares.shape[1]
    share_ids = lax.axis_index("dp") * share_rows + jnp.arange(share_rows, dtype=jnp.int32)
    live = (share_ids[None, :] < counts[:, None])[:, :, None, None]
    first_new = 0.9 * first_moment + 0.1 * shares
    second_new = 0.95 * second_moment + 0.05 * shares * shares
    update = jnp.where(live, first_new / (jnp.sqrt(second_new) + EPSILON), 0.0)
    return (outputs, input_grad, update)


def solution(mesh):
    in_specs = (
        P("dp", "tensor"),
        P("dp", "tensor"),
        P(None, "tensor", None, None),
        P(None, "tensor", None),
        P("tensor", None),
        P(None, ("tensor", "dp"), None, None),
        P(None, ("tensor", "dp"), None, None),
    )
    out_specs = (P("dp", "tensor"), P("dp", "tensor"), P(None, ("tensor", "dp"), None, None))
    return jax.shard_map(local, mesh=mesh, in_specs=in_specs, out_specs=out_specs, check_vma=False)
```

```python
import functools
import jax
import jax.numpy as jnp
from jax import lax
from jax.experimental import pallas as pl
from jax.experimental.pallas import tpu as pltpu
from jax.sharding import PartitionSpec as P

HB_DEV = 14
EPSILON = 1e-08
GROUP = 8
VMEM_LIMIT = 32 * 1024 * 1024


def group_of(capacity):
    return next(g for g in (GROUP, 4, 2, 1) if capacity % g == 0)


def feature_block(ref, block, size):
    per_shard = ref.shape[2] // size
    start = pl.multiple_of(lax.rem(block, per_shard) * size, size)
    return ref.at[lax.div(block, per_shard), :, pl.ds(start, size)]


def slot_pair(index_ref, matrix, slot, capacity):
    at = (matrix * capacity + slot) * 2
    return index_ref[at], index_ref[at + 1]


def each_group(count, group, body):
    def step(i, carry):
        body([i * group + u for u in range(group)])
        return carry

    lax.fori_loop(0, lax.div(count + (group - 1), group), step, 0)


def dot(a, b, contract):
    return lax.dot_general(a, b, ((contract[0], contract[1]), ((), ())), preferred_element_type=jnp.float32)


def load_shards(pieces, held, me):
    if len(pieces) == 1:
        return pieces[0]
    own, below, above, across, far = pieces
    last = held.shape[0] - 1
    held[me] = own[...]
    held[lax.bitwise_xor(me, 2)] = across[...]

    @pl.when(me > 0)
    def _():
        held[me - 1] = below[...]

    @pl.when(me < last)
    def _():
        held[me + 1] = above[...]

    @pl.when((me == 0) | (me == last))
    def _():
        held[last - me] = far[...]

    return held


def load_matrices(weights, held, sems, matrices):
    copies = [pltpu.make_async_copy(weights.at[k], held.at[i], sems.at[i]) for i, k in enumerate(matrices)]
    for copy in copies:
        copy.start()
    return [copy.wait for copy in copies]


def store_shards(total, outs, me, per_shard, size):
    if len(outs) == 1:
        shards = range(outs[0].shape[0])
        places = [(outs[0].at[t], t) for t in shards]
    else:
        last = len(outs) - 2
        own, below, above, across, far = outs
        places = [
            (own, me),
            (below, jnp.maximum(me - 1, 0)),
            (above, jnp.minimum(me + 1, last)),
            (across, lax.bitwise_xor(me, 2)),
            (far, last - me),
        ]
    for out, t in places:
        for c in range(per_shard):
            out[:, c * size : (c + 1) * size] = total[t * per_shard + c].astype(out.dtype)


def forward_kernel(n_pieces, n_outs, me_ref, index_ref, count_ref, *refs):
    pieces, refs = refs[:n_pieces], refs[n_pieces:]
    weights, hidden_ref, act_ref, slope_ref = refs[:4]
    outs, (held, w_ref, sems, gate, up, total) = refs[4 : 4 + n_outs], refs[4 + n_outs :]
    me = me_ref[0]
    ready = load_matrices(weights, w_ref, sems, (0, 1, 2))
    x_ref = load_shards(pieces, held, me)
    capacity, size = w_ref.shape[1], w_ref.shape[2]
    group = group_of(capacity)
    hidden_blocks = hidden_ref.shape[0]
    per_shard = x_ref.shape[2] // size
    feature_blocks = x_ref.shape[0] * per_shard
    gate[...] = jnp.zeros_like(gate)
    up[...] = jnp.zeros_like(up)
    total[...] = jnp.zeros_like(total)
    for matrix, acc in ((0, gate), (1, up)):
        count = count_ref[matrix]
        ready[matrix]()

        def project(slots, matrix=matrix, acc=acc, count=count):
            products, targets = [], []
            for s in slots:
                f, h = slot_pair(index_ref, matrix, s, capacity)
                targets.append(jnp.where(s < count, h, hidden_blocks))
                products.append(dot(feature_block(x_ref, f, size)[...], w_ref[matrix, s], ((1,), (0,))))
            for h, p in zip(targets, products):
                acc[h] += p

        each_group(count, group, project)
    for h in range(hidden_blocks):
        g, u = gate[h], up[h]
        sig = 1.0 / (1.0 + jnp.exp(-g))
        act = g * sig
        act_ref[h] = act
        slope_ref[h] = u * sig * (1.0 + g * (1.0 - sig))
        hidden_ref[h] = (act * u).astype(hidden_ref.dtype)
    count = count_ref[2]
    ready[2]()

    def down(slots):
        products, targets = [], []
        for s in slots:
            f, h = slot_pair(index_ref, 2, s, capacity)
            targets.append(jnp.where(s < count, f, feature_blocks))
            products.append(dot(hidden_ref[h], w_ref[2, s], ((1,), (0,))))
        for f, p in zip(targets, products):
            total[f] += p

    each_group(count, group, down)
    store_shards(total, outs, me, per_shard, size)


def rows_kernel(n_pieces, me_ref, index_ref, count_ref, *refs):
    pieces, refs = refs[:n_pieces], refs[n_pieces:]
    act_ref, slope_ref, weights, gate_rows_ref, up_rows_ref, held, w_ref, sems, acc = refs
    (ready,) = load_matrices(weights, w_ref, sems, (2,))
    og_ref = load_shards(pieces, held, me_ref[0])
    capacity, size = w_ref.shape[1], w_ref.shape[2]
    group = group_of(capacity)
    hidden_blocks = act_ref.shape[0]
    acc[...] = jnp.zeros_like(acc)
    count = count_ref[2]
    ready()

    def back(slots):
        products, targets = [], []
        for s in slots:
            f, h = slot_pair(index_ref, 2, s, capacity)
            targets.append(jnp.where(s < count, h, hidden_blocks))
            products.append(dot(feature_block(og_ref, f, size)[...], w_ref[0, s], ((1,), (1,))))
        for h, p in zip(targets, products):
            acc[h] += p

    each_group(count, group, back)
    for h in range(hidden_blocks):
        gate_rows_ref[h] = (acc[h] * slope_ref[h]).astype(gate_rows_ref.dtype)
        up_rows_ref[h] = (acc[h] * act_ref[h]).astype(up_rows_ref.dtype)


def grads_kernel(matrix, n_pieces, me_ref, index_ref, count_ref, *refs):
    pieces, refs = refs[:n_pieces], refs[n_pieces:]
    rows_ref, keep_ref, send_ref, held = refs
    size, share = keep_ref.shape[2], keep_ref.shape[1]
    places = keep_ref.shape[0]
    replica = me_ref[1]
    tok_ref = load_shards(pieces, held, me_ref[0])
    capacity = 2 * places * share
    count = count_ref[matrix]
    for out, bit in ((send_ref, 1), (keep_ref, 0)):

        def one_place(q, carry, out=out, bit=bit):
            first = lax.bitwise_xor(replica, 2 * q + bit) * share

            @pl.when(first < count)
            def _():
                for s in range(share):
                    f, h = slot_pair(index_ref, matrix, first + s, capacity)
                    tok = feature_block(tok_ref, f, size)[...]
                    row = rows_ref[h]
                    left, right = (row, tok) if matrix == 2 else (tok, row)
                    out[q, s] = dot(left, right, ((0,), (0,))).astype(out.dtype)

            return carry

        lax.fori_loop(0, places, one_place, 0)


def input_kernel(n_outs, me_ref, index_ref, count_ref, gate_rows_ref, up_rows_ref, weights, *refs):
    outs, (w_ref, sems, total) = refs[:n_outs], refs[n_outs:]
    ready = load_matrices(weights, w_ref, sems, (0, 1))
    capacity, size = w_ref.shape[1], w_ref.shape[2]
    group = group_of(capacity)
    feature_blocks = total.shape[0] - 1
    per_shard = outs[0].shape[-1] // size
    total[...] = jnp.zeros_like(total)
    for matrix, rows in ((0, gate_rows_ref), (1, up_rows_ref)):
        count = count_ref[matrix]
        ready[matrix]()

        def back(slots, matrix=matrix, rows=rows, count=count):
            products, targets = [], []
            for s in slots:
                f, h = slot_pair(index_ref, matrix, s, capacity)
                targets.append(jnp.where(s < count, f, feature_blocks))
                products.append(dot(rows[h], w_ref[matrix, s], ((1,), (1,))))
            for f, p in zip(targets, products):
                total[f] += p

        each_group(count, group, back)
    store_shards(total, outs, me_ref[0], per_shard, size)


SMEM = pl.BlockSpec(memory_space=pltpu.SMEM)
VMEM = pl.BlockSpec(memory_space=pltpu.VMEM)
ANY = pl.BlockSpec(memory_space=pl.ANY)


def call(kernel, name, outs, scratch, scalars, operands, weights=()):
    return pl.pallas_call(
        kernel,
        name=name,
        out_shape=outs,
        in_specs=[SMEM] * len(scalars) + [VMEM] * len(operands) + [ANY] * len(weights),
        out_specs=jax.tree.map(lambda _: VMEM, outs),
        scratch_shapes=scratch,
        compiler_params=pltpu.CompilerParams(vmem_limit_bytes=VMEM_LIMIT),
    )(*scalars, *operands, *weights)


def matrices_held(count, weights):
    return [pltpu.VMEM((count, *weights.shape[1:]), weights.dtype), pltpu.SemaphoreType.DMA((count,))]


def parts_of(shards, rows, width):
    if shards == 4:
        return [jax.ShapeDtypeStruct((rows, width), jnp.bfloat16)] * 5
    return [jax.ShapeDtypeStruct((shards, rows, width), jnp.bfloat16)]


def gather_line(v, shards):
    if shards != 4:
        return [lax.all_gather(v, "tensor", axis=0)]
    across = lax.ppermute(v, "tensor", [(a, a ^ 2) for a in range(4)])
    below = lax.ppermute(v, "tensor", [(a, a + 1) for a in range(3)])
    above = lax.ppermute(v, "tensor", [(a + 1, a) for a in range(3)])
    far = lax.ppermute(across, "tensor", [(2, 3), (1, 0)])
    return [v, below, above, across, far]


def scatter_line(parts):
    if len(parts) == 1:
        return lax.psum_scatter(parts[0], "tensor", scatter_dimension=0)
    own, below, above, across, far = parts
    far = lax.ppermute(far, "tensor", [(3, 2), (0, 1)])
    below = lax.ppermute(below, "tensor", [(a + 1, a) for a in range(3)])
    above = lax.ppermute(above, "tensor", [(a, a + 1) for a in range(3)])
    across = lax.ppermute(across + far, "tensor", [(a, a ^ 2) for a in range(4)])
    wide = [p.astype(jnp.float32) for p in (own, below, above, across)]
    return (wide[0] + wide[1] + wide[2] + wide[3]).astype(jnp.bfloat16)


def swap(v, replicas, bit):
    return lax.ppermute(v, "dp", [(a, a ^ bit) for a in range(replicas)])


def replica_sum(keep, send, replicas):
    total = keep + swap(send, replicas, 1)
    levels = (replicas // 2).bit_length() - 1
    share = keep.shape[1]
    cut = share // 2
    rest = keep.shape[1:]
    total = total.reshape((2,) * levels + rest)
    halves = []
    for part, order in ((total[..., :cut, :, :], range(levels)), (total[..., cut:, :, :], reversed(range(levels)))):
        done = []
        for level in order:
            axis = levels - 1 - level
            axis -= sum(1 for d in done if d > level)
            mine = lax.index_in_dim(part, 0, axis, keepdims=False)
            theirs = lax.index_in_dim(part, 1, axis, keepdims=False)
            got = swap(theirs, replicas, 2 << level)
            done.append(level)
            if len(done) == levels:
                part = mine.astype(jnp.float32) + got.astype(jnp.float32)
            else:
                part = mine + got
        halves.append(part)
    return jnp.concatenate(halves, axis=0)


def local(replicas, shards, inputs, out_grad, weights, block_index, block_counts, first_moment, second_moment):
    capacity, size = weights.shape[1], weights.shape[2]
    rows, width = inputs.shape
    f32, bf16 = jnp.float32, jnp.bfloat16
    shape = jax.ShapeDtypeStruct
    counts = block_counts[0]
    me = jnp.stack([lax.axis_index("tensor"), lax.axis_index("dp")]).astype(jnp.int32)
    scalars = (me, block_index.reshape(-1), counts)
    features = shards * width // size
    x = gather_line(inputs, shards)
    og = gather_line(out_grad, shards)
    parts = parts_of(shards, rows, width)
    held = pltpu.VMEM((shards, rows, width), bf16)
    wide = shape((HB_DEV, rows, size), f32)
    narrow = shape((HB_DEV, rows, size), bf16)
    acc = pltpu.VMEM((HB_DEV + 1, rows, size), f32)
    total = pltpu.VMEM((features + 1, rows, size), f32)
    hidden, act, slope, *out_parts = call(
        functools.partial(forward_kernel, len(x), len(parts)),
        "forward",
        [narrow, wide, wide, *parts],
        [held, *matrices_held(3, weights), acc, acc, total],
        scalars,
        x,
        [weights],
    )
    outputs = scatter_line(out_parts)
    places, share = replicas // 2, capacity // replicas
    half = shape((places, share, size, size), bf16)

    def grads(matrix, tok, row):
        keep, send = call(
            functools.partial(grads_kernel, matrix, len(tok)), ("gate_grads", "up_grads", "down_grads")[matrix],
            [half, half], [held], scalars, [*tok, row],
        )
        return replica_sum(keep, send, replicas)

    down_grad = grads(2, og, hidden)
    gate_rows, up_rows = call(
        functools.partial(rows_kernel, len(og)), "row_grads", [narrow, narrow],
        [held, *matrices_held(1, weights), acc], scalars, [*og, act, slope], [weights],
    )
    gate_grad = grads(0, x, gate_rows)
    in_parts = call(
        functools.partial(input_kernel, len(parts)), "input_grads", parts, [*matrices_held(2, weights), total],
        scalars, [gate_rows, up_rows], [weights],
    )
    input_grad = scatter_line(in_parts)
    up_grad = grads(1, x, up_rows)
    share_ids = lax.axis_index("dp") * share + jnp.arange(share, dtype=jnp.int32)
    updates = []
    for matrix, g in enumerate((gate_grad, up_grad, down_grad)):
        live = (share_ids < counts[matrix])[:, None, None]
        first_new = 0.9 * first_moment[matrix] + 0.1 * g
        second_new = 0.95 * second_moment[matrix] + 0.05 * g * g
        updates.append(jnp.where(live, first_new / (jnp.sqrt(second_new) + EPSILON), 0.0))
    return (outputs, input_grad, jnp.stack(updates))


def solution(mesh):
    in_specs = (
        P("dp", "tensor"),
        P("dp", "tensor"),
        P(None, "tensor", None, None),
        P(None, "tensor", None),
        P("tensor", None),
        P(None, ("tensor", "dp"), None, None),
        P(None, ("tensor", "dp"), None, None),
    )
    out_specs = (P("dp", "tensor"), P("dp", "tensor"), P(None, ("tensor", "dp"), None, None))
    body = functools.partial(local, mesh.shape["dp"], mesh.shape["tensor"])
    return jax.shard_map(body, mesh=mesh, in_specs=in_specs, out_specs=out_specs, check_vma=False)
```

```python
import functools
import jax
import jax.numpy as jnp
from jax import lax
from jax.experimental import pallas as pl
from jax.experimental.pallas import tpu as pltpu
from jax.sharding import PartitionSpec as P

HB_DEV = 14
EPSILON = 1e-08
GROUP = 8
VMEM_LIMIT = 32 * 1024 * 1024
F32, BF16 = jnp.float32, jnp.bfloat16
SHAPE = jax.ShapeDtypeStruct
SMEM = pl.BlockSpec(memory_space=pltpu.SMEM)
VMEM = pl.BlockSpec(memory_space=pltpu.VMEM)
ANY = pl.BlockSpec(memory_space=pl.ANY)
TOKEN = SHAPE((1,), jnp.int32)


def group_of(capacity):
    return next(g for g in (GROUP, 4, 2, 1) if capacity % g == 0)


def feature_block(ref, block, size):
    per_shard = ref.shape[2] // size
    start = pl.multiple_of(lax.rem(block, per_shard) * size, size)
    return ref.at[lax.div(block, per_shard), :, pl.ds(start, size)]


def slot_pair(index_ref, matrix, slot, capacity):
    at = (matrix * capacity + slot) * 2
    return index_ref[at], index_ref[at + 1]


def each_group(count, group, body):
    def step(i, carry):
        body([i * group + u for u in range(group)])
        return carry

    lax.fori_loop(0, lax.div(count + (group - 1), group), step, 0)


def dot(a, b, contract):
    return lax.dot_general(a, b, (contract, ((), ())), preferred_element_type=F32)


def accumulate(index_ref, matrix, count, capacity, acc, into, product):
    trash = acc.shape[0] - 1

    def body(slots):
        products, targets = [], []
        for s in slots:
            pair = slot_pair(index_ref, matrix, s, capacity)
            targets.append(jnp.where(s < count, pair[into], trash))
            products.append(product(s, *pair))
        for t, p in zip(targets, products):
            acc[t] += p

    each_group(count, group_of(capacity), body)


def load_shards(pieces, held, me):
    if len(pieces) == 1:
        return pieces[0]
    if len(pieces) == 4:
        for offset, piece in enumerate(pieces):
            held[lax.bitwise_xor(me, offset)] = piece[...]
        return held
    own, below, above, across, far = pieces
    last = held.shape[0] - 1
    held[me] = own[...]
    held[lax.bitwise_xor(me, 2)] = across[...]

    @pl.when(me > 0)
    def _():
        held[me - 1] = below[...]

    @pl.when(me < last)
    def _():
        held[me + 1] = above[...]

    @pl.when((me == 0) | (me == last))
    def _():
        held[last - me] = far[...]

    return held


def store_shards(total, outs, me, per_shard, size):
    if len(outs) == 1:
        places = [(outs[0].at[t], t) for t in range(outs[0].shape[0])]
    elif len(outs) == 4:
        places = [(out, lax.bitwise_xor(me, offset)) for offset, out in enumerate(outs)]
    else:
        last = len(outs) - 2
        own, below, above, across, far = outs
        places = [
            (own, me),
            (below, jnp.maximum(me - 1, 0)),
            (above, jnp.minimum(me + 1, last)),
            (across, lax.bitwise_xor(me, 2)),
            (far, last - me),
        ]
    for out, t in places:
        for c in range(per_shard):
            out[:, c * size : (c + 1) * size] = total[t * per_shard + c].astype(out.dtype)


def forward_kernel(n_pieces, n_outs, me_ref, index_ref, count_ref, *refs):
    pieces, refs = refs[:n_pieces], refs[n_pieces:]
    w_ref, hidden_ref, turned_ref, act_ref, slope_ref = refs[:5]
    outs, (held, gate, up, total) = refs[5 : 5 + n_outs], refs[5 + n_outs :]
    me = me_ref[0]
    x_ref = load_shards(pieces, held, me)
    capacity, size = w_ref.shape[1], w_ref.shape[2]
    gate[...] = jnp.zeros_like(gate)
    up[...] = jnp.zeros_like(up)
    total[...] = jnp.zeros_like(total)
    for matrix, acc in ((0, gate), (1, up)):
        accumulate(
            index_ref, matrix, count_ref[matrix], capacity, acc, 1,
            lambda s, f, h, matrix=matrix: dot(feature_block(x_ref, f, size)[...], w_ref[matrix, s], ((1,), (0,))),
        )
    for h in range(hidden_ref.shape[0]):
        g, u = gate[h], up[h]
        sig = 1.0 / (1.0 + jnp.exp(-g))
        act = g * sig
        act_ref[h] = act
        slope_ref[h] = u * sig * (1.0 + g * (1.0 - sig))
        hidden = (act * u).astype(hidden_ref.dtype)
        hidden_ref[h] = hidden
        turned_ref[h] = hidden.T
    accumulate(
        index_ref, 2, count_ref[2], capacity, total, 0,
        lambda s, f, h: dot(hidden_ref[h], w_ref[2, s], ((1,), (0,))),
    )
    store_shards(total, outs, me, x_ref.shape[2] // size, size)


def turn_kernel(n_pieces, me_ref, *refs):
    pieces, (turned_ref, held) = refs[:n_pieces], refs[n_pieces:]
    x_ref = load_shards(pieces, held, me_ref[0])
    size = turned_ref.shape[1]
    per_shard = x_ref.shape[2] // size
    for f in range(turned_ref.shape[0]):
        c = f % per_shard
        turned_ref[f] = x_ref[f // per_shard, :, c * size : (c + 1) * size].T


def rows_kernel(n_pieces, me_ref, index_ref, count_ref, *refs):
    pieces, refs = refs[:n_pieces], refs[n_pieces:]
    w_ref, act_ref, slope_ref, gate_rows_ref, up_rows_ref, held, acc = refs
    og_ref = load_shards(pieces, held, me_ref[0])
    capacity, size = w_ref.shape[1], w_ref.shape[2]
    acc[...] = jnp.zeros_like(acc)
    accumulate(
        index_ref, 2, count_ref[2], capacity, acc, 1,
        lambda s, f, h: dot(feature_block(og_ref, f, size)[...], w_ref[2, s], ((1,), (1,))),
    )
    for h in range(act_ref.shape[0]):
        gate_rows_ref[h] = (acc[h] * slope_ref[h]).astype(gate_rows_ref.dtype)
        up_rows_ref[h] = (acc[h] * act_ref[h]).astype(up_rows_ref.dtype)


def spread(place, core, places):
    levels = places.bit_length() - 1
    turned = sum(lax.shift_left(lax.bitwise_and(lax.shift_right_logical(place, b), 1), levels - 1 - b) for b in range(levels))
    return 2 * jnp.where(core == 0, place, turned)


def grads_kernel(matrix, n_pieces, me_ref, index_ref, count_ref, *refs):
    pieces, refs = refs[:n_pieces], refs[n_pieces:]
    turned_ref, keep_ref, send_ref, held = refs
    size, share = keep_ref.shape[2], keep_ref.shape[1]
    places = keep_ref.shape[0]
    replica = me_ref[1]
    right_ref = load_shards(pieces, held, me_ref[0])
    capacity = 2 * places * share
    count = count_ref[matrix]
    for out, bit in ((send_ref, 1), (keep_ref, 0)):

        def one_place(q, carry, out=out, bit=bit):
            owner = lax.bitwise_xor(replica, bit)
            first = lax.bitwise_xor(owner, spread(q, lax.bitwise_and(owner, 1), places)) * share

            @pl.when(first < count)
            def _():
                for s in range(share):
                    f, h = slot_pair(index_ref, matrix, first + s, capacity)
                    if matrix == 2:
                        left, right = turned_ref[h], feature_block(right_ref, f, size)[...]
                    else:
                        left, right = turned_ref[f], right_ref[h]
                    out[q, s] = dot(left, right, ((1,), (0,))).astype(out.dtype)

            return carry

        lax.fori_loop(0, places, one_place, 0)


def input_kernel(n_outs, me_ref, index_ref, count_ref, gate_rows_ref, up_rows_ref, w_ref, *refs):
    outs, (total,) = refs[:n_outs], refs[n_outs:]
    capacity, size = w_ref.shape[1], w_ref.shape[2]
    total[...] = jnp.zeros_like(total)
    for matrix, rows in ((0, gate_rows_ref), (1, up_rows_ref)):
        accumulate(
            index_ref, matrix, count_ref[matrix], capacity, total, 0,
            lambda s, f, h, matrix=matrix, rows=rows: dot(rows[h], w_ref[matrix, s], ((1,), (1,))),
        )
    store_shards(total, outs, me_ref[0], outs[0].shape[-1] // size, size)


def fold_kernel(keep_ref, got_ref, keep_out, send_out):
    half = keep_out.shape[0]
    keep_out[...] = keep_ref[:half] + got_ref[:half]
    send_out[...] = keep_ref[half:] + got_ref[half:]


def add_kernel(a_ref, b_ref, out_ref):
    out_ref[...] = a_ref[...] + b_ref[...]


def sum_kernel(*refs):
    *parts, out_ref = refs
    total = parts[0][...].astype(F32)
    for part in parts[1:]:
        total += part[...].astype(F32)
    out_ref[...] = total.astype(out_ref.dtype)


def update_kernel(matrix, me_ref, count_ref, keep_ref, got_ref, m1_ref, m2_ref, *refs):
    out_ref = refs[-1]
    share = keep_ref.shape[1]
    first = me_ref[1] * share
    for s in range(share):
        g = keep_ref[0, s].astype(F32) + got_ref[0, s].astype(F32)
        first_new = 0.9 * m1_ref[0, s] + 0.1 * g
        second_new = 0.95 * m2_ref[0, s] + 0.05 * g * g
        live = first + s < count_ref[matrix]
        out_ref[0, s] = jnp.where(live, first_new / (jnp.sqrt(second_new) + EPSILON), 0.0)


def hold_kernel(v_ref, _, out_ref):
    out_ref[...] = v_ref[...]


class Line:
    token = None

    def __call__(self, kernel, name, outs, scratch, operands, scalars=(), specs=None, out_specs=None, aliases=None, **more):
        tokens = [] if self.token is None else [self.token]
        n_in, n_out = len(scalars) + len(operands), len(outs)

        def body(*refs):
            ins, rest = refs[:n_in], refs[n_in + len(tokens) :]
            results, token, scratches = rest[:n_out], rest[n_out], rest[n_out + 1 :]
            token[0] = 0
            kernel(*ins, *results, *scratches)

        *results, self.token = pl.pallas_call(
            body,
            name=name,
            out_shape=[*outs, TOKEN],
            in_specs=[SMEM] * len(scalars) + (specs or [VMEM] * len(operands)) + [SMEM] * len(tokens),
            out_specs=[*(out_specs or [VMEM] * n_out), SMEM],
            scratch_shapes=scratch,
            input_output_aliases=aliases or {},
            compiler_params=pltpu.CompilerParams(vmem_limit_bytes=VMEM_LIMIT),
            **more,
        )(*scalars, *operands, *tokens)
        return results


def flip(v, shards, bit):
    return lax.ppermute(v, "tensor", [(a, a ^ bit) for a in range(shards)])


def gather_near(v):
    across, beside = flip(v, 4, 2), flip(v, 4, 1)
    return [v, beside, across, flip(across, 4, 1)]


def gather_line(v):
    across = flip(v, 4, 2)
    below = lax.ppermute(v, "tensor", [(a, a + 1) for a in range(3)])
    above = lax.ppermute(v, "tensor", [(a + 1, a) for a in range(3)])
    far = lax.ppermute(across, "tensor", [(2, 3), (1, 0)])
    return [v, below, above, across, far]


def scatter_first(parts):
    if len(parts) == 4:
        own, beside, across, far = parts
        return [own, flip(beside, 4, 1)], across, flip(far, 4, 1)
    own, below, above, across, far = parts
    far = lax.ppermute(far, "tensor", [(3, 2), (0, 1)])
    below = lax.ppermute(below, "tensor", [(a + 1, a) for a in range(3)])
    above = lax.ppermute(above, "tensor", [(a, a + 1) for a in range(3)])
    return [own, below, above], across, far


def core_swap(v, replicas):
    return lax.ppermute(v, "dp", [(a, a ^ 1) for a in range(replicas)])


def axis_swap(v, replicas, step):
    levels = replicas.bit_length() - 2
    pairs = [(a, a ^ (1 << (1 + step if a & 1 else levels - step))) for a in range(replicas)]
    return lax.ppermute(v, "dp", pairs)


def local(replicas, shards, inputs, out_grad, weights, block_index, block_counts, first_moment, second_moment):
    capacity, size = weights.shape[1], weights.shape[2]
    rows, width = inputs.shape
    me = jnp.stack([lax.axis_index("tensor"), lax.axis_index("dp")]).astype(jnp.int32)
    scalars = (me, block_index.reshape(-1), block_counts[0])
    features = shards * width // size
    places, share = replicas // 2, capacity // replicas
    levels = places.bit_length() - 1
    held = pltpu.VMEM((shards, rows, width), BF16)
    acc = pltpu.VMEM((HB_DEV + 1, rows, size), F32)
    total = pltpu.VMEM((features + 1, rows, size), F32)
    wide = SHAPE((HB_DEV, rows, size), F32)
    narrow = SHAPE((HB_DEV, rows, size), BF16)
    turned = SHAPE((HB_DEV, size, rows), BF16)
    piece = SHAPE((rows, width), BF16)
    line = Line()
    lined = shards == 4

    def gather(v, form):
        return form(v) if lined else [lax.all_gather(v, "tensor", axis=0)]

    def parts_of(count):
        return [piece] * count if lined else [SHAPE((shards, rows, width), BF16)]

    def grads(matrix, right, left):
        half = SHAPE((places, share, size, size), BF16)
        name = ("gate_grads", "up_grads", "down_grads")[matrix]
        kernel = functools.partial(grads_kernel, matrix, len(right))
        keep, send = line(kernel, name, [half, half], [held], [*right, left], scalars)
        return keep, core_swap(send, replicas)

    def fold(keep, got, step):
        half = SHAPE((keep.shape[0] // 2, *keep.shape[1:]), BF16)
        keep, send = line(fold_kernel, "fold", [half, half], [], [keep, got])
        return keep, axis_swap(send, replicas, step)

    def update(matrix, keep, got, buffer):
        block = pl.BlockSpec((1, share, size, size), lambda i: (matrix, 0, 0, 0))
        extra = [] if buffer is None else [buffer]
        return line(
            functools.partial(update_kernel, matrix),
            "update",
            [SHAPE(first_moment.shape, F32)],
            [],
            [keep, got, first_moment, second_moment, *extra],
            (me, scalars[2]),
            specs=[VMEM, VMEM, block, block] + [ANY] * len(extra),
            out_specs=[block],
            aliases={6: 0} if extra else {},
            grid=(1,),
        )[0]

    def join(across, far):
        return flip(line(add_kernel, "join", [piece], [], [across, far])[0], 4, 2)

    def finish(held_parts, across):
        return line(sum_kernel, "finish", [piece], [], [*held_parts, across])[0]

    x = gather(inputs, gather_near)
    if lined:
        (out_grad,) = line(hold_kernel, "hold", [piece], [], [out_grad, x[2]])
    og = gather(out_grad, gather_line)
    out_parts, in_parts = parts_of(5), parts_of(4)
    hidden, hidden_turned, act, slope, *out_parts = line(
        functools.partial(forward_kernel, len(x), len(out_parts)),
        "forward",
        [narrow, turned, wide, wide, *out_parts],
        [held, acc, acc, total],
        [*x, weights],
        scalars,
    )
    if lined:
        out_held, across, far = scatter_first(out_parts)
    else:
        outputs = lax.psum_scatter(out_parts[0], "tensor", scatter_dimension=0)
    (x_turned,) = line(
        functools.partial(turn_kernel, len(x)), "turn", [SHAPE((features, size, rows), BF16)], [held], x, (me,)
    )
    if lined:
        across = join(across, far)
    gate_rows, up_rows = line(
        functools.partial(rows_kernel, len(og)),
        "row_grads",
        [narrow, narrow],
        [held, acc],
        [*og, weights, act, slope],
        scalars,
    )
    in_parts = line(
        functools.partial(input_kernel, len(in_parts)),
        "input_grads",
        in_parts,
        [total],
        [gate_rows, up_rows, weights],
        scalars,
    )
    if lined:
        in_held, in_across, in_far = scatter_first(in_parts)
    else:
        input_grad = lax.psum_scatter(in_parts[0], "tensor", scatter_dimension=0)
    down = grads(2, og, hidden_turned)
    gate = grads(0, [gate_rows], x_turned)
    down = fold(*down, 0)
    if lined:
        in_across = join(in_across, in_far)
    up = grads(1, [up_rows], x_turned)
    gate = fold(*gate, 0)
    if lined:
        outputs = finish(out_held, across)
    for step in range(1, levels):
        down = fold(*down, step)
        if step == 1:
            up = fold(*up, 0)
        gate = fold(*gate, step)
    buffer = update(2, *down, None)
    for step in range(1, levels):
        up = fold(*up, step)
    buffer = update(0, *gate, buffer)
    if lined:
        input_grad = finish(in_held, in_across)
    buffer = update(1, *up, buffer)
    return (outputs, input_grad, buffer)


def solution(mesh):
    in_specs = (
        P("dp", "tensor"),
        P("dp", "tensor"),
        P(None, "tensor", None, None),
        P(None, "tensor", None),
        P("tensor", None),
        P(None, ("tensor", "dp"), None, None),
        P(None, ("tensor", "dp"), None, None),
    )
    out_specs = (P("dp", "tensor"), P("dp", "tensor"), P(None, ("tensor", "dp"), None, None))
    body = functools.partial(local, mesh.shape["dp"], mesh.shape["tensor"])
    return jax.shard_map(body, mesh=mesh, in_specs=in_specs, out_specs=out_specs, check_vma=False)
```

```python
import functools
import jax
import jax.numpy as jnp
from jax import lax
from jax.experimental import pallas as pl
from jax.experimental.pallas import tpu as pltpu
from jax.sharding import PartitionSpec as P

HB_DEV = 14
EPSILON = 1e-08
GROUP = 8
VMEM_LIMIT = 32 * 1024 * 1024
F32, BF16 = jnp.float32, jnp.bfloat16
SHAPE = jax.ShapeDtypeStruct
SMEM = pl.BlockSpec(memory_space=pltpu.SMEM)
VMEM = pl.BlockSpec(memory_space=pltpu.VMEM)
ANY = pl.BlockSpec(memory_space=pl.ANY)
TOKEN = SHAPE((1,), jnp.int32)


def group_of(capacity):
    return next(g for g in (GROUP, 4, 2, 1) if capacity % g == 0)


def feature_block(ref, block, size):
    per_shard = ref.shape[2] // size
    start = pl.multiple_of(lax.rem(block, per_shard) * size, size)
    return ref.at[lax.div(block, per_shard), :, pl.ds(start, size)]


def slot_pair(index_ref, matrix, slot, capacity):
    at = (matrix * capacity + slot) * 2
    return index_ref[at], index_ref[at + 1]


def each_group(count, group, body):
    def step(i, carry):
        body([i * group + u for u in range(group)])
        return carry

    lax.fori_loop(0, lax.div(count + (group - 1), group), step, 0)


def dot(a, b, contract):
    return lax.dot_general(a, b, (contract, ((), ())), preferred_element_type=F32)


def accumulate(index_ref, matrix, count, capacity, acc, into, product):
    trash = acc.shape[0] - 1

    def body(slots):
        products, targets = [], []
        for s in slots:
            pair = slot_pair(index_ref, matrix, s, capacity)
            targets.append(jnp.where(s < count, pair[into], trash))
            products.append(product(s, *pair))
        for t, p in zip(targets, products):
            acc[t] += p

    each_group(count, group_of(capacity), body)


def load_shards(pieces, held, me):
    if len(pieces) == 1:
        return pieces[0]
    if len(pieces) == 4:
        for offset, piece in enumerate(pieces):
            held[lax.bitwise_xor(me, offset)] = piece[...]
        return held
    own, below, above, across, far = pieces
    last = held.shape[0] - 1
    held[me] = own[...]
    held[lax.bitwise_xor(me, 2)] = across[...]

    @pl.when(me > 0)
    def _():
        held[me - 1] = below[...]

    @pl.when(me < last)
    def _():
        held[me + 1] = above[...]

    @pl.when((me == 0) | (me == last))
    def _():
        held[last - me] = far[...]

    return held


def store_shards(total, outs, me, per_shard, size):
    if len(outs) == 1:
        places = [(outs[0].at[t], t) for t in range(outs[0].shape[0])]
    elif len(outs) == 4:
        places = [(out, lax.bitwise_xor(me, offset)) for offset, out in enumerate(outs)]
    else:
        last = len(outs) - 2
        own, below, above, across, far = outs
        places = [
            (own, me),
            (below, jnp.maximum(me - 1, 0)),
            (above, jnp.minimum(me + 1, last)),
            (across, lax.bitwise_xor(me, 2)),
            (far, last - me),
        ]
    for out, t in places:
        for c in range(per_shard):
            out[:, c * size : (c + 1) * size] = total[t * per_shard + c].astype(out.dtype)


def forward_kernel(n_pieces, n_outs, me_ref, index_ref, count_ref, *refs):
    pieces, refs = refs[:n_pieces], refs[n_pieces:]
    w_ref, hidden_ref, turned_ref, act_ref, slope_ref = refs[:5]
    outs, (held, gate, up, total) = refs[5 : 5 + n_outs], refs[5 + n_outs :]
    me = me_ref[0]
    x_ref = load_shards(pieces, held, me)
    capacity, size = w_ref.shape[1], w_ref.shape[2]
    gate[...] = jnp.zeros_like(gate)
    up[...] = jnp.zeros_like(up)
    total[...] = jnp.zeros_like(total)
    for matrix, acc in ((0, gate), (1, up)):
        accumulate(
            index_ref, matrix, count_ref[matrix], capacity, acc, 1,
            lambda s, f, h, matrix=matrix: dot(feature_block(x_ref, f, size)[...], w_ref[matrix, s], ((1,), (0,))),
        )
    for h in range(hidden_ref.shape[0]):
        g, u = gate[h], up[h]
        sig = 1.0 / (1.0 + jnp.exp(-g))
        act = g * sig
        act_ref[h] = act
        slope_ref[h] = u * sig * (1.0 + g * (1.0 - sig))
        hidden = (act * u).astype(hidden_ref.dtype)
        hidden_ref[h] = hidden
        turned_ref[h] = hidden.T
    accumulate(
        index_ref, 2, count_ref[2], capacity, total, 0,
        lambda s, f, h: dot(hidden_ref[h], w_ref[2, s], ((1,), (0,))),
    )
    store_shards(total, outs, me, x_ref.shape[2] // size, size)


def turn_kernel(n_pieces, me_ref, *refs):
    pieces, (turned_ref, held) = refs[:n_pieces], refs[n_pieces:]
    x_ref = load_shards(pieces, held, me_ref[0])
    size = turned_ref.shape[1]
    per_shard = x_ref.shape[2] // size
    for f in range(turned_ref.shape[0]):
        c = f % per_shard
        turned_ref[f] = x_ref[f // per_shard, :, c * size : (c + 1) * size].T


def rows_kernel(n_pieces, me_ref, index_ref, count_ref, *refs):
    pieces, refs = refs[:n_pieces], refs[n_pieces:]
    w_ref, act_ref, slope_ref, gate_rows_ref, up_rows_ref, held, acc = refs
    og_ref = load_shards(pieces, held, me_ref[0])
    capacity, size = w_ref.shape[1], w_ref.shape[2]
    acc[...] = jnp.zeros_like(acc)
    accumulate(
        index_ref, 2, count_ref[2], capacity, acc, 1,
        lambda s, f, h: dot(feature_block(og_ref, f, size)[...], w_ref[2, s], ((1,), (1,))),
    )
    for h in range(act_ref.shape[0]):
        gate_rows_ref[h] = (acc[h] * slope_ref[h]).astype(gate_rows_ref.dtype)
        up_rows_ref[h] = (acc[h] * act_ref[h]).astype(up_rows_ref.dtype)


def spread(place, core, places):
    levels = places.bit_length() - 1
    turned = sum(lax.shift_left(lax.bitwise_and(lax.shift_right_logical(place, b), 1), levels - 1 - b) for b in range(levels))
    return 2 * jnp.where(core == 0, place, turned)


def grads_kernel(matrix, n_pieces, me_ref, index_ref, count_ref, *refs):
    pieces, refs = refs[:n_pieces], refs[n_pieces:]
    turned_ref, keep_ref, send_ref, held = refs
    size, share = keep_ref.shape[2], keep_ref.shape[1]
    places = keep_ref.shape[0]
    replica = me_ref[1]
    right_ref = load_shards(pieces, held, me_ref[0])
    capacity = 2 * places * share
    count = count_ref[matrix]
    for out, bit in ((send_ref, 1), (keep_ref, 0)):

        def one_place(q, carry, out=out, bit=bit):
            owner = lax.bitwise_xor(replica, bit)
            first = lax.bitwise_xor(owner, spread(q, lax.bitwise_and(owner, 1), places)) * share

            @pl.when(first < count)
            def _():
                for s in range(share):
                    f, h = slot_pair(index_ref, matrix, first + s, capacity)
                    if matrix == 2:
                        left, right = turned_ref[h], feature_block(right_ref, f, size)[...]
                    else:
                        left, right = turned_ref[f], right_ref[h]
                    out[q, s] = dot(left, right, ((1,), (0,))).astype(out.dtype)

            return carry

        lax.fori_loop(0, places, one_place, 0)


def input_kernel(n_outs, me_ref, index_ref, count_ref, gate_rows_ref, up_rows_ref, w_ref, *refs):
    outs, (total,) = refs[:n_outs], refs[n_outs:]
    capacity, size = w_ref.shape[1], w_ref.shape[2]
    total[...] = jnp.zeros_like(total)
    for matrix, rows in ((0, gate_rows_ref), (1, up_rows_ref)):
        accumulate(
            index_ref, matrix, count_ref[matrix], capacity, total, 0,
            lambda s, f, h, matrix=matrix, rows=rows: dot(rows[h], w_ref[matrix, s], ((1,), (1,))),
        )
    store_shards(total, outs, me_ref[0], outs[0].shape[-1] // size, size)


def fold_kernel(keep_ref, got_ref, keep_out, send_out):
    half = keep_out.shape[0]
    keep_out[...] = keep_ref[:half] + got_ref[:half]
    send_out[...] = keep_ref[half:] + got_ref[half:]


def add_kernel(a_ref, b_ref, out_ref):
    out_ref[...] = a_ref[...] + b_ref[...]


def sum_kernel(*refs):
    *parts, out_ref = refs
    total = parts[0][...].astype(F32)
    for part in parts[1:]:
        total += part[...].astype(F32)
    out_ref[...] = total.astype(out_ref.dtype)


def update_kernel(matrix, me_ref, count_ref, keep_ref, got_ref, m1_ref, m2_ref, *refs):
    out_ref = refs[-1]
    share = keep_ref.shape[1]
    first = me_ref[1] * share
    for s in range(share):
        g = keep_ref[0, s].astype(F32) + got_ref[0, s].astype(F32)
        first_new = 0.9 * m1_ref[0, s] + 0.1 * g
        second_new = 0.95 * m2_ref[0, s] + 0.05 * g * g
        live = first + s < count_ref[matrix]
        out_ref[0, s] = jnp.where(live, first_new / (jnp.sqrt(second_new) + EPSILON), 0.0)


def hold_kernel(v_ref, _, out_ref):
    out_ref[...] = v_ref[...]


class Line:
    token = None

    def __call__(self, kernel, name, outs, scratch, operands, scalars=(), specs=None, out_specs=None, aliases=None, **more):
        tokens = [] if self.token is None else [self.token]
        n_in, n_out = len(scalars) + len(operands), len(outs)

        def body(*refs):
            ins, rest = refs[:n_in], refs[n_in + len(tokens) :]
            results, token, scratches = rest[:n_out], rest[n_out], rest[n_out + 1 :]
            token[0] = 0
            kernel(*ins, *results, *scratches)

        *results, self.token = pl.pallas_call(
            body,
            name=name,
            out_shape=[*outs, TOKEN],
            in_specs=[SMEM] * len(scalars) + (specs or [VMEM] * len(operands)) + [SMEM] * len(tokens),
            out_specs=[*(out_specs or [VMEM] * n_out), SMEM],
            scratch_shapes=scratch,
            input_output_aliases=aliases or {},
            compiler_params=pltpu.CompilerParams(vmem_limit_bytes=VMEM_LIMIT),
            cost_estimate=pl.CostEstimate(flops=10**15, bytes_accessed=10**12, transcendentals=0),
            **more,
        )(*scalars, *operands, *tokens)
        return results


def flip(v, shards, bit):
    return lax.ppermute(v, "tensor", [(a, a ^ bit) for a in range(shards)])


def gather_near(v):
    across, beside = flip(v, 4, 2), flip(v, 4, 1)
    return [v, beside, across, flip(across, 4, 1)]


def gather_line(v):
    across = flip(v, 4, 2)
    below = lax.ppermute(v, "tensor", [(a, a + 1) for a in range(3)])
    above = lax.ppermute(v, "tensor", [(a + 1, a) for a in range(3)])
    far = lax.ppermute(across, "tensor", [(2, 3), (1, 0)])
    return [v, below, above, across, far]


def scatter_first(parts):
    if len(parts) == 4:
        own, beside, across, far = parts
        return [own, flip(beside, 4, 1)], across, flip(far, 4, 1)
    own, below, above, across, far = parts
    far = lax.ppermute(far, "tensor", [(3, 2), (0, 1)])
    below = lax.ppermute(below, "tensor", [(a + 1, a) for a in range(3)])
    above = lax.ppermute(above, "tensor", [(a, a + 1) for a in range(3)])
    return [own, below, above], across, far


def core_swap(v, replicas):
    return lax.ppermute(v, "dp", [(a, a ^ 1) for a in range(replicas)])


def axis_swap(v, replicas, step):
    levels = replicas.bit_length() - 2
    pairs = [(a, a ^ (1 << (1 + step if a & 1 else levels - step))) for a in range(replicas)]
    return lax.ppermute(v, "dp", pairs)


def local(replicas, shards, inputs, out_grad, weights, block_index, block_counts, first_moment, second_moment):
    capacity, size = weights.shape[1], weights.shape[2]
    rows, width = inputs.shape
    me = jnp.stack([lax.axis_index("tensor"), lax.axis_index("dp")]).astype(jnp.int32)
    scalars = (me, block_index.reshape(-1), block_counts[0])
    features = shards * width // size
    places, share = replicas // 2, capacity // replicas
    levels = places.bit_length() - 1
    held = pltpu.VMEM((shards, rows, width), BF16)
    acc = pltpu.VMEM((HB_DEV + 1, rows, size), F32)
    total = pltpu.VMEM((features + 1, rows, size), F32)
    wide = SHAPE((HB_DEV, rows, size), F32)
    narrow = SHAPE((HB_DEV, rows, size), BF16)
    turned = SHAPE((HB_DEV, size, rows), BF16)
    piece = SHAPE((rows, width), BF16)
    line = Line()
    lined = shards == 4

    def gather(v, form):
        return form(v) if lined else [lax.all_gather(v, "tensor", axis=0)]

    def parts_of(count):
        return [piece] * count if lined else [SHAPE((shards, rows, width), BF16)]

    def grads(matrix, right, left):
        half = SHAPE((places, share, size, size), BF16)
        name = ("gate_grads", "up_grads", "down_grads")[matrix]
        kernel = functools.partial(grads_kernel, matrix, len(right))
        keep, send = line(kernel, name, [half, half], [held], [*right, left], scalars)
        return keep, core_swap(send, replicas)

    def fold(keep, got, step):
        half = SHAPE((keep.shape[0] // 2, *keep.shape[1:]), BF16)
        keep, send = line(fold_kernel, "fold", [half, half], [], [keep, got])
        return keep, axis_swap(send, replicas, step)

    def update(matrix, keep, got, buffer):
        block = pl.BlockSpec((1, share, size, size), lambda i: (matrix, 0, 0, 0))
        extra = [] if buffer is None else [buffer]
        return line(
            functools.partial(update_kernel, matrix),
            "update",
            [SHAPE(first_moment.shape, F32)],
            [],
            [keep, got, first_moment, second_moment, *extra],
            (me, scalars[2]),
            specs=[VMEM, VMEM, block, block] + [ANY] * len(extra),
            out_specs=[block],
            aliases={6: 0} if extra else {},
            grid=(1,),
        )[0]

    def join(across, far):
        return flip(line(add_kernel, "join", [piece], [], [across, far])[0], 4, 2)

    def finish(held_parts, across):
        return line(sum_kernel, "finish", [piece], [], [*held_parts, across])[0]

    x = gather(inputs, gather_near)
    if lined:
        (out_grad,) = line(hold_kernel, "hold", [piece], [], [out_grad, x[2]])
    og = gather(out_grad, gather_line)
    out_parts, in_parts = parts_of(5), parts_of(4)
    hidden, hidden_turned, act, slope, *out_parts = line(
        functools.partial(forward_kernel, len(x), len(out_parts)),
        "forward",
        [narrow, turned, wide, wide, *out_parts],
        [held, acc, acc, total],
        [*x, weights],
        scalars,
    )
    if lined:
        out_held, across, far = scatter_first(out_parts)
    else:
        outputs = lax.psum_scatter(out_parts[0], "tensor", scatter_dimension=0)
    (x_turned,) = line(
        functools.partial(turn_kernel, len(x)), "turn", [SHAPE((features, size, rows), BF16)], [held], x, (me,)
    )
    if lined:
        across = join(across, far)
    gate_rows, up_rows = line(
        functools.partial(rows_kernel, len(og)),
        "row_grads",
        [narrow, narrow],
        [held, acc],
        [*og, weights, act, slope],
        scalars,
    )
    in_parts = line(
        functools.partial(input_kernel, len(in_parts)),
        "input_grads",
        in_parts,
        [total],
        [gate_rows, up_rows, weights],
        scalars,
    )
    if lined:
        in_held, in_across, in_far = scatter_first(in_parts)
    else:
        input_grad = lax.psum_scatter(in_parts[0], "tensor", scatter_dimension=0)
    down = grads(2, og, hidden_turned)
    gate = grads(0, [gate_rows], x_turned)
    down = fold(*down, 0)
    if lined:
        in_across = join(in_across, in_far)
    up = grads(1, [up_rows], x_turned)
    gate = fold(*gate, 0)
    if lined:
        outputs = finish(out_held, across)
    for step in range(1, levels):
        down = fold(*down, step)
        if step == 1:
            up = fold(*up, 0)
        gate = fold(*gate, step)
    buffer = update(2, *down, None)
    for step in range(1, levels):
        up = fold(*up, step)
    buffer = update(0, *gate, buffer)
    if lined:
        input_grad = finish(in_held, in_across)
    buffer = update(1, *up, buffer)
    return (outputs, input_grad, buffer)


def solution(mesh):
    in_specs = (
        P("dp", "tensor"),
        P("dp", "tensor"),
        P(None, "tensor", None, None),
        P(None, "tensor", None),
        P("tensor", None),
        P(None, ("tensor", "dp"), None, None),
        P(None, ("tensor", "dp"), None, None),
    )
    out_specs = (P("dp", "tensor"), P("dp", "tensor"), P(None, ("tensor", "dp"), None, None))
    body = functools.partial(local, mesh.shape["dp"], mesh.shape["tensor"])
    return jax.shard_map(body, mesh=mesh, in_specs=in_specs, out_specs=out_specs, check_vma=False)
```

```python
import functools
import jax
import jax.numpy as jnp
from jax import lax
from jax.experimental import pallas as pl
from jax.experimental.pallas import tpu as pltpu
from jax.sharding import PartitionSpec as P

HB_DEV = 14
EPSILON = 1e-08
GROUP = 16
COST = 10**10
VMEM_LIMIT = 32 * 1024 * 1024
F32, BF16 = jnp.float32, jnp.bfloat16
SHAPE = jax.ShapeDtypeStruct
SMEM = pl.BlockSpec(memory_space=pltpu.SMEM)
VMEM = pl.BlockSpec(memory_space=pltpu.VMEM)
ANY = pl.BlockSpec(memory_space=pl.ANY)
TOKEN = SHAPE((1,), jnp.int32)


def group_of(capacity):
    return next(g for g in (GROUP, 8, 4, 2, 1) if capacity % g == 0)


def feature_block(ref, block, size):
    per_shard = ref.shape[2] // size
    start = pl.multiple_of(lax.rem(block, per_shard) * size, size)
    return ref.at[lax.div(block, per_shard), :, pl.ds(start, size)]


def slot_pair(index_ref, matrix, slot, capacity):
    at = (matrix * capacity + slot) * 2
    return index_ref[at], index_ref[at + 1]


def each_group(count, group, body):
    def step(i, carry):
        body([i * group + u for u in range(group)])
        return carry

    lax.fori_loop(0, lax.div(count + (group - 1), group), step, 0)


def dot(a, b, contract):
    return lax.dot_general(a, b, (contract, ((), ())), preferred_element_type=F32)


def accumulate(index_ref, matrix, count, capacity, acc, into, product):
    trash = acc.shape[0] - 1

    def body(slots):
        products, targets = [], []
        for s in slots:
            pair = slot_pair(index_ref, matrix, s, capacity)
            targets.append(jnp.where(s < count, pair[into], trash))
            products.append(product(s, *pair))
        for t, p in zip(targets, products):
            acc[t] += p

    each_group(count, group_of(capacity), body)


def load_shards(pieces, held, me):
    if len(pieces) == 1:
        return pieces[0]
    if len(pieces) == 4:
        for offset, piece in enumerate(pieces):
            held[lax.bitwise_xor(me, offset)] = piece[...]
        return held
    own, below, above, across, far = pieces
    last = held.shape[0] - 1
    held[me] = own[...]
    held[lax.bitwise_xor(me, 2)] = across[...]

    @pl.when(me > 0)
    def _():
        held[me - 1] = below[...]

    @pl.when(me < last)
    def _():
        held[me + 1] = above[...]

    @pl.when((me == 0) | (me == last))
    def _():
        held[last - me] = far[...]

    return held


def store_shards(total, outs, me, per_shard, size):
    if len(outs) == 1:
        places = [(outs[0].at[t], t) for t in range(outs[0].shape[0])]
    elif len(outs) == 4:
        places = [(out, lax.bitwise_xor(me, offset)) for offset, out in enumerate(outs)]
    else:
        last = len(outs) - 2
        own, below, above, across, far = outs
        places = [
            (own, me),
            (below, jnp.maximum(me - 1, 0)),
            (above, jnp.minimum(me + 1, last)),
            (across, lax.bitwise_xor(me, 2)),
            (far, last - me),
        ]
    for out, t in places:
        for c in range(per_shard):
            out[:, c * size : (c + 1) * size] = total[t * per_shard + c].astype(out.dtype)


def forward_kernel(n_pieces, n_outs, me_ref, index_ref, count_ref, *refs):
    pieces, refs = refs[:n_pieces], refs[n_pieces:]
    w_ref, hidden_ref, turned_ref, act_ref, slope_ref = refs[:5]
    outs, (held, gate, up, total) = refs[5 : 5 + n_outs], refs[5 + n_outs :]
    me = me_ref[0]
    x_ref = load_shards(pieces, held, me)
    capacity, size = w_ref.shape[1], w_ref.shape[2]
    gate[...] = jnp.zeros_like(gate)
    up[...] = jnp.zeros_like(up)
    total[...] = jnp.zeros_like(total)
    for matrix, acc in ((0, gate), (1, up)):
        accumulate(
            index_ref, matrix, count_ref[matrix], capacity, acc, 1,
            lambda s, f, h, matrix=matrix: dot(feature_block(x_ref, f, size)[...], w_ref[matrix, s], ((1,), (0,))),
        )
    for h in range(hidden_ref.shape[0]):
        g, u = gate[h], up[h]
        sig = 1.0 / (1.0 + jnp.exp(-g))
        act = g * sig
        act_ref[h] = act
        slope_ref[h] = u * sig * (1.0 + g * (1.0 - sig))
        hidden = (act * u).astype(hidden_ref.dtype)
        hidden_ref[h] = hidden
        turned_ref[h] = hidden.T
    accumulate(
        index_ref, 2, count_ref[2], capacity, total, 0,
        lambda s, f, h: dot(hidden_ref[h], w_ref[2, s], ((1,), (0,))),
    )
    store_shards(total, outs, me, x_ref.shape[2] // size, size)


def turn_kernel(n_pieces, me_ref, *refs):
    pieces, (turned_ref, held) = refs[:n_pieces], refs[n_pieces:]
    x_ref = load_shards(pieces, held, me_ref[0])
    size = turned_ref.shape[1]
    per_shard = x_ref.shape[2] // size
    for f in range(turned_ref.shape[0]):
        c = f % per_shard
        turned_ref[f] = x_ref[f // per_shard, :, c * size : (c + 1) * size].T


def rows_kernel(n_pieces, me_ref, index_ref, count_ref, *refs):
    pieces, refs = refs[:n_pieces], refs[n_pieces:]
    w_ref, act_ref, slope_ref, gate_rows_ref, up_rows_ref, held, acc = refs
    og_ref = load_shards(pieces, held, me_ref[0])
    capacity, size = w_ref.shape[1], w_ref.shape[2]
    acc[...] = jnp.zeros_like(acc)
    accumulate(
        index_ref, 2, count_ref[2], capacity, acc, 1,
        lambda s, f, h: dot(feature_block(og_ref, f, size)[...], w_ref[2, s], ((1,), (1,))),
    )
    for h in range(act_ref.shape[0]):
        gate_rows_ref[h] = (acc[h] * slope_ref[h]).astype(gate_rows_ref.dtype)
        up_rows_ref[h] = (acc[h] * act_ref[h]).astype(up_rows_ref.dtype)


def spread(place, core, places):
    levels = places.bit_length() - 1
    turned = sum(lax.shift_left(lax.bitwise_and(lax.shift_right_logical(place, b), 1), levels - 1 - b) for b in range(levels))
    return 2 * jnp.where(core == 0, place, turned)


def grads_kernel(matrix, n_pieces, me_ref, index_ref, count_ref, *refs):
    pieces, refs = refs[:n_pieces], refs[n_pieces:]
    turned_ref, keep_ref, send_ref, held = refs
    size, share = keep_ref.shape[2], keep_ref.shape[1]
    places = keep_ref.shape[0]
    replica = me_ref[1]
    right_ref = load_shards(pieces, held, me_ref[0])
    capacity = 2 * places * share
    count = count_ref[matrix]
    for out, bit in ((send_ref, 1), (keep_ref, 0)):

        def one_place(q, carry, out=out, bit=bit):
            owner = lax.bitwise_xor(replica, bit)
            first = lax.bitwise_xor(owner, spread(q, lax.bitwise_and(owner, 1), places)) * share

            @pl.when(first < count)
            def _():
                for s in range(share):
                    f, h = slot_pair(index_ref, matrix, first + s, capacity)
                    if matrix == 2:
                        left, right = turned_ref[h], feature_block(right_ref, f, size)[...]
                    else:
                        left, right = turned_ref[f], right_ref[h]
                    out[q, s] = dot(left, right, ((1,), (0,))).astype(out.dtype)

            return carry

        lax.fori_loop(0, places, one_place, 0)


def input_kernel(n_outs, me_ref, index_ref, count_ref, gate_rows_ref, up_rows_ref, w_ref, *refs):
    outs, (total,) = refs[:n_outs], refs[n_outs:]
    capacity, size = w_ref.shape[1], w_ref.shape[2]
    total[...] = jnp.zeros_like(total)
    for matrix, rows in ((0, gate_rows_ref), (1, up_rows_ref)):
        accumulate(
            index_ref, matrix, count_ref[matrix], capacity, total, 0,
            lambda s, f, h, matrix=matrix, rows=rows: dot(rows[h], w_ref[matrix, s], ((1,), (1,))),
        )
    store_shards(total, outs, me_ref[0], outs[0].shape[-1] // size, size)


def fold_kernel(keep_ref, got_ref, keep_out, send_out):
    half = keep_out.shape[0]
    keep_out[...] = keep_ref[:half] + got_ref[:half]
    send_out[...] = keep_ref[half:] + got_ref[half:]


def join_kernel(*refs):
    ins, outs = refs[: len(refs) // 2 + 1], refs[len(refs) // 2 + 1 :]
    outs[0][...] = ins[0][...] + ins[1][...]
    for source, out in zip(ins[2:], outs[1:]):
        out[...] = source[...]


def sum_kernel(*refs):
    *parts, out_ref = refs
    total = parts[0][...].astype(F32)
    for part in parts[1:]:
        total += part[...].astype(F32)
    out_ref[...] = total.astype(out_ref.dtype)


def update_kernel(matrix, me_ref, count_ref, keep_ref, got_ref, m1_ref, m2_ref, *refs):
    out_ref = refs[-1]
    share = keep_ref.shape[1]
    first = me_ref[1] * share
    for s in range(share):
        g = keep_ref[0, s].astype(F32) + got_ref[0, s].astype(F32)
        first_new = 0.9 * m1_ref[0, s] + 0.1 * g
        second_new = 0.95 * m2_ref[0, s] + 0.05 * g * g
        live = first + s < count_ref[matrix]
        out_ref[0, s] = jnp.where(live, first_new / (jnp.sqrt(second_new) + EPSILON), 0.0)


def hold_kernel(v_ref, _, out_ref):
    out_ref[...] = v_ref[...]


class Line:
    token = None

    def __call__(self, kernel, name, outs, scratch, operands, scalars=(), specs=None, out_specs=None, aliases=None, cost=COST, **more):
        tokens = [] if self.token is None else [self.token]
        n_in, n_out = len(scalars) + len(operands), len(outs)

        def body(*refs):
            ins, rest = refs[:n_in], refs[n_in + len(tokens) :]
            results, token, scratches = rest[:n_out], rest[n_out], rest[n_out + 1 :]
            token[0] = 0
            kernel(*ins, *results, *scratches)

        *results, self.token = pl.pallas_call(
            body,
            name=name,
            out_shape=[*outs, TOKEN],
            in_specs=[SMEM] * len(scalars) + (specs or [VMEM] * len(operands)) + [SMEM] * len(tokens),
            out_specs=[*(out_specs or [VMEM] * n_out), SMEM],
            scratch_shapes=scratch,
            input_output_aliases=aliases or {},
            compiler_params=pltpu.CompilerParams(vmem_limit_bytes=VMEM_LIMIT),
            cost_estimate=pl.CostEstimate(flops=cost, bytes_accessed=0, transcendentals=0),
            **more,
        )(*scalars, *operands, *tokens)
        return results


def flip(v, shards, bit):
    return lax.ppermute(v, "tensor", [(a, a ^ bit) for a in range(shards)])


def gather_near(v):
    across, beside = flip(v, 4, 2), flip(v, 4, 1)
    return [v, beside, across, flip(across, 4, 1)]


def gather_line(v):
    across = flip(v, 4, 2)
    below = lax.ppermute(v, "tensor", [(a, a + 1) for a in range(3)])
    above = lax.ppermute(v, "tensor", [(a + 1, a) for a in range(3)])
    far = lax.ppermute(across, "tensor", [(2, 3), (1, 0)])
    return [v, below, above, across, far]


def scatter_first(parts):
    if len(parts) == 4:
        return flip(parts[3], 4, 1)
    return lax.ppermute(parts[4], "tensor", [(3, 2), (0, 1)])


def scatter_second(line, parts, far):
    piece = SHAPE(far.shape, far.dtype)
    if len(parts) == 4:
        own, beside, across, _ = parts
        across, beside = line(join_kernel, "join", [piece] * 2, [], [across, far, beside])
        return [own, flip(across, 4, 2), flip(beside, 4, 1)]
    own, below, above, across, _ = parts
    across, below, above = line(join_kernel, "join", [piece] * 3, [], [across, far, below, above])
    below = lax.ppermute(below, "tensor", [(a + 1, a) for a in range(3)])
    above = lax.ppermute(above, "tensor", [(a, a + 1) for a in range(3)])
    return [own, flip(across, 4, 2), below, above]


def core_swap(v, replicas):
    return lax.ppermute(v, "dp", [(a, a ^ 1) for a in range(replicas)])


def axis_swap(v, replicas, step):
    levels = replicas.bit_length() - 2
    pairs = [(a, a ^ (1 << (1 + step if a & 1 else levels - step))) for a in range(replicas)]
    return lax.ppermute(v, "dp", pairs)


def local(replicas, shards, inputs, out_grad, weights, block_index, block_counts, first_moment, second_moment):
    capacity, size = weights.shape[1], weights.shape[2]
    rows, width = inputs.shape
    me = jnp.stack([lax.axis_index("tensor"), lax.axis_index("dp")]).astype(jnp.int32)
    scalars = (me, block_index.reshape(-1), block_counts[0])
    features = shards * width // size
    places, share = replicas // 2, capacity // replicas
    levels = places.bit_length() - 1
    held = pltpu.VMEM((shards, rows, width), BF16)
    acc = pltpu.VMEM((HB_DEV + 1, rows, size), F32)
    total = pltpu.VMEM((features + 1, rows, size), F32)
    wide = SHAPE((HB_DEV, rows, size), F32)
    narrow = SHAPE((HB_DEV, rows, size), BF16)
    turned = SHAPE((HB_DEV, size, rows), BF16)
    piece = SHAPE((rows, width), BF16)
    line = Line()
    lined = shards == 4

    def gather(v, form):
        return form(v) if lined else [lax.all_gather(v, "tensor", axis=0)]

    def parts_of(count):
        return [piece] * count if lined else [SHAPE((shards, rows, width), BF16)]

    def grads(matrix, right, left):
        half = SHAPE((places, share, size, size), BF16)
        name = ("gate_grads", "up_grads", "down_grads")[matrix]
        kernel = functools.partial(grads_kernel, matrix, len(right))
        keep, send = line(kernel, name, [half, half], [held], [*right, left], scalars)
        return keep, core_swap(send, replicas)

    def fold(keep, got, step):
        half = SHAPE((keep.shape[0] // 2, *keep.shape[1:]), BF16)
        keep, send = line(fold_kernel, "fold", [half, half], [], [keep, got])
        return keep, axis_swap(send, replicas, step)

    def update(matrix, keep, got, buffer):
        block = pl.BlockSpec((1, share, size, size), lambda i: (matrix, 0, 0, 0))
        extra = [] if buffer is None else [buffer]
        return line(
            functools.partial(update_kernel, matrix),
            "update",
            [SHAPE(first_moment.shape, F32)],
            [],
            [keep, got, first_moment, second_moment, *extra],
            (me, scalars[2]),
            specs=[VMEM, VMEM, block, block] + [ANY] * len(extra),
            out_specs=[block],
            aliases={6: 0} if extra else {},
            grid=(1,),
        )[0]

    def finish(held_parts):
        return line(sum_kernel, "finish", [piece], [], held_parts)[0]

    x = gather(inputs, gather_near)
    if lined:
        (out_grad,) = line(hold_kernel, "hold", [piece], [], [out_grad, x[2]])
    og = gather(out_grad, gather_line)
    out_parts, in_parts = parts_of(5), parts_of(4)
    hidden, hidden_turned, act, slope, *out_parts = line(
        functools.partial(forward_kernel, len(x), len(out_parts)),
        "forward",
        [narrow, turned, wide, wide, *out_parts],
        [held, acc, acc, total],
        [*x, weights],
        scalars,
    )
    if lined:
        out_far = scatter_first(out_parts)
    else:
        outputs = lax.psum_scatter(out_parts[0], "tensor", scatter_dimension=0)
    (x_turned,) = line(
        functools.partial(turn_kernel, len(x)), "turn", [SHAPE((features, size, rows), BF16)], [held], x, (me,)
    )
    if lined:
        out_sums = scatter_second(line, out_parts, out_far)
    gate_rows, up_rows = line(
        functools.partial(rows_kernel, len(og)),
        "row_grads",
        [narrow, narrow],
        [held, acc],
        [*og, weights, act, slope],
        scalars,
    )
    down = grads(2, og, hidden_turned)
    in_parts = line(
        functools.partial(input_kernel, len(in_parts)),
        "input_grads",
        in_parts,
        [total],
        [gate_rows, up_rows, weights],
        scalars,
    )
    if lined:
        in_far = scatter_first(in_parts)
    else:
        input_grad = lax.psum_scatter(in_parts[0], "tensor", scatter_dimension=0)
    if lined:
        outputs = finish(out_sums)
    down = fold(*down, 0)
    gate = grads(0, [gate_rows], x_turned)
    up = grads(1, [up_rows], x_turned)
    if lined:
        in_sums = scatter_second(line, in_parts, in_far)
    gate = fold(*gate, 0)
    for step in range(1, levels):
        down = fold(*down, step)
        if step == 1:
            up = fold(*up, 0)
        gate = fold(*gate, step)
    buffer = update(2, *down, None)
    for step in range(1, levels):
        up = fold(*up, step)
    buffer = update(0, *gate, buffer)
    if lined:
        input_grad = finish(in_sums)
    buffer = update(1, *up, buffer)
    return (outputs, input_grad, buffer)


def solution(mesh):
    in_specs = (
        P("dp", "tensor"),
        P("dp", "tensor"),
        P(None, "tensor", None, None),
        P(None, "tensor", None),
        P("tensor", None),
        P(None, ("tensor", "dp"), None, None),
        P(None, ("tensor", "dp"), None, None),
    )
    out_specs = (P("dp", "tensor"), P("dp", "tensor"), P(None, ("tensor", "dp"), None, None))
    body = functools.partial(local, mesh.shape["dp"], mesh.shape["tensor"])
    return jax.shard_map(body, mesh=mesh, in_specs=in_specs, out_specs=out_specs, check_vma=False)
```

```python
import functools
import jax
import jax.numpy as jnp
from jax import lax
from jax.experimental import pallas as pl
from jax.experimental.pallas import tpu as pltpu
from jax.sharding import PartitionSpec as P

HB_DEV = 14
EPSILON = 1e-08
GROUP = 16
COST = 2 * 10**10
VMEM_LIMIT = 32 * 1024 * 1024
F32, BF16 = jnp.float32, jnp.bfloat16
SHAPE = jax.ShapeDtypeStruct
SMEM = pl.BlockSpec(memory_space=pltpu.SMEM)
VMEM = pl.BlockSpec(memory_space=pltpu.VMEM)
ANY = pl.BlockSpec(memory_space=pl.ANY)
TOKEN = SHAPE((1,), jnp.int32)


def group_of(capacity):
    return next(g for g in (GROUP, 8, 4, 2, 1) if capacity % g == 0)


def feature_block(ref, block, size):
    per_shard = ref.shape[2] // size
    start = pl.multiple_of(lax.rem(block, per_shard) * size, size)
    return ref.at[lax.div(block, per_shard), :, pl.ds(start, size)]


def slot_pair(index_ref, matrix, slot, capacity):
    at = (matrix * capacity + slot) * 2
    return index_ref[at], index_ref[at + 1]


def each_group(count, group, body):
    def step(i, carry):
        body([i * group + u for u in range(group)])
        return carry

    lax.fori_loop(0, lax.div(count + (group - 1), group), step, 0)


def dot(a, b, contract):
    return lax.dot_general(a, b, (contract, ((), ())), preferred_element_type=F32)


def accumulate(index_ref, matrix, count, capacity, acc, into, product):
    trash = acc.shape[0] - 1

    def body(slots):
        products, targets = [], []
        for s in slots:
            pair = slot_pair(index_ref, matrix, s, capacity)
            targets.append(jnp.where(s < count, pair[into], trash))
            products.append(product(s, *pair))
        for t, p in zip(targets, products):
            acc[t] += p

    each_group(count, group_of(capacity), body)


def load_shards(pieces, held, me):
    if len(pieces) == 1:
        return pieces[0]
    if len(pieces) == 4:
        for offset, piece in enumerate(pieces):
            held[lax.bitwise_xor(me, offset)] = piece[...]
        return held
    own, below, above, across, far = pieces
    last = held.shape[0] - 1
    held[me] = own[...]
    held[lax.bitwise_xor(me, 2)] = across[...]

    @pl.when(me > 0)
    def _():
        held[me - 1] = below[...]

    @pl.when(me < last)
    def _():
        held[me + 1] = above[...]

    @pl.when((me == 0) | (me == last))
    def _():
        held[last - me] = far[...]

    return held


def store_shards(total, outs, me, per_shard, size):
    if len(outs) == 1:
        places = [(outs[0].at[t], t) for t in range(outs[0].shape[0])]
    elif len(outs) == 4:
        places = [(out, lax.bitwise_xor(me, offset)) for offset, out in enumerate(outs)]
    else:
        last = 3
        own, beside, across, far, middle = outs
        places = [(out, lax.bitwise_xor(me, offset)) for offset, out in enumerate((own, beside, across, far))]
        places.append((middle, last - me))
    for out, t in places:
        for c in range(per_shard):
            out[:, c * size : (c + 1) * size] = total[t * per_shard + c].astype(out.dtype)


def forward_kernel(n_pieces, n_outs, me_ref, index_ref, count_ref, *refs):
    pieces, refs = refs[:n_pieces], refs[n_pieces:]
    w_ref, hidden_ref, turned_ref, act_ref, slope_ref = refs[:5]
    outs, (held, gate, up, total) = refs[5 : 5 + n_outs], refs[5 + n_outs :]
    me = me_ref[0]
    x_ref = load_shards(pieces, held, me)
    capacity, size = w_ref.shape[1], w_ref.shape[2]
    gate[...] = jnp.zeros_like(gate)
    up[...] = jnp.zeros_like(up)
    total[...] = jnp.zeros_like(total)
    for matrix, acc in ((0, gate), (1, up)):
        accumulate(
            index_ref, matrix, count_ref[matrix], capacity, acc, 1,
            lambda s, f, h, matrix=matrix: dot(feature_block(x_ref, f, size)[...], w_ref[matrix, s], ((1,), (0,))),
        )
    for h in range(hidden_ref.shape[0]):
        g, u = gate[h], up[h]
        sig = 1.0 / (1.0 + jnp.exp(-g))
        act = g * sig
        act_ref[h] = act
        slope_ref[h] = u * sig * (1.0 + g * (1.0 - sig))
        hidden = (act * u).astype(hidden_ref.dtype)
        hidden_ref[h] = hidden
        turned_ref[h] = hidden.T
    accumulate(
        index_ref, 2, count_ref[2], capacity, total, 0,
        lambda s, f, h: dot(hidden_ref[h], w_ref[2, s], ((1,), (0,))),
    )
    store_shards(total, outs, me, x_ref.shape[2] // size, size)


def turn_kernel(n_pieces, me_ref, *refs):
    pieces, (turned_ref, held) = refs[:n_pieces], refs[n_pieces:]
    x_ref = load_shards(pieces, held, me_ref[0])
    size = turned_ref.shape[1]
    per_shard = x_ref.shape[2] // size
    for f in range(turned_ref.shape[0]):
        c = f % per_shard
        turned_ref[f] = x_ref[f // per_shard, :, c * size : (c + 1) * size].T


def rows_kernel(n_pieces, me_ref, index_ref, count_ref, *refs):
    pieces, refs = refs[:n_pieces], refs[n_pieces:]
    w_ref, act_ref, slope_ref, gate_rows_ref, up_rows_ref, held, acc = refs
    og_ref = load_shards(pieces, held, me_ref[0])
    capacity, size = w_ref.shape[1], w_ref.shape[2]
    acc[...] = jnp.zeros_like(acc)
    accumulate(
        index_ref, 2, count_ref[2], capacity, acc, 1,
        lambda s, f, h: dot(feature_block(og_ref, f, size)[...], w_ref[2, s], ((1,), (1,))),
    )
    for h in range(act_ref.shape[0]):
        gate_rows_ref[h] = (acc[h] * slope_ref[h]).astype(gate_rows_ref.dtype)
        up_rows_ref[h] = (acc[h] * act_ref[h]).astype(up_rows_ref.dtype)


def spread(place, core, places):
    levels = places.bit_length() - 1
    turned = sum(lax.shift_left(lax.bitwise_and(lax.shift_right_logical(place, b), 1), levels - 1 - b) for b in range(levels))
    return 2 * jnp.where(core == 0, place, turned)


def grads_kernel(matrix, n_pieces, me_ref, index_ref, count_ref, *refs):
    pieces, refs = refs[:n_pieces], refs[n_pieces:]
    turned_ref, keep_ref, send_ref, held = refs
    size, share = keep_ref.shape[2], keep_ref.shape[1]
    places = keep_ref.shape[0]
    replica = me_ref[1]
    right_ref = load_shards(pieces, held, me_ref[0])
    capacity = 2 * places * share
    count = count_ref[matrix]
    for out, bit in ((send_ref, 1), (keep_ref, 0)):

        def one_place(q, carry, out=out, bit=bit):
            owner = lax.bitwise_xor(replica, bit)
            first = lax.bitwise_xor(owner, spread(q, lax.bitwise_and(owner, 1), places)) * share

            @pl.when(first < count)
            def _():
                for s in range(share):
                    f, h = slot_pair(index_ref, matrix, first + s, capacity)
                    if matrix == 2:
                        left, right = turned_ref[h], feature_block(right_ref, f, size)[...]
                    else:
                        left, right = turned_ref[f], right_ref[h]
                    out[q, s] = dot(left, right, ((1,), (0,))).astype(out.dtype)

            return carry

        lax.fori_loop(0, places, one_place, 0)


def input_kernel(n_outs, me_ref, index_ref, count_ref, gate_rows_ref, up_rows_ref, w_ref, *refs):
    outs, (total,) = refs[:n_outs], refs[n_outs:]
    capacity, size = w_ref.shape[1], w_ref.shape[2]
    total[...] = jnp.zeros_like(total)
    for matrix, rows in ((0, gate_rows_ref), (1, up_rows_ref)):
        accumulate(
            index_ref, matrix, count_ref[matrix], capacity, total, 0,
            lambda s, f, h, matrix=matrix, rows=rows: dot(rows[h], w_ref[matrix, s], ((1,), (1,))),
        )
    store_shards(total, outs, me_ref[0], outs[0].shape[-1] // size, size)


def fold_kernel(keep_ref, got_ref, keep_out, send_out):
    half = keep_out.shape[0]
    keep_out[...] = keep_ref[:half] + got_ref[:half]
    send_out[...] = keep_ref[half:] + got_ref[half:]


def join_kernel(*refs):
    ins, outs = refs[: len(refs) // 2 + 1], refs[len(refs) // 2 + 1 :]
    outs[0][...] = ins[0][...] + ins[1][...]
    for source, out in zip(ins[2:], outs[1:]):
        out[...] = source[...]


def sum_kernel(*refs):
    *parts, out_ref = refs
    total = parts[0][...].astype(F32)
    for part in parts[1:]:
        total += part[...].astype(F32)
    out_ref[...] = total.astype(out_ref.dtype)


def update_kernel(matrix, me_ref, count_ref, keep_ref, got_ref, m1_ref, m2_ref, *refs):
    out_ref = refs[-1]
    share = keep_ref.shape[1]
    first = me_ref[1] * share
    for s in range(share):
        g = keep_ref[0, s].astype(F32) + got_ref[0, s].astype(F32)
        first_new = 0.9 * m1_ref[0, s] + 0.1 * g
        second_new = 0.95 * m2_ref[0, s] + 0.05 * g * g
        live = first + s < count_ref[matrix]
        out_ref[0, s] = jnp.where(live, first_new / (jnp.sqrt(second_new) + EPSILON), 0.0)


def hold_kernel(v_ref, _, out_ref):
    out_ref[...] = v_ref[...]


class Line:
    token = None

    def __call__(self, kernel, name, outs, scratch, operands, scalars=(), specs=None, out_specs=None, aliases=None, cost=COST, **more):
        tokens = [] if self.token is None else [self.token]
        n_in, n_out = len(scalars) + len(operands), len(outs)

        def body(*refs):
            ins, rest = refs[:n_in], refs[n_in + len(tokens) :]
            results, token, scratches = rest[:n_out], rest[n_out], rest[n_out + 1 :]
            token[0] = 0
            kernel(*ins, *results, *scratches)

        *results, self.token = pl.pallas_call(
            body,
            name=name,
            out_shape=[*outs, TOKEN],
            in_specs=[SMEM] * len(scalars) + (specs or [VMEM] * len(operands)) + [SMEM] * len(tokens),
            out_specs=[*(out_specs or [VMEM] * n_out), SMEM],
            scratch_shapes=scratch,
            input_output_aliases=aliases or {},
            compiler_params=pltpu.CompilerParams(vmem_limit_bytes=VMEM_LIMIT),
            cost_estimate=pl.CostEstimate(flops=cost, bytes_accessed=0, transcendentals=0),
            **more,
        )(*scalars, *operands, *tokens)
        return results


def flip(v, shards, bit):
    return lax.ppermute(v, "tensor", [(a, a ^ bit) for a in range(shards)])


def gather_near(v):
    across, beside = flip(v, 4, 2), flip(v, 4, 1)
    return [v, beside, across, flip(across, 4, 1)]


def gather_line(v):
    across = flip(v, 4, 2)
    below = lax.ppermute(v, "tensor", [(a, a + 1) for a in range(3)])
    above = lax.ppermute(v, "tensor", [(a + 1, a) for a in range(3)])
    far = lax.ppermute(across, "tensor", [(2, 3), (1, 0)])
    return [v, below, above, across, far]


def scatter_first(parts):
    if len(parts) == 4:
        return [flip(parts[3], 4, 1)]
    return [lax.ppermute(parts[3], "tensor", [(0, 1), (3, 2)]), lax.ppermute(parts[4], "tensor", [(1, 2), (2, 1)])]


def scatter_second(line, parts, came):
    piece = SHAPE(parts[0].shape, parts[0].dtype)
    own, beside, across = parts[:3]
    across, beside, *came = line(join_kernel, "join", [piece] * (1 + len(came)), [], [across, came[0], beside, *came[1:]])
    return [own, flip(across, 4, 2), flip(beside, 4, 1), *came]


def core_swap(v, replicas):
    return lax.ppermute(v, "dp", [(a, a ^ 1) for a in range(replicas)])


def axis_swap(v, replicas, step):
    levels = replicas.bit_length() - 2
    pairs = [(a, a ^ (1 << (1 + step if a & 1 else levels - step))) for a in range(replicas)]
    return lax.ppermute(v, "dp", pairs)


def local(replicas, shards, inputs, out_grad, weights, block_index, block_counts, first_moment, second_moment):
    capacity, size = weights.shape[1], weights.shape[2]
    rows, width = inputs.shape
    me = jnp.stack([lax.axis_index("tensor"), lax.axis_index("dp")]).astype(jnp.int32)
    scalars = (me, block_index.reshape(-1), block_counts[0])
    features = shards * width // size
    places, share = replicas // 2, capacity // replicas
    levels = places.bit_length() - 1
    held = pltpu.VMEM((shards, rows, width), BF16)
    acc = pltpu.VMEM((HB_DEV + 1, rows, size), F32)
    total = pltpu.VMEM((features + 1, rows, size), F32)
    wide = SHAPE((HB_DEV, rows, size), F32)
    narrow = SHAPE((HB_DEV, rows, size), BF16)
    turned = SHAPE((HB_DEV, size, rows), BF16)
    piece = SHAPE((rows, width), BF16)
    line = Line()
    lined = shards == 4

    def gather(v, form):
        return form(v) if lined else [lax.all_gather(v, "tensor", axis=0)]

    def parts_of(count):
        return [piece] * count if lined else [SHAPE((shards, rows, width), BF16)]

    def grads(matrix, right, left):
        half = SHAPE((places, share, size, size), BF16)
        name = ("gate_grads", "up_grads", "down_grads")[matrix]
        kernel = functools.partial(grads_kernel, matrix, len(right))
        keep, send = line(kernel, name, [half, half], [held], [*right, left], scalars)
        return keep, core_swap(send, replicas)

    def fold(keep, got, step):
        half = SHAPE((keep.shape[0] // 2, *keep.shape[1:]), BF16)
        keep, send = line(fold_kernel, "fold", [half, half], [], [keep, got])
        return keep, axis_swap(send, replicas, step)

    def update(matrix, keep, got, buffer):
        block = pl.BlockSpec((1, share, size, size), lambda i: (matrix, 0, 0, 0))
        extra = [] if buffer is None else [buffer]
        return line(
            functools.partial(update_kernel, matrix),
            "update",
            [SHAPE(first_moment.shape, F32)],
            [],
            [keep, got, first_moment, second_moment, *extra],
            (me, scalars[2]),
            specs=[VMEM, VMEM, block, block] + [ANY] * len(extra),
            out_specs=[block],
            aliases={6: 0} if extra else {},
            grid=(1,),
        )[0]

    def finish(held_parts):
        return line(sum_kernel, "finish", [piece], [], held_parts)[0]

    x = gather(inputs, gather_near)
    if lined:
        (out_grad,) = line(hold_kernel, "hold", [piece], [], [out_grad, x[2]])
    og = gather(out_grad, gather_line)
    out_parts, in_parts = parts_of(5), parts_of(4)
    hidden, hidden_turned, act, slope, *out_parts = line(
        functools.partial(forward_kernel, len(x), len(out_parts)),
        "forward",
        [narrow, turned, wide, wide, *out_parts],
        [held, acc, acc, total],
        [*x, weights],
        scalars,
    )
    if lined:
        out_far = scatter_first(out_parts)
    else:
        outputs = lax.psum_scatter(out_parts[0], "tensor", scatter_dimension=0)
    (x_turned,) = line(
        functools.partial(turn_kernel, len(x)), "turn", [SHAPE((features, size, rows), BF16)], [held], x, (me,)
    )
    if lined:
        out_sums = scatter_second(line, out_parts, out_far)
    down = grads(2, og, hidden_turned)
    gate_rows, up_rows = line(
        functools.partial(rows_kernel, len(og)),
        "row_grads",
        [narrow, narrow],
        [held, acc],
        [*og, weights, act, slope],
        scalars,
    )
    down = fold(*down, 0)
    in_parts = line(
        functools.partial(input_kernel, len(in_parts)),
        "input_grads",
        in_parts,
        [total],
        [gate_rows, up_rows, weights],
        scalars,
    )
    if lined:
        in_came = scatter_first(in_parts)
    else:
        input_grad = lax.psum_scatter(in_parts[0], "tensor", scatter_dimension=0)
    gate = grads(0, [gate_rows], x_turned)
    for step in range(1, levels):
        down = fold(*down, step)
    if lined:
        outputs = finish(out_sums)
    gate = fold(*gate, 0)
    up = grads(1, [up_rows], x_turned)
    if lined:
        in_sums = scatter_second(line, in_parts, in_came)
    for step in range(1, levels):
        gate = fold(*gate, step)
    up = fold(*up, 0)
    buffer = update(2, *down, None)
    buffer = update(0, *gate, buffer)
    for step in range(1, levels):
        up = fold(*up, step)
    if lined:
        input_grad = finish(in_sums)
    buffer = update(1, *up, buffer)
    return (outputs, input_grad, buffer)


def solution(mesh):
    in_specs = (
        P("dp", "tensor"),
        P("dp", "tensor"),
        P(None, "tensor", None, None),
        P(None, "tensor", None),
        P("tensor", None),
        P(None, ("tensor", "dp"), None, None),
        P(None, ("tensor", "dp"), None, None),
    )
    out_specs = (P("dp", "tensor"), P("dp", "tensor"), P(None, ("tensor", "dp"), None, None))
    body = functools.partial(local, mesh.shape["dp"], mesh.shape["tensor"])
    return jax.shard_map(body, mesh=mesh, in_specs=in_specs, out_specs=out_specs, check_vma=False)
```

```python
import functools
import jax
import jax.numpy as jnp
from jax import lax
from jax.experimental import pallas as pl
from jax.experimental.pallas import tpu as pltpu
from jax.sharding import PartitionSpec as P

HB_DEV = 14
EPSILON = 1e-08
GROUP = 16
COST = 2 * 10**10
VMEM_LIMIT = 32 * 1024 * 1024
F32, BF16 = jnp.float32, jnp.bfloat16
SHAPE = jax.ShapeDtypeStruct
SMEM = pl.BlockSpec(memory_space=pltpu.SMEM)
VMEM = pl.BlockSpec(memory_space=pltpu.VMEM)
ANY = pl.BlockSpec(memory_space=pl.ANY)
TOKEN = SHAPE((8, 128), F32)
HEAD = 5


def group_of(capacity):
    return next(g for g in (GROUP, 8, 4, 2, 1) if capacity % g == 0)


def feature_block(ref, block, size):
    per_shard = ref.shape[2] // size
    start = pl.multiple_of(lax.rem(block, per_shard) * size, size)
    return ref.at[lax.div(block, per_shard), :, pl.ds(start, size)]


def slot_pair(plan_ref, matrix, slot, capacity):
    at = HEAD + (matrix * capacity + slot) * 2
    return plan_ref[at], plan_ref[at + 1]


def each_group(count, group, body):
    def step(i, carry):
        body([i * group + u for u in range(group)])
        return carry

    lax.fori_loop(0, lax.div(count + (group - 1), group), step, 0)


def dot(a, b, contract):
    return lax.dot_general(a, b, (contract, ((), ())), preferred_element_type=F32)


def accumulate(plan_ref, matrix, capacity, acc, into, product):
    trash = acc.shape[0] - 1
    count = plan_ref[2 + matrix]

    def body(slots):
        products, targets = [], []
        for s in slots:
            pair = slot_pair(plan_ref, matrix, s, capacity)
            targets.append(jnp.where(s < count, pair[into], trash))
            products.append(product(s, *pair))
        for t, p in zip(targets, products):
            acc[t] += p

    each_group(count, group_of(capacity), body)


def load_shards(pieces, held, me):
    if len(pieces) == 1:
        return pieces[0]
    if len(pieces) == 4:
        for offset, piece in enumerate(pieces):
            held[lax.bitwise_xor(me, offset)] = piece[...]
        return held
    own, below, above, across, far = pieces
    last = held.shape[0] - 1
    held[me] = own[...]
    held[lax.bitwise_xor(me, 2)] = across[...]

    @pl.when(me > 0)
    def _():
        held[me - 1] = below[...]

    @pl.when(me < last)
    def _():
        held[me + 1] = above[...]

    @pl.when((me == 0) | (me == last))
    def _():
        held[last - me] = far[...]

    return held


def store_shards(total, outs, me, per_shard, size):
    if len(outs) == 1:
        places = [(outs[0].at[t], t) for t in range(outs[0].shape[0])]
    elif len(outs) == 4:
        places = [(out, lax.bitwise_xor(me, offset)) for offset, out in enumerate(outs)]
    else:
        last = 3
        own, beside, across, far, middle = outs
        places = [(out, lax.bitwise_xor(me, offset)) for offset, out in enumerate((own, beside, across, far))]
        places.append((middle, last - me))
    for out, t in places:
        for c in range(per_shard):
            out[:, c * size : (c + 1) * size] = total[t * per_shard + c].astype(out.dtype)


def forward_kernel(n_pieces, n_outs, plan_ref, *refs):
    pieces, refs = refs[:n_pieces], refs[n_pieces:]
    w_ref, hidden_ref, turned_ref, act_ref, slope_ref = refs[:5]
    outs, (held, gate, up, total) = refs[5 : 5 + n_outs], refs[5 + n_outs :]
    me = plan_ref[0]
    x_ref = load_shards(pieces, held, me)
    capacity, size = w_ref.shape[1], w_ref.shape[2]
    gate[...] = jnp.zeros_like(gate)
    up[...] = jnp.zeros_like(up)
    total[...] = jnp.zeros_like(total)
    for matrix, acc in ((0, gate), (1, up)):
        accumulate(
            plan_ref, matrix, capacity, acc, 1,
            lambda s, f, h, matrix=matrix: dot(feature_block(x_ref, f, size)[...], w_ref[matrix, s], ((1,), (0,))),
        )
    for h in range(hidden_ref.shape[0]):
        g, u = gate[h], up[h]
        sig = 1.0 / (1.0 + jnp.exp(-g))
        act = g * sig
        act_ref[h] = act
        slope_ref[h] = u * sig * (1.0 + g * (1.0 - sig))
        hidden = (act * u).astype(hidden_ref.dtype)
        hidden_ref[h] = hidden
        turned_ref[h] = hidden.T
    accumulate(
        plan_ref, 2, capacity, total, 0,
        lambda s, f, h: dot(hidden_ref[h], w_ref[2, s], ((1,), (0,))),
    )
    store_shards(total, outs, me, x_ref.shape[2] // size, size)


def turn_kernel(n_pieces, plan_ref, *refs):
    pieces, (turned_ref, held) = refs[:n_pieces], refs[n_pieces:]
    x_ref = load_shards(pieces, held, plan_ref[0])
    size = turned_ref.shape[1]
    per_shard = x_ref.shape[2] // size
    for f in range(turned_ref.shape[0]):
        c = f % per_shard
        turned_ref[f] = x_ref[f // per_shard, :, c * size : (c + 1) * size].T


def rows_kernel(n_pieces, plan_ref, *refs):
    pieces, refs = refs[:n_pieces], refs[n_pieces:]
    w_ref, act_ref, slope_ref, gate_rows_ref, up_rows_ref, held, acc = refs
    og_ref = load_shards(pieces, held, plan_ref[0])
    capacity, size = w_ref.shape[1], w_ref.shape[2]
    acc[...] = jnp.zeros_like(acc)
    accumulate(
        plan_ref, 2, capacity, acc, 1,
        lambda s, f, h: dot(feature_block(og_ref, f, size)[...], w_ref[2, s], ((1,), (1,))),
    )
    for h in range(act_ref.shape[0]):
        gate_rows_ref[h] = (acc[h] * slope_ref[h]).astype(gate_rows_ref.dtype)
        up_rows_ref[h] = (acc[h] * act_ref[h]).astype(up_rows_ref.dtype)


def spread(place, core, places):
    levels = places.bit_length() - 1
    turned = sum(lax.shift_left(lax.bitwise_and(lax.shift_right_logical(place, b), 1), levels - 1 - b) for b in range(levels))
    return 2 * jnp.where(core == 0, place, turned)


def grads_kernel(matrix, n_pieces, plan_ref, *refs):
    pieces, refs = refs[:n_pieces], refs[n_pieces:]
    turned_ref, keep_ref, send_ref, held = refs
    size, share = keep_ref.shape[2], keep_ref.shape[1]
    places = keep_ref.shape[0]
    replica = plan_ref[1]
    right_ref = load_shards(pieces, held, plan_ref[0])
    capacity = 2 * places * share
    count = plan_ref[2 + matrix]
    for out, bit in ((send_ref, 1), (keep_ref, 0)):

        def one_place(q, carry, out=out, bit=bit):
            owner = lax.bitwise_xor(replica, bit)
            first = lax.bitwise_xor(owner, spread(q, lax.bitwise_and(owner, 1), places)) * share

            @pl.when(first < count)
            def _():
                for s in range(share):
                    f, h = slot_pair(plan_ref, matrix, first + s, capacity)
                    if matrix == 2:
                        left, right = turned_ref[h], feature_block(right_ref, f, size)[...]
                    else:
                        left, right = turned_ref[f], right_ref[h]
                    out[q, s] = dot(left, right, ((1,), (0,))).astype(out.dtype)

            return carry

        lax.fori_loop(0, places, one_place, 0)


def input_kernel(n_outs, plan_ref, gate_rows_ref, up_rows_ref, w_ref, *refs):
    outs, (total,) = refs[:n_outs], refs[n_outs:]
    capacity, size = w_ref.shape[1], w_ref.shape[2]
    total[...] = jnp.zeros_like(total)
    for matrix, rows in ((0, gate_rows_ref), (1, up_rows_ref)):
        accumulate(
            plan_ref, matrix, capacity, total, 0,
            lambda s, f, h, matrix=matrix, rows=rows: dot(rows[h], w_ref[matrix, s], ((1,), (1,))),
        )
    store_shards(total, outs, plan_ref[0], outs[0].shape[-1] // size, size)


def fold_kernel(keep_ref, got_ref, keep_out, send_out):
    half = keep_out.shape[0]
    keep_out[...] = keep_ref[:half] + got_ref[:half]
    send_out[...] = keep_ref[half:] + got_ref[half:]


def join_kernel(*refs):
    ins, outs = refs[: len(refs) // 2 + 1], refs[len(refs) // 2 + 1 :]
    outs[0][...] = ins[0][...] + ins[1][...]
    for source, out in zip(ins[2:], outs[1:]):
        out[...] = source[...]


def sum_kernel(*refs):
    *parts, out_ref = refs
    total = parts[0][...].astype(F32)
    for part in parts[1:]:
        total += part[...].astype(F32)
    out_ref[...] = total.astype(out_ref.dtype)


def update_kernel(matrix, plan_ref, keep_ref, got_ref, m1_ref, m2_ref, *refs):
    out_ref = refs[-1]
    share = keep_ref.shape[1]
    first = plan_ref[1] * share
    for s in range(share):
        g = keep_ref[0, s].astype(F32) + got_ref[0, s].astype(F32)
        first_new = 0.9 * m1_ref[0, s] + 0.1 * g
        second_new = 0.95 * m2_ref[0, s] + 0.05 * g * g
        live = first + s < plan_ref[2 + matrix]
        out_ref[0, s] = jnp.where(live, first_new / (jnp.sqrt(second_new) + EPSILON), 0.0)


def hold_kernel(v_ref, _, out_ref):
    out_ref[...] = v_ref[...]


class Line:
    token = None

    def __call__(self, kernel, name, outs, scratch, operands, plan=None, after=(), specs=None, out_specs=None, **more):
        scalars = [] if plan is None else [plan]
        extra = [*after] if self.token is None else [*after, self.token]
        n_in, n_out = len(scalars) + len(operands), len(outs)

        def body(*refs):
            ins, rest = refs[:n_in], refs[n_in + len(extra) :]
            results, token, scratches = rest[:n_out], rest[n_out], rest[n_out + 1 :]
            token[...] = jnp.zeros_like(token)
            kernel(*ins, *results, *scratches)

        *results, self.token = pl.pallas_call(
            body,
            name=name,
            out_shape=[*outs, TOKEN],
            in_specs=[SMEM] * len(scalars) + (specs or [VMEM] * len(operands)) + [VMEM] * len(extra),
            out_specs=[*(out_specs or [VMEM] * n_out), VMEM],
            scratch_shapes=scratch,
            compiler_params=pltpu.CompilerParams(vmem_limit_bytes=VMEM_LIMIT),
            cost_estimate=pl.CostEstimate(flops=COST, bytes_accessed=0, transcendentals=0),
            **more,
        )(*scalars, *operands, *extra)
        return results


def flip(v, shards, bit):
    return lax.ppermute(v, "tensor", [(a, a ^ bit) for a in range(shards)])


def gather_near(v):
    across, beside = flip(v, 4, 2), flip(v, 4, 1)
    return [v, beside, across, flip(across, 4, 1)]


def gather_line(v):
    across = flip(v, 4, 2)
    below = lax.ppermute(v, "tensor", [(a, a + 1) for a in range(3)])
    above = lax.ppermute(v, "tensor", [(a + 1, a) for a in range(3)])
    far = lax.ppermute(across, "tensor", [(2, 3), (1, 0)])
    return [v, below, above, across, far]


def scatter_first(parts):
    if len(parts) == 4:
        return [flip(parts[3], 4, 1)]
    return [lax.ppermute(parts[3], "tensor", [(0, 1), (3, 2)]), lax.ppermute(parts[4], "tensor", [(1, 2), (2, 1)])]


def scatter_second(line, parts, came):
    piece = SHAPE(parts[0].shape, parts[0].dtype)
    own, beside, across = parts[:3]
    across, beside = line(join_kernel, "join", [piece] * 2, [], [across, came[0], beside])
    return [own, flip(across, 4, 2), flip(beside, 4, 1), *came[1:]]


def core_swap(v, replicas):
    return lax.ppermute(v, "dp", [(a, a ^ 1) for a in range(replicas)])


def axis_swap(v, replicas, step):
    levels = replicas.bit_length() - 2
    pairs = [(a, a ^ (1 << (1 + step if a & 1 else levels - step))) for a in range(replicas)]
    return lax.ppermute(v, "dp", pairs)


def local(replicas, shards, inputs, out_grad, weights, block_index, block_counts, first_moment, second_moment):
    capacity, size = weights.shape[1], weights.shape[2]
    rows, width = inputs.shape
    me = jnp.stack([lax.axis_index("tensor"), lax.axis_index("dp")]).astype(jnp.int32)
    plan = jnp.concatenate([me, block_counts[0], block_index.reshape(-1)])
    features = shards * width // size
    places, share = replicas // 2, capacity // replicas
    levels = places.bit_length() - 1
    held = pltpu.VMEM((shards, rows, width), BF16)
    acc = pltpu.VMEM((HB_DEV + 1, rows, size), F32)
    total = pltpu.VMEM((features + 1, rows, size), F32)
    wide = SHAPE((HB_DEV, rows, size), F32)
    narrow = SHAPE((HB_DEV, rows, size), BF16)
    turned = SHAPE((HB_DEV, size, rows), BF16)
    piece = SHAPE((rows, width), BF16)
    line = Line()
    lined = shards == 4

    def gather(v, form):
        return form(v) if lined else [lax.all_gather(v, "tensor", axis=0)]

    def parts_of(count):
        return [piece] * count if lined else [SHAPE((shards, rows, width), BF16)]

    def grads(matrix, right, left, after=()):
        half = SHAPE((places, share, size, size), BF16)
        name = ("gate_grads", "up_grads", "down_grads")[matrix]
        kernel = functools.partial(grads_kernel, matrix, len(right))
        keep, send = line(kernel, name, [half, half], [held], [*right, left], plan, after)
        return keep, core_swap(send, replicas)

    def fold(keep, got, step):
        half = SHAPE((keep.shape[0] // 2, *keep.shape[1:]), BF16)
        keep, send = line(fold_kernel, "fold", [half, half], [], [keep, got])
        return keep, axis_swap(send, replicas, step)

    def update(matrix, keep, got, buffer):
        block = pl.BlockSpec((1, share, size, size), lambda i: (matrix, 0, 0, 0))
        extra = [] if buffer is None else [buffer]
        return line(
            functools.partial(update_kernel, matrix),
            "update",
            [SHAPE(first_moment.shape, F32)],
            [],
            [keep, got, first_moment, second_moment, *extra],
            plan,
            specs=[VMEM, VMEM, block, block] + [ANY] * len(extra),
            out_specs=[block],
            input_output_aliases={5: 0} if extra else {},
            grid=(1,),
        )[0]

    def finish(held_parts):
        return line(sum_kernel, "finish", [piece], [], held_parts)[0]

    x = gather(inputs, gather_near)
    if lined:
        (out_grad,) = line(hold_kernel, "hold", [piece], [], [out_grad, x[2]])
    og = gather(out_grad, gather_line)
    out_parts, in_parts = parts_of(5), parts_of(4)
    hidden, hidden_turned, act, slope, *out_parts = line(
        functools.partial(forward_kernel, len(x), len(out_parts)),
        "forward",
        [narrow, turned, wide, wide, *out_parts],
        [held, acc, acc, total],
        [*x, weights],
        plan,
    )
    if lined:
        out_far = scatter_first(out_parts)
    else:
        outputs = lax.psum_scatter(out_parts[0], "tensor", scatter_dimension=0)
    (x_turned,) = line(
        functools.partial(turn_kernel, len(x)), "turn", [SHAPE((features, size, rows), BF16)], [held], x, plan
    )
    if lined:
        out_sums = scatter_second(line, out_parts, out_far)
    down = grads(2, og, hidden_turned, out_far[1:] if lined else ())
    gate_rows, up_rows = line(
        functools.partial(rows_kernel, len(og)),
        "row_grads",
        [narrow, narrow],
        [held, acc],
        [*og, weights, act, slope],
        plan,
    )
    down = fold(*down, 0)
    in_parts = line(
        functools.partial(input_kernel, len(in_parts)),
        "input_grads",
        in_parts,
        [total],
        [gate_rows, up_rows, weights],
        plan,
    )
    if lined:
        in_came = scatter_first(in_parts)
    else:
        input_grad = lax.psum_scatter(in_parts[0], "tensor", scatter_dimension=0)
    gate = grads(0, [gate_rows], x_turned)
    for step in range(1, levels):
        down = fold(*down, step)
    if lined:
        outputs = finish(out_sums)
    gate = fold(*gate, 0)
    up = grads(1, [up_rows], x_turned)
    for step in range(1, levels):
        gate = fold(*gate, step)
    if lined:
        in_sums = scatter_second(line, in_parts, in_came)
    up = fold(*up, 0)
    buffer = update(2, *down, None)
    buffer = update(0, *gate, buffer)
    for step in range(1, levels):
        up = fold(*up, step)
    if lined:
        input_grad = finish(in_sums)
    buffer = update(1, *up, buffer)
    return (outputs, input_grad, buffer)


def solution(mesh):
    in_specs = (
        P("dp", "tensor"),
        P("dp", "tensor"),
        P(None, "tensor", None, None),
        P(None, "tensor", None),
        P("tensor", None),
        P(None, ("tensor", "dp"), None, None),
        P(None, ("tensor", "dp"), None, None),
    )
    out_specs = (P("dp", "tensor"), P("dp", "tensor"), P(None, ("tensor", "dp"), None, None))
    body = functools.partial(local, mesh.shape["dp"], mesh.shape["tensor"])
    return jax.shard_map(body, mesh=mesh, in_specs=in_specs, out_specs=out_specs, check_vma=False)
```

```python
import functools
import jax
import jax.numpy as jnp
from jax import lax
from jax.experimental import pallas as pl
from jax.experimental.pallas import tpu as pltpu
from jax.sharding import PartitionSpec as P

HB_DEV = 14
EPSILON = 1e-08
GROUP = 16
COST = 2 * 10**10
VMEM_LIMIT = 32 * 1024 * 1024
F32, BF16 = jnp.float32, jnp.bfloat16
SHAPE = jax.ShapeDtypeStruct
SMEM = pl.BlockSpec(memory_space=pltpu.SMEM)
VMEM = pl.BlockSpec(memory_space=pltpu.VMEM)
ANY = pl.BlockSpec(memory_space=pl.ANY)
TOKEN = SHAPE((8, 128), F32)
HEAD = 5


def group_of(capacity):
    return next(g for g in (GROUP, 8, 4, 2, 1) if capacity % g == 0)


def feature_block(ref, block, size):
    per_shard = ref.shape[2] // size
    start = pl.multiple_of(lax.rem(block, per_shard) * size, size)
    return ref.at[lax.div(block, per_shard), :, pl.ds(start, size)]


def slot_pair(plan_ref, matrix, slot, capacity):
    at = HEAD + (matrix * capacity + slot) * 2
    return plan_ref[at], plan_ref[at + 1]


def each_group(first, last, group, body):
    def step(i, carry):
        body([first + i * group + u for u in range(group)])
        return carry

    lax.fori_loop(0, lax.div(last - first + (group - 1), group), step, 0)


def dot(a, b, contract):
    return lax.dot_general(a, b, (contract, ((), ())), preferred_element_type=F32)


def accumulate(plan_ref, matrix, capacity, acc, into, product, order=None, base=0):
    trash = acc.shape[0] - 1
    order_ref, first, last = order or (None, 0, plan_ref[2 + matrix])

    def body(places):
        products, targets = [], []
        for p in places:
            s = p if order is None else jnp.where(p < last, order_ref[p], 0)
            pair = slot_pair(plan_ref, matrix, s, capacity)
            targets.append(jnp.where(p < last, pair[into] - base, trash))
            products.append(product(s, *pair))
        for t, p in zip(targets, products):
            acc[t] += p

    each_group(first, last, group_of(capacity), body)


def order_kernel(per_shard, capacity, plan_ref, order_ref):
    far = lax.bitwise_xor(plan_ref[0], 3)
    for matrix in (0, 1):

        def is_far(s, matrix=matrix):
            return lax.div(slot_pair(plan_ref, matrix, s, capacity)[0], per_shard) == far

        def count(s, total):
            return total + is_far(s).astype(jnp.int32)

        def put(s, at):
            here, there = at
            found = is_far(s)
            order_ref[matrix * capacity + jnp.where(found, here, there)] = s
            step = found.astype(jnp.int32)
            return here + step, there + 1 - step

        live = plan_ref[2 + matrix]
        total = lax.fori_loop(0, live, count, 0)
        order_ref[2 * capacity + matrix] = total
        lax.fori_loop(0, live, put, (0, total))


def load_shards(pieces, held, me):
    if len(pieces) == 1:
        return pieces[0]
    if len(pieces) == 4:
        for offset, piece in enumerate(pieces):
            held[lax.bitwise_xor(me, offset)] = piece[...]
        return held
    own, below, above, across, far = pieces
    last = held.shape[0] - 1
    held[me] = own[...]
    held[lax.bitwise_xor(me, 2)] = across[...]

    @pl.when(me > 0)
    def _():
        held[me - 1] = below[...]

    @pl.when(me < last)
    def _():
        held[me + 1] = above[...]

    @pl.when((me == 0) | (me == last))
    def _():
        held[last - me] = far[...]

    return held


def store_shards(total, outs, me, per_shard, size):
    if len(outs) == 1:
        places = [(outs[0].at[t], t) for t in range(outs[0].shape[0])]
    elif len(outs) == 4:
        places = [(out, lax.bitwise_xor(me, offset)) for offset, out in enumerate(outs)]
    else:
        last = 3
        own, beside, across, far, middle = outs
        places = [(out, lax.bitwise_xor(me, offset)) for offset, out in enumerate((own, beside, across, far))]
        places.append((middle, last - me))
    for out, t in places:
        for c in range(per_shard):
            out[:, c * size : (c + 1) * size] = total[t * per_shard + c].astype(out.dtype)


def forward_kernel(n_pieces, n_outs, plan_ref, *refs):
    pieces, refs = refs[:n_pieces], refs[n_pieces:]
    w_ref, hidden_ref, turned_ref, act_ref, slope_ref = refs[:5]
    outs, (held, gate, up, total) = refs[5 : 5 + n_outs], refs[5 + n_outs :]
    me = plan_ref[0]
    x_ref = load_shards(pieces, held, me)
    capacity, size = w_ref.shape[1], w_ref.shape[2]
    gate[...] = jnp.zeros_like(gate)
    up[...] = jnp.zeros_like(up)
    total[...] = jnp.zeros_like(total)
    for matrix, acc in ((0, gate), (1, up)):
        accumulate(
            plan_ref, matrix, capacity, acc, 1,
            lambda s, f, h, matrix=matrix: dot(feature_block(x_ref, f, size)[...], w_ref[matrix, s], ((1,), (0,))),
        )
    for h in range(hidden_ref.shape[0]):
        g, u = gate[h], up[h]
        sig = 1.0 / (1.0 + jnp.exp(-g))
        act = g * sig
        act_ref[h] = act
        slope_ref[h] = u * sig * (1.0 + g * (1.0 - sig))
        hidden = (act * u).astype(hidden_ref.dtype)
        hidden_ref[h] = hidden
        turned_ref[h] = hidden.T
    accumulate(
        plan_ref, 2, capacity, total, 0,
        lambda s, f, h: dot(hidden_ref[h], w_ref[2, s], ((1,), (0,))),
    )
    store_shards(total, outs, me, x_ref.shape[2] // size, size)


def turn_kernel(n_pieces, plan_ref, *refs):
    pieces, (turned_ref, held) = refs[:n_pieces], refs[n_pieces:]
    x_ref = load_shards(pieces, held, plan_ref[0])
    size = turned_ref.shape[1]
    per_shard = x_ref.shape[2] // size
    for f in range(turned_ref.shape[0]):
        c = f % per_shard
        turned_ref[f] = x_ref[f // per_shard, :, c * size : (c + 1) * size].T


def rows_kernel(n_pieces, plan_ref, *refs):
    pieces, refs = refs[:n_pieces], refs[n_pieces:]
    w_ref, act_ref, slope_ref, gate_rows_ref, up_rows_ref, held, acc = refs
    og_ref = load_shards(pieces, held, plan_ref[0])
    capacity, size = w_ref.shape[1], w_ref.shape[2]
    acc[...] = jnp.zeros_like(acc)
    accumulate(
        plan_ref, 2, capacity, acc, 1,
        lambda s, f, h: dot(feature_block(og_ref, f, size)[...], w_ref[2, s], ((1,), (1,))),
    )
    for h in range(act_ref.shape[0]):
        gate_rows_ref[h] = (acc[h] * slope_ref[h]).astype(gate_rows_ref.dtype)
        up_rows_ref[h] = (acc[h] * act_ref[h]).astype(up_rows_ref.dtype)


def spread(place, core, places):
    levels = places.bit_length() - 1
    turned = sum(lax.shift_left(lax.bitwise_and(lax.shift_right_logical(place, b), 1), levels - 1 - b) for b in range(levels))
    return 2 * jnp.where(core == 0, place, turned)


def grads_kernel(matrix, n_pieces, plan_ref, *refs):
    pieces, refs = refs[:n_pieces], refs[n_pieces:]
    turned_ref, keep_ref, send_ref, held = refs
    size, share = keep_ref.shape[2], keep_ref.shape[1]
    places = keep_ref.shape[0]
    replica = plan_ref[1]
    right_ref = load_shards(pieces, held, plan_ref[0])
    capacity = 2 * places * share
    count = plan_ref[2 + matrix]
    for out, bit in ((send_ref, 1), (keep_ref, 0)):

        def one_place(q, carry, out=out, bit=bit):
            owner = lax.bitwise_xor(replica, bit)
            first = lax.bitwise_xor(owner, spread(q, lax.bitwise_and(owner, 1), places)) * share

            @pl.when(first < count)
            def _():
                for s in range(share):
                    f, h = slot_pair(plan_ref, matrix, first + s, capacity)
                    if matrix == 2:
                        left, right = turned_ref[h], feature_block(right_ref, f, size)[...]
                    else:
                        left, right = turned_ref[f], right_ref[h]
                    out[q, s] = dot(left, right, ((1,), (0,))).astype(out.dtype)

            return carry

        lax.fori_loop(0, places, one_place, 0)


def input_kernel(n_outs, plan_ref, gate_rows_ref, up_rows_ref, w_ref, *refs):
    outs, (total,) = refs[:n_outs], refs[n_outs:]
    capacity, size = w_ref.shape[1], w_ref.shape[2]
    total[...] = jnp.zeros_like(total)
    for matrix, rows in ((0, gate_rows_ref), (1, up_rows_ref)):
        accumulate(
            plan_ref, matrix, capacity, total, 0,
            lambda s, f, h, matrix=matrix, rows=rows: dot(rows[h], w_ref[matrix, s], ((1,), (1,))),
        )
    store_shards(total, outs, plan_ref[0], outs[0].shape[-1] // size, size)


def input_part_kernel(is_far, plan_ref, order_ref, gate_rows_ref, up_rows_ref, w_ref, *refs):
    *outs, total = refs
    capacity, size = w_ref.shape[1], w_ref.shape[2]
    per_shard = outs[0].shape[-1] // size
    me = plan_ref[0]
    base = lax.bitwise_xor(me, 3) * per_shard if is_far else 0
    total[...] = jnp.zeros_like(total)
    for matrix, rows in ((0, gate_rows_ref), (1, up_rows_ref)):
        at = matrix * capacity
        cut = at + order_ref[2 * capacity + matrix]
        accumulate(
            plan_ref, matrix, capacity, total, 0,
            lambda s, f, h, matrix=matrix, rows=rows: dot(rows[h], w_ref[matrix, s], ((1,), (1,))),
            (order_ref, at, cut) if is_far else (order_ref, cut, at + plan_ref[2 + matrix]),
            base,
        )
    for offset, out in enumerate(outs):
        first = 0 if is_far else lax.bitwise_xor(me, offset) * per_shard
        for c in range(per_shard):
            out[:, c * size : (c + 1) * size] = total[first + c].astype(out.dtype)


def fold_kernel(keep_ref, got_ref, keep_out, send_out):
    half = keep_out.shape[0]
    keep_out[...] = keep_ref[:half] + got_ref[:half]
    send_out[...] = keep_ref[half:] + got_ref[half:]


def join_kernel(*refs):
    ins, outs = refs[: len(refs) // 2 + 1], refs[len(refs) // 2 + 1 :]
    outs[0][...] = ins[0][...] + ins[1][...]
    for source, out in zip(ins[2:], outs[1:]):
        out[...] = source[...]


def sum_kernel(*refs):
    *parts, out_ref = refs
    total = parts[0][...].astype(F32)
    for part in parts[1:]:
        total += part[...].astype(F32)
    out_ref[...] = total.astype(out_ref.dtype)


def update_kernel(matrix, plan_ref, keep_ref, got_ref, m1_ref, m2_ref, *refs):
    out_ref = refs[-1]
    share = keep_ref.shape[1]
    first = plan_ref[1] * share
    for s in range(share):
        g = keep_ref[0, s].astype(F32) + got_ref[0, s].astype(F32)
        first_new = 0.9 * m1_ref[0, s] + 0.1 * g
        second_new = 0.95 * m2_ref[0, s] + 0.05 * g * g
        live = first + s < plan_ref[2 + matrix]
        out_ref[0, s] = jnp.where(live, first_new / (jnp.sqrt(second_new) + EPSILON), 0.0)


def hold_kernel(v_ref, _, out_ref):
    out_ref[...] = v_ref[...]


class Line:
    token = None

    def __call__(self, kernel, name, outs, scratch, operands, plan=(), after=(), specs=None, out_specs=None, cost=COST, **more):
        scalars = [*plan]
        extra = [*after] if self.token is None else [*after, self.token]
        n_in, n_out = len(scalars) + len(operands), len(outs)

        def body(*refs):
            ins, rest = refs[:n_in], refs[n_in + len(extra) :]
            results, token, scratches = rest[:n_out], rest[n_out], rest[n_out + 1 :]
            token[...] = jnp.zeros_like(token)
            kernel(*ins, *results, *scratches)

        *results, self.token = pl.pallas_call(
            body,
            name=name,
            out_shape=[*outs, TOKEN],
            in_specs=[SMEM] * len(scalars) + (specs or [VMEM] * len(operands)) + [VMEM] * len(extra),
            out_specs=[*(out_specs or [VMEM] * n_out), VMEM],
            scratch_shapes=scratch,
            compiler_params=pltpu.CompilerParams(vmem_limit_bytes=VMEM_LIMIT),
            cost_estimate=pl.CostEstimate(flops=cost, bytes_accessed=0, transcendentals=0),
            **more,
        )(*scalars, *operands, *extra)
        return results


def flip(v, shards, bit):
    return lax.ppermute(v, "tensor", [(a, a ^ bit) for a in range(shards)])


def gather_near(v):
    across, beside = flip(v, 4, 2), flip(v, 4, 1)
    return [v, beside, across, flip(across, 4, 1)]


def gather_line(v):
    across = flip(v, 4, 2)
    below = lax.ppermute(v, "tensor", [(a, a + 1) for a in range(3)])
    above = lax.ppermute(v, "tensor", [(a + 1, a) for a in range(3)])
    far = lax.ppermute(across, "tensor", [(2, 3), (1, 0)])
    return [v, below, above, across, far]


def scatter_first(parts):
    return [lax.ppermute(parts[3], "tensor", [(0, 1), (3, 2)]), lax.ppermute(parts[4], "tensor", [(1, 2), (2, 1)])]


def scatter_second(line, parts, came):
    piece = SHAPE(parts[0].shape, parts[0].dtype)
    own, beside, across = parts[:3]
    across, beside = line(join_kernel, "join", [piece] * 2, [], [across, came[0], beside])
    return [own, flip(across, 4, 2), flip(beside, 4, 1), *came[1:]]


def core_swap(v, replicas):
    return lax.ppermute(v, "dp", [(a, a ^ 1) for a in range(replicas)])


def axis_swap(v, replicas, step):
    levels = replicas.bit_length() - 2
    pairs = [(a, a ^ (1 << (1 + step if a & 1 else levels - step))) for a in range(replicas)]
    return lax.ppermute(v, "dp", pairs)


def local(replicas, shards, inputs, out_grad, weights, block_index, block_counts, first_moment, second_moment):
    capacity, size = weights.shape[1], weights.shape[2]
    rows, width = inputs.shape
    me = jnp.stack([lax.axis_index("tensor"), lax.axis_index("dp")]).astype(jnp.int32)
    plan = (jnp.concatenate([me, block_counts[0], block_index.reshape(-1)]),)
    features = shards * width // size
    places, share = replicas // 2, capacity // replicas
    levels = places.bit_length() - 1
    held = pltpu.VMEM((shards, rows, width), BF16)
    acc = pltpu.VMEM((HB_DEV + 1, rows, size), F32)
    total = pltpu.VMEM((features + 1, rows, size), F32)
    wide = SHAPE((HB_DEV, rows, size), F32)
    narrow = SHAPE((HB_DEV, rows, size), BF16)
    turned = SHAPE((HB_DEV, size, rows), BF16)
    piece = SHAPE((rows, width), BF16)
    line = Line()
    lined = shards == 4

    def gather(v, form):
        return form(v) if lined else [lax.all_gather(v, "tensor", axis=0)]

    def parts_of(count):
        return [piece] * count if lined else [SHAPE((shards, rows, width), BF16)]

    def grads(matrix, right, left, after=()):
        half = SHAPE((places, share, size, size), BF16)
        name = ("gate_grads", "up_grads", "down_grads")[matrix]
        kernel = functools.partial(grads_kernel, matrix, len(right))
        keep, send = line(kernel, name, [half, half], [held], [*right, left], plan, after)
        return keep, core_swap(send, replicas)

    def fold(keep, got, step):
        half = SHAPE((keep.shape[0] // 2, *keep.shape[1:]), BF16)
        keep, send = line(fold_kernel, "fold", [half, half], [], [keep, got])
        return keep, axis_swap(send, replicas, step)

    def update(matrix, keep, got, buffer):
        block = pl.BlockSpec((1, share, size, size), lambda i: (matrix, 0, 0, 0))
        extra = [] if buffer is None else [buffer]
        return line(
            functools.partial(update_kernel, matrix),
            "update",
            [SHAPE(first_moment.shape, F32)],
            [],
            [keep, got, first_moment, second_moment, *extra],
            plan,
            specs=[VMEM, VMEM, block, block] + [ANY] * len(extra),
            out_specs=[block],
            input_output_aliases={5: 0} if extra else {},
            grid=(1,),
        )[0]

    def finish(held_parts):
        return line(sum_kernel, "finish", [piece], [], held_parts)[0]

    x = gather(inputs, gather_near)
    if lined:
        (order,) = line(
            functools.partial(order_kernel, width // size, capacity), "order",
            [SHAPE((2 * capacity + 2,), jnp.int32)], [], [], plan, out_specs=[SMEM],
        )
    if lined:
        (out_grad,) = line(hold_kernel, "hold", [piece], [], [out_grad, x[2]])
    og = gather(out_grad, gather_line)
    out_parts, in_parts = parts_of(5), parts_of(4)
    hidden, hidden_turned, act, slope, *out_parts = line(
        functools.partial(forward_kernel, len(x), len(out_parts)),
        "forward",
        [narrow, turned, wide, wide, *out_parts],
        [held, acc, acc, total],
        [*x, weights],
        plan,
    )
    if lined:
        out_far = scatter_first(out_parts)
    else:
        outputs = lax.psum_scatter(out_parts[0], "tensor", scatter_dimension=0)
    (x_turned,) = line(
        functools.partial(turn_kernel, len(x)), "turn", [SHAPE((features, size, rows), BF16)], [held], x, plan
    )
    if lined:
        out_sums = scatter_second(line, out_parts, out_far)
    down = grads(2, og, hidden_turned)
    gate_rows, up_rows = line(
        functools.partial(rows_kernel, len(og)),
        "row_grads",
        [narrow, narrow],
        [held, acc],
        [*og, weights, act, slope],
        plan,
    )
    down = fold(*down, 0)
    if lined:
        part_total = pltpu.VMEM((width // size + 1, rows, size), F32)
        in_operands = [gate_rows, up_rows, weights]
        (in_far,) = line(
            functools.partial(input_part_kernel, True), "input_far", [piece], [part_total], in_operands, (*plan, order)
        )
        in_far = flip(in_far, 4, 1)
    if lined:
        in_parts = line(
            functools.partial(input_part_kernel, False), "input_rest", [piece] * 3, [total], in_operands, (*plan, order)
        )
    else:
        in_parts = line(
            functools.partial(input_kernel, 1), "input_grads", in_parts, [total], [gate_rows, up_rows, weights], plan
        )
        input_grad = lax.psum_scatter(in_parts[0], "tensor", scatter_dimension=0)
    gate = grads(0, [gate_rows], x_turned)
    for step in range(1, levels):
        down = fold(*down, step)
    if lined:
        outputs = finish(out_sums)
    gate = fold(*gate, 0)
    buffer = update(2, *down, None)
    up = grads(1, [up_rows], x_turned)
    if lined:
        in_sums = scatter_second(line, in_parts, [in_far])
    up = fold(*up, 0)
    for step in range(1, levels):
        gate = fold(*gate, step)
    for step in range(1, levels):
        up = fold(*up, step)
    buffer = update(0, *gate, buffer)
    if lined:
        input_grad = finish(in_sums)
    buffer = update(1, *up, buffer)
    return (outputs, input_grad, buffer)


def solution(mesh):
    in_specs = (
        P("dp", "tensor"),
        P("dp", "tensor"),
        P(None, "tensor", None, None),
        P(None, "tensor", None),
        P("tensor", None),
        P(None, ("tensor", "dp"), None, None),
        P(None, ("tensor", "dp"), None, None),
    )
    out_specs = (P("dp", "tensor"), P("dp", "tensor"), P(None, ("tensor", "dp"), None, None))
    body = functools.partial(local, mesh.shape["dp"], mesh.shape["tensor"])
    return jax.shard_map(body, mesh=mesh, in_specs=in_specs, out_specs=out_specs, check_vma=False)
```

```python
import functools
import jax
import jax.numpy as jnp
from jax import lax
from jax.experimental import pallas as pl
from jax.experimental.pallas import tpu as pltpu
from jax.sharding import PartitionSpec as P

HB_DEV = 14
EPSILON = 1e-08
GROUPS = (32, 8)
COST = 2 * 10**10
VMEM_LIMIT = 32 * 1024 * 1024
F32, BF16 = jnp.float32, jnp.bfloat16
SHAPE = jax.ShapeDtypeStruct
SMEM = pl.BlockSpec(memory_space=pltpu.SMEM)
VMEM = pl.BlockSpec(memory_space=pltpu.VMEM)
ANY = pl.BlockSpec(memory_space=pl.ANY)
TOKEN = SHAPE((8, 128), F32)
HEAD = 5


def feature_block(ref, block, size):
    per_shard = ref.shape[2] // size
    start = pl.multiple_of(lax.rem(block, per_shard) * size, size)
    return ref.at[lax.div(block, per_shard), :, pl.ds(start, size)]


def slot_pair(plan_ref, matrix, slot, capacity):
    at = HEAD + (matrix * capacity + slot) * 2
    return plan_ref[at], plan_ref[at + 1]


def each_group(first, last, body):
    large, small = GROUPS

    def run(at, size, count, whole):
        def step(i, carry):
            body([at + i * size + u for u in range(size)], whole)
            return carry

        lax.fori_loop(0, count, step, 0)

    full = lax.div(last - first, large)
    rest = first + full * large
    run(first, large, full, True)
    run(rest, small, lax.div(last - rest + (small - 1), small), False)


def dot(a, b, contract):
    return lax.dot_general(a, b, (contract, ((), ())), preferred_element_type=F32)


def accumulate(plan_ref, matrix, capacity, acc, into, product, order=None, base=0):
    trash = acc.shape[0] - 1
    order_ref, first, last = order or (None, 0, plan_ref[2 + matrix])

    def body(places, whole):
        products, targets = [], []
        for p in places:
            here = p if whole else jnp.minimum(p, last - 1)
            s = here if order is None else order_ref[here]
            pair = slot_pair(plan_ref, matrix, s, capacity)
            target = pair[into] - base
            targets.append(target if whole else jnp.where(p < last, target, trash))
            products.append(product(s, *pair))
        for t, p in zip(targets, products):
            acc[t] += p

    each_group(first, last, body)


def order_kernel(per_shard, capacity, plan_ref, order_ref):
    far = lax.bitwise_xor(plan_ref[0], 3)
    for matrix in (0, 1):

        def is_far(s, matrix=matrix):
            return lax.div(slot_pair(plan_ref, matrix, s, capacity)[0], per_shard) == far

        def count(s, total):
            return total + is_far(s).astype(jnp.int32)

        def put(s, at):
            here, there = at
            found = is_far(s)
            order_ref[matrix * capacity + jnp.where(found, here, there)] = s
            step = found.astype(jnp.int32)
            return here + step, there + 1 - step

        live = plan_ref[2 + matrix]
        total = lax.fori_loop(0, live, count, 0)
        order_ref[2 * capacity + matrix] = total
        lax.fori_loop(0, live, put, (0, total))


def load_shards(pieces, held, me):
    if len(pieces) == 1:
        return pieces[0]
    if len(pieces) == 4:
        for offset, piece in enumerate(pieces):
            held[lax.bitwise_xor(me, offset)] = piece[...]
        return held
    own, below, above, across, far = pieces
    last = held.shape[0] - 1
    held[me] = own[...]
    held[lax.bitwise_xor(me, 2)] = across[...]

    @pl.when(me > 0)
    def _():
        held[me - 1] = below[...]

    @pl.when(me < last)
    def _():
        held[me + 1] = above[...]

    @pl.when((me == 0) | (me == last))
    def _():
        held[last - me] = far[...]

    return held


def store_shards(total, outs, me, per_shard, size):
    if len(outs) == 1:
        places = [(outs[0].at[t], t) for t in range(outs[0].shape[0])]
    elif len(outs) == 4:
        places = [(out, lax.bitwise_xor(me, offset)) for offset, out in enumerate(outs)]
    else:
        last = 3
        own, beside, across, far, middle = outs
        places = [(out, lax.bitwise_xor(me, offset)) for offset, out in enumerate((own, beside, across, far))]
        places.append((middle, last - me))
    for out, t in places:
        for c in range(per_shard):
            out[:, c * size : (c + 1) * size] = total[t * per_shard + c].astype(out.dtype)


def forward_kernel(n_pieces, n_outs, plan_ref, *refs):
    pieces, refs = refs[:n_pieces], refs[n_pieces:]
    w_ref, hidden_ref, turned_ref, act_ref, slope_ref = refs[:5]
    outs, (held, gate, up, total) = refs[5 : 5 + n_outs], refs[5 + n_outs :]
    me = plan_ref[0]
    x_ref = load_shards(pieces, held, me)
    capacity, size = w_ref.shape[1], w_ref.shape[2]
    gate[...] = jnp.zeros_like(gate)
    up[...] = jnp.zeros_like(up)
    total[...] = jnp.zeros_like(total)
    for matrix, acc in ((0, gate), (1, up)):
        accumulate(
            plan_ref, matrix, capacity, acc, 1,
            lambda s, f, h, matrix=matrix: dot(feature_block(x_ref, f, size)[...], w_ref[matrix, s], ((1,), (0,))),
        )
    for h in range(hidden_ref.shape[0]):
        g, u = gate[h], up[h]
        sig = 1.0 / (1.0 + jnp.exp(-g))
        act = g * sig
        act_ref[h] = act
        slope_ref[h] = u * sig * (1.0 + g * (1.0 - sig))
        hidden = (act * u).astype(hidden_ref.dtype)
        hidden_ref[h] = hidden
        turned_ref[h] = hidden.T
    accumulate(
        plan_ref, 2, capacity, total, 0,
        lambda s, f, h: dot(hidden_ref[h], w_ref[2, s], ((1,), (0,))),
    )
    store_shards(total, outs, me, x_ref.shape[2] // size, size)


def turn_kernel(n_pieces, plan_ref, *refs):
    pieces, (turned_ref, held) = refs[:n_pieces], refs[n_pieces:]
    x_ref = load_shards(pieces, held, plan_ref[0])
    size = turned_ref.shape[1]
    per_shard = x_ref.shape[2] // size
    for f in range(turned_ref.shape[0]):
        c = f % per_shard
        turned_ref[f] = x_ref[f // per_shard, :, c * size : (c + 1) * size].T


def rows_kernel(n_pieces, plan_ref, *refs):
    pieces, refs = refs[:n_pieces], refs[n_pieces:]
    w_ref, act_ref, slope_ref, gate_rows_ref, up_rows_ref, held, acc = refs
    og_ref = load_shards(pieces, held, plan_ref[0])
    capacity, size = w_ref.shape[1], w_ref.shape[2]
    acc[...] = jnp.zeros_like(acc)
    accumulate(
        plan_ref, 2, capacity, acc, 1,
        lambda s, f, h: dot(feature_block(og_ref, f, size)[...], w_ref[2, s], ((1,), (1,))),
    )
    for h in range(act_ref.shape[0]):
        gate_rows_ref[h] = (acc[h] * slope_ref[h]).astype(gate_rows_ref.dtype)
        up_rows_ref[h] = (acc[h] * act_ref[h]).astype(up_rows_ref.dtype)


def spread(place, core, places):
    levels = places.bit_length() - 1
    turned = sum(lax.shift_left(lax.bitwise_and(lax.shift_right_logical(place, b), 1), levels - 1 - b) for b in range(levels))
    return 2 * jnp.where(core == 0, place, turned)


def grads_kernel(matrix, n_pieces, plan_ref, *refs):
    pieces, refs = refs[:n_pieces], refs[n_pieces:]
    turned_ref, keep_ref, send_ref, held = refs
    size, share = keep_ref.shape[2], keep_ref.shape[1]
    places = keep_ref.shape[0]
    replica = plan_ref[1]
    right_ref = load_shards(pieces, held, plan_ref[0])
    capacity = 2 * places * share
    count = plan_ref[2 + matrix]

    def one_place(q, carry):
        todo = []
        for out, bit in ((send_ref, 1), (keep_ref, 0)):
            owner = lax.bitwise_xor(replica, bit)
            todo.append((out, lax.bitwise_xor(owner, spread(q, lax.bitwise_and(owner, 1), places)) * share))

        @pl.when(jnp.minimum(todo[0][1], todo[1][1]) < count)
        def _():
            for out, first in todo:
                for s in range(share):
                    f, h = slot_pair(plan_ref, matrix, first + s, capacity)
                    if matrix == 2:
                        left, right = turned_ref[h], feature_block(right_ref, f, size)[...]
                    else:
                        left, right = turned_ref[f], right_ref[h]
                    out[q, s] = dot(left, right, ((1,), (0,))).astype(out.dtype)

        return carry

    lax.fori_loop(0, places, one_place, 0)


def input_kernel(n_outs, plan_ref, gate_rows_ref, up_rows_ref, w_ref, *refs):
    outs, (total,) = refs[:n_outs], refs[n_outs:]
    capacity, size = w_ref.shape[1], w_ref.shape[2]
    total[...] = jnp.zeros_like(total)
    for matrix, rows in ((0, gate_rows_ref), (1, up_rows_ref)):
        accumulate(
            plan_ref, matrix, capacity, total, 0,
            lambda s, f, h, matrix=matrix, rows=rows: dot(rows[h], w_ref[matrix, s], ((1,), (1,))),
        )
    store_shards(total, outs, plan_ref[0], outs[0].shape[-1] // size, size)


def input_part_kernel(is_far, plan_ref, order_ref, gate_rows_ref, up_rows_ref, w_ref, *refs):
    *outs, total = refs
    capacity, size = w_ref.shape[1], w_ref.shape[2]
    per_shard = outs[0].shape[-1] // size
    me = plan_ref[0]
    base = lax.bitwise_xor(me, 3) * per_shard if is_far else 0
    total[...] = jnp.zeros_like(total)
    for matrix, rows in ((0, gate_rows_ref), (1, up_rows_ref)):
        at = matrix * capacity
        cut = at + order_ref[2 * capacity + matrix]
        accumulate(
            plan_ref, matrix, capacity, total, 0,
            lambda s, f, h, matrix=matrix, rows=rows: dot(rows[h], w_ref[matrix, s], ((1,), (1,))),
            (order_ref, at, cut) if is_far else (order_ref, cut, at + plan_ref[2 + matrix]),
            base,
        )
    for offset, out in enumerate(outs):
        first = 0 if is_far else lax.bitwise_xor(me, offset) * per_shard
        for c in range(per_shard):
            out[:, c * size : (c + 1) * size] = total[first + c].astype(out.dtype)


def fold_kernel(keep_ref, got_ref, keep_out, send_out):
    half = keep_out.shape[0]
    keep_out[...] = keep_ref[:half] + got_ref[:half]
    send_out[...] = keep_ref[half:] + got_ref[half:]


def join_kernel(*refs):
    ins, outs = refs[: len(refs) // 2 + 1], refs[len(refs) // 2 + 1 :]
    outs[0][...] = ins[0][...] + ins[1][...]
    for source, out in zip(ins[2:], outs[1:]):
        out[...] = source[...]


def sum_kernel(*refs):
    *parts, out_ref = refs
    total = parts[0][...].astype(F32)
    for part in parts[1:]:
        total += part[...].astype(F32)
    out_ref[...] = total.astype(out_ref.dtype)


def update_kernel(matrix, plan_ref, keep_ref, got_ref, m1_ref, m2_ref, *refs):
    out_ref = refs[-1]
    share, part = keep_ref.shape[1], out_ref.shape[1]
    skip = pl.program_id(0) * part
    first = plan_ref[1] * share + skip
    for s in range(part):
        g = keep_ref[0, skip + s].astype(F32) + got_ref[0, skip + s].astype(F32)
        first_new = 0.9 * m1_ref[0, s] + 0.1 * g
        second_new = 0.95 * m2_ref[0, s] + 0.05 * g * g
        live = first + s < plan_ref[2 + matrix]
        out_ref[0, s] = jnp.where(live, first_new / (jnp.sqrt(second_new) + EPSILON), 0.0)


def hold_kernel(v_ref, _, out_ref):
    out_ref[...] = v_ref[...]


class Line:
    token = None

    def __call__(self, kernel, name, outs, scratch, operands, plan=(), after=(), specs=None, out_specs=None, cost=COST, **more):
        scalars = [*plan]
        extra = [*after] if self.token is None else [*after, self.token]
        n_in, n_out = len(scalars) + len(operands), len(outs)

        def body(*refs):
            ins, rest = refs[:n_in], refs[n_in + len(extra) :]
            results, token, scratches = rest[:n_out], rest[n_out], rest[n_out + 1 :]
            token[...] = jnp.zeros_like(token)
            kernel(*ins, *results, *scratches)

        *results, self.token = pl.pallas_call(
            body,
            name=name,
            out_shape=[*outs, TOKEN],
            in_specs=[SMEM] * len(scalars) + (specs or [VMEM] * len(operands)) + [VMEM] * len(extra),
            out_specs=[*(out_specs or [VMEM] * n_out), VMEM],
            scratch_shapes=scratch,
            compiler_params=pltpu.CompilerParams(vmem_limit_bytes=VMEM_LIMIT),
            cost_estimate=pl.CostEstimate(flops=cost, bytes_accessed=0, transcendentals=0),
            **more,
        )(*scalars, *operands, *extra)
        return results


def flip(v, shards, bit):
    return lax.ppermute(v, "tensor", [(a, a ^ bit) for a in range(shards)])


def gather_near(v):
    across, beside = flip(v, 4, 2), flip(v, 4, 1)
    return [v, beside, across, flip(across, 4, 1)]


def gather_line(v):
    across = flip(v, 4, 2)
    below = lax.ppermute(v, "tensor", [(a, a + 1) for a in range(3)])
    above = lax.ppermute(v, "tensor", [(a + 1, a) for a in range(3)])
    far = lax.ppermute(across, "tensor", [(2, 3), (1, 0)])
    return [v, below, above, across, far]


def scatter_first(parts):
    return [lax.ppermute(parts[3], "tensor", [(0, 1), (3, 2)]), lax.ppermute(parts[4], "tensor", [(1, 2), (2, 1)])]


def scatter_second(line, parts, came):
    piece = SHAPE(parts[0].shape, parts[0].dtype)
    own, beside, across = parts[:3]
    across, beside = line(join_kernel, "join", [piece] * 2, [], [across, came[0], beside])
    return [own, flip(across, 4, 2), flip(beside, 4, 1), *came[1:]]


def core_swap(v, replicas):
    return lax.ppermute(v, "dp", [(a, a ^ 1) for a in range(replicas)])


def axis_swap(v, replicas, step):
    levels = replicas.bit_length() - 2
    pairs = [(a, a ^ (1 << (1 + step if a & 1 else levels - step))) for a in range(replicas)]
    return lax.ppermute(v, "dp", pairs)


def local(replicas, shards, inputs, out_grad, weights, block_index, block_counts, first_moment, second_moment):
    capacity, size = weights.shape[1], weights.shape[2]
    rows, width = inputs.shape
    me = jnp.stack([lax.axis_index("tensor"), lax.axis_index("dp")]).astype(jnp.int32)
    plan = (jnp.concatenate([me, block_counts[0], block_index.reshape(-1)]),)
    features = shards * width // size
    places, share = replicas // 2, capacity // replicas
    levels = places.bit_length() - 1
    held = pltpu.VMEM((shards, rows, width), BF16)
    acc = pltpu.VMEM((HB_DEV + 1, rows, size), F32)
    total = pltpu.VMEM((features + 1, rows, size), F32)
    wide = SHAPE((HB_DEV, rows, size), F32)
    narrow = SHAPE((HB_DEV, rows, size), BF16)
    turned = SHAPE((HB_DEV, size, rows), BF16)
    piece = SHAPE((rows, width), BF16)
    line = Line()
    lined = shards == 4

    def gather(v, form):
        return form(v) if lined else [lax.all_gather(v, "tensor", axis=0)]

    def parts_of(count):
        return [piece] * count if lined else [SHAPE((shards, rows, width), BF16)]

    def grads(matrix, right, left, after=()):
        half = SHAPE((places, share, size, size), BF16)
        name = ("gate_grads", "up_grads", "down_grads")[matrix]
        kernel = functools.partial(grads_kernel, matrix, len(right))
        keep, send = line(kernel, name, [half, half], [held], [*right, left], plan, after)
        return keep, core_swap(send, replicas)

    def fold(keep, got, step):
        half = SHAPE((keep.shape[0] // 2, *keep.shape[1:]), BF16)
        keep, send = line(fold_kernel, "fold", [half, half], [], [keep, got])
        return keep, axis_swap(send, replicas, step)

    def update(matrix, keep, got, buffer):
        steps = 3 if share % 3 == 0 else 1
        block = pl.BlockSpec((1, share // steps, size, size), lambda i: (matrix, i, 0, 0))
        extra = [] if buffer is None else [buffer]
        return line(
            functools.partial(update_kernel, matrix),
            "update",
            [SHAPE(first_moment.shape, F32)],
            [],
            [keep, got, first_moment, second_moment, *extra],
            plan,
            specs=[VMEM, VMEM, block, block] + [ANY] * len(extra),
            out_specs=[block],
            input_output_aliases={5: 0} if extra else {},
            grid=(steps,),
        )[0]

    def finish(held_parts):
        return line(sum_kernel, "finish", [piece], [], held_parts)[0]

    x = gather(inputs, gather_near)
    if lined:
        (order,) = line(
            functools.partial(order_kernel, width // size, capacity), "order",
            [SHAPE((2 * capacity + 2,), jnp.int32)], [], [], plan, out_specs=[SMEM],
        )
    if lined:
        (out_grad,) = line(hold_kernel, "hold", [piece], [], [out_grad, x[2]])
    og = gather(out_grad, gather_line)
    out_parts, in_parts = parts_of(5), parts_of(4)
    hidden, hidden_turned, act, slope, *out_parts = line(
        functools.partial(forward_kernel, len(x), len(out_parts)),
        "forward",
        [narrow, turned, wide, wide, *out_parts],
        [held, acc, acc, total],
        [*x, weights],
        plan,
    )
    if lined:
        out_far = scatter_first(out_parts)
    else:
        outputs = lax.psum_scatter(out_parts[0], "tensor", scatter_dimension=0)
    (x_turned,) = line(
        functools.partial(turn_kernel, len(x)), "turn", [SHAPE((features, size, rows), BF16)], [held], x, plan
    )
    if lined:
        out_sums = scatter_second(line, out_parts, out_far)
    down = grads(2, og, hidden_turned)
    gate_rows, up_rows = line(
        functools.partial(rows_kernel, len(og)),
        "row_grads",
        [narrow, narrow],
        [held, acc],
        [*og, weights, act, slope],
        plan,
    )
    down = fold(*down, 0)
    if lined:
        part_total = pltpu.VMEM((width // size + 1, rows, size), F32)
        in_operands = [gate_rows, up_rows, weights]
        (in_far,) = line(
            functools.partial(input_part_kernel, True), "input_far", [piece], [part_total], in_operands, (*plan, order)
        )
        in_far = flip(in_far, 4, 1)
    if lined:
        in_parts = line(
            functools.partial(input_part_kernel, False), "input_rest", [piece] * 3, [total], in_operands, (*plan, order)
        )
    else:
        in_parts = line(
            functools.partial(input_kernel, 1), "input_grads", in_parts, [total], [gate_rows, up_rows, weights], plan
        )
        input_grad = lax.psum_scatter(in_parts[0], "tensor", scatter_dimension=0)
    gate = grads(0, [gate_rows], x_turned)
    for step in range(1, levels):
        down = fold(*down, step)
    if lined:
        outputs = finish(out_sums)
    gate = fold(*gate, 0)
    buffer = update(2, *down, None)
    up = grads(1, [up_rows], x_turned)
    if lined:
        in_sums = scatter_second(line, in_parts, [in_far])
    up = fold(*up, 0)
    for step in range(1, levels):
        gate = fold(*gate, step)
    for step in range(1, levels):
        up = fold(*up, step)
    buffer = update(0, *gate, buffer)
    if lined:
        input_grad = finish(in_sums)
    buffer = update(1, *up, buffer)
    return (outputs, input_grad, buffer)


def solution(mesh):
    in_specs = (
        P("dp", "tensor"),
        P("dp", "tensor"),
        P(None, "tensor", None, None),
        P(None, "tensor", None),
        P("tensor", None),
        P(None, ("tensor", "dp"), None, None),
        P(None, ("tensor", "dp"), None, None),
    )
    out_specs = (P("dp", "tensor"), P("dp", "tensor"), P(None, ("tensor", "dp"), None, None))
    body = functools.partial(local, mesh.shape["dp"], mesh.shape["tensor"])
    return jax.shard_map(body, mesh=mesh, in_specs=in_specs, out_specs=out_specs, check_vma=False)
```

```python
import functools
import jax
import jax.numpy as jnp
from jax import lax
from jax.experimental import pallas as pl
from jax.experimental.pallas import tpu as pltpu
from jax.sharding import PartitionSpec as P

HB_DEV = 14
EPSILON = 1e-08
GROUPS = (32, 8)
COST = 2 * 10**10
VMEM_LIMIT = 32 * 1024 * 1024
F32, BF16 = jnp.float32, jnp.bfloat16
SHAPE = jax.ShapeDtypeStruct
SMEM = pl.BlockSpec(memory_space=pltpu.SMEM)
VMEM = pl.BlockSpec(memory_space=pltpu.VMEM)
ANY = pl.BlockSpec(memory_space=pl.ANY)
TOKEN = SHAPE((8, 128), F32)
HEAD = 5


def feature_block(ref, block, size):
    per_shard = ref.shape[2] // size
    start = pl.multiple_of(lax.rem(block, per_shard) * size, size)
    return ref.at[lax.div(block, per_shard), :, pl.ds(start, size)]


def slot_pair(plan_ref, matrix, slot, capacity):
    at = HEAD + (matrix * capacity + slot) * 2
    return plan_ref[at], plan_ref[at + 1]


def each_group(first, last, body):
    large, small = GROUPS

    def run(at, size, count, whole):
        def step(i, carry):
            body([at + i * size + u for u in range(size)], whole)
            return carry

        lax.fori_loop(0, count, step, 0)

    full = lax.div(last - first, large)
    rest = first + full * large
    run(first, large, full, True)
    run(rest, small, lax.div(last - rest + (small - 1), small), False)


def dot(a, b, contract):
    return lax.dot_general(a, b, (contract, ((), ())), preferred_element_type=F32)


def accumulate(plan_ref, matrix, capacity, acc, into, product, order=None, base=0):
    trash = acc.shape[0] - 1
    order_ref, first, last = order or (None, 0, plan_ref[2 + matrix])

    def body(places, whole):
        products, targets = [], []
        for p in places:
            here = p if whole else jnp.minimum(p, last - 1)
            s = here if order is None else order_ref[here]
            pair = slot_pair(plan_ref, matrix, s, capacity)
            target = pair[into] - base
            targets.append(target if whole else jnp.where(p < last, target, trash))
            products.append(product(s, *pair))
        for t, p in zip(targets, products):
            acc[t] += p

    each_group(first, last, body)


def order_kernel(per_shard, capacity, plan_ref, order_ref):
    far = lax.bitwise_xor(plan_ref[0], 3)
    for matrix in (0, 1):

        def is_far(s, matrix=matrix):
            return lax.div(slot_pair(plan_ref, matrix, s, capacity)[0], per_shard) == far

        def count(s, total):
            return total + is_far(s).astype(jnp.int32)

        def put(s, at):
            here, there = at
            found = is_far(s)
            order_ref[matrix * capacity + jnp.where(found, here, there)] = s
            step = found.astype(jnp.int32)
            return here + step, there + 1 - step

        live = plan_ref[2 + matrix]
        total = lax.fori_loop(0, live, count, 0)
        order_ref[2 * capacity + matrix] = total
        lax.fori_loop(0, live, put, (0, total))


def load_shards(pieces, held, me):
    if len(pieces) == 1:
        return pieces[0]
    if len(pieces) == 4:
        for offset, piece in enumerate(pieces):
            held[lax.bitwise_xor(me, offset)] = piece[...]
        return held
    own, below, above, across, far = pieces
    last = held.shape[0] - 1
    held[me] = own[...]
    held[lax.bitwise_xor(me, 2)] = across[...]

    @pl.when(me > 0)
    def _():
        held[me - 1] = below[...]

    @pl.when(me < last)
    def _():
        held[me + 1] = above[...]

    @pl.when((me == 0) | (me == last))
    def _():
        held[last - me] = far[...]

    return held


def store_shards(total, outs, me, per_shard, size):
    if len(outs) == 1:
        places = [(outs[0].at[t], t) for t in range(outs[0].shape[0])]
    elif len(outs) == 4:
        places = [(out, lax.bitwise_xor(me, offset)) for offset, out in enumerate(outs)]
    else:
        last = 3
        own, beside, across, far, middle = outs
        places = [(out, lax.bitwise_xor(me, offset)) for offset, out in enumerate((own, beside, across, far))]
        places.append((middle, last - me))
    for out, t in places:
        for c in range(per_shard):
            out[:, c * size : (c + 1) * size] = total[t * per_shard + c].astype(out.dtype)


def forward_kernel(n_pieces, n_outs, plan_ref, *refs):
    pieces, refs = refs[:n_pieces], refs[n_pieces:]
    w_ref, hidden_ref, turned_ref, act_ref, slope_ref = refs[:5]
    outs, (held, gate, up, total) = refs[5 : 5 + n_outs], refs[5 + n_outs :]
    me = plan_ref[0]
    x_ref = load_shards(pieces, held, me)
    capacity, size = w_ref.shape[1], w_ref.shape[2]
    gate[...] = jnp.zeros_like(gate)
    up[...] = jnp.zeros_like(up)
    total[...] = jnp.zeros_like(total)
    for matrix, acc in ((0, gate), (1, up)):
        accumulate(
            plan_ref, matrix, capacity, acc, 1,
            lambda s, f, h, matrix=matrix: dot(feature_block(x_ref, f, size)[...], w_ref[matrix, s], ((1,), (0,))),
        )
    for h in range(hidden_ref.shape[0]):
        g, u = gate[h], up[h]
        sig = 1.0 / (1.0 + jnp.exp(-g))
        act = g * sig
        act_ref[h] = act
        slope_ref[h] = u * sig * (1.0 + g * (1.0 - sig))
        hidden = (act * u).astype(hidden_ref.dtype)
        hidden_ref[h] = hidden
        turned_ref[h] = hidden.T
    accumulate(
        plan_ref, 2, capacity, total, 0,
        lambda s, f, h: dot(hidden_ref[h], w_ref[2, s], ((1,), (0,))),
    )
    store_shards(total, outs, me, x_ref.shape[2] // size, size)


def turn_kernel(n_pieces, plan_ref, *refs):
    pieces, (turned_ref, held) = refs[:n_pieces], refs[n_pieces:]
    x_ref = load_shards(pieces, held, plan_ref[0])
    size = turned_ref.shape[1]
    per_shard = x_ref.shape[2] // size
    for f in range(turned_ref.shape[0]):
        c = f % per_shard
        turned_ref[f] = x_ref[f // per_shard, :, c * size : (c + 1) * size].T


def rows_kernel(n_pieces, plan_ref, *refs):
    pieces, refs = refs[:n_pieces], refs[n_pieces:]
    w_ref, act_ref, slope_ref, gate_rows_ref, up_rows_ref, held, acc = refs
    og_ref = load_shards(pieces, held, plan_ref[0])
    capacity, size = w_ref.shape[1], w_ref.shape[2]
    acc[...] = jnp.zeros_like(acc)
    accumulate(
        plan_ref, 2, capacity, acc, 1,
        lambda s, f, h: dot(feature_block(og_ref, f, size)[...], w_ref[2, s], ((1,), (1,))),
    )
    for h in range(act_ref.shape[0]):
        gate_rows_ref[h] = (acc[h] * slope_ref[h]).astype(gate_rows_ref.dtype)
        up_rows_ref[h] = (acc[h] * act_ref[h]).astype(up_rows_ref.dtype)


def spread(place, core, places):
    levels = places.bit_length() - 1
    turned = sum(lax.shift_left(lax.bitwise_and(lax.shift_right_logical(place, b), 1), levels - 1 - b) for b in range(levels))
    return 2 * jnp.where(core == 0, place, turned)


def grads_kernel(matrix, n_pieces, plan_ref, *refs):
    pieces, refs = refs[:n_pieces], refs[n_pieces:]
    turned_ref, keep_ref, send_ref, held = refs
    size, share = keep_ref.shape[2], keep_ref.shape[1]
    places = keep_ref.shape[0]
    replica = plan_ref[1]
    right_ref = load_shards(pieces, held, plan_ref[0])
    capacity = 2 * places * share
    count = plan_ref[2 + matrix]

    def one_place(q, carry):
        todo = []
        for out, bit in ((send_ref, 1), (keep_ref, 0)):
            owner = lax.bitwise_xor(replica, bit)
            todo.append((out, lax.bitwise_xor(owner, spread(q, lax.bitwise_and(owner, 1), places)) * share))

        @pl.when(jnp.minimum(todo[0][1], todo[1][1]) < count)
        def _():
            for out, first in todo:
                for s in range(share):
                    f, h = slot_pair(plan_ref, matrix, first + s, capacity)
                    if matrix == 2:
                        left, right = turned_ref[h], feature_block(right_ref, f, size)[...]
                    else:
                        left, right = turned_ref[f], right_ref[h]
                    out[q, s] = dot(left, right, ((1,), (0,))).astype(out.dtype)

        return carry

    lax.fori_loop(0, places, one_place, 0)


def input_kernel(n_outs, plan_ref, gate_rows_ref, up_rows_ref, w_ref, *refs):
    outs, (total,) = refs[:n_outs], refs[n_outs:]
    capacity, size = w_ref.shape[1], w_ref.shape[2]
    total[...] = jnp.zeros_like(total)
    for matrix, rows in ((0, gate_rows_ref), (1, up_rows_ref)):
        accumulate(
            plan_ref, matrix, capacity, total, 0,
            lambda s, f, h, matrix=matrix, rows=rows: dot(rows[h], w_ref[matrix, s], ((1,), (1,))),
        )
    store_shards(total, outs, plan_ref[0], outs[0].shape[-1] // size, size)


def input_part_kernel(is_far, plan_ref, order_ref, gate_rows_ref, up_rows_ref, w_ref, *refs):
    *outs, total = refs
    capacity, size = w_ref.shape[1], w_ref.shape[2]
    per_shard = outs[0].shape[-1] // size
    me = plan_ref[0]
    base = lax.bitwise_xor(me, 3) * per_shard if is_far else 0
    total[...] = jnp.zeros_like(total)
    for matrix, rows in ((0, gate_rows_ref), (1, up_rows_ref)):
        at = matrix * capacity
        cut = at + order_ref[2 * capacity + matrix]
        accumulate(
            plan_ref, matrix, capacity, total, 0,
            lambda s, f, h, matrix=matrix, rows=rows: dot(rows[h], w_ref[matrix, s], ((1,), (1,))),
            (order_ref, at, cut) if is_far else (order_ref, cut, at + plan_ref[2 + matrix]),
            base,
        )
    for offset, out in enumerate(outs):
        first = 0 if is_far else lax.bitwise_xor(me, offset) * per_shard
        for c in range(per_shard):
            out[:, c * size : (c + 1) * size] = total[first + c].astype(out.dtype)


def fold_kernel(keep_ref, got_ref, keep_out, send_out):
    half = keep_out.shape[0]
    keep_out[...] = keep_ref[:half] + got_ref[:half]
    send_out[...] = keep_ref[half:] + got_ref[half:]


def join_kernel(*refs):
    ins, outs = refs[: len(refs) // 2 + 1], refs[len(refs) // 2 + 1 :]
    outs[0][...] = ins[0][...] + ins[1][...]
    for source, out in zip(ins[2:], outs[1:]):
        out[...] = source[...]


def sum_kernel(*refs):
    *parts, out_ref = refs
    total = parts[0][...].astype(F32)
    for part in parts[1:]:
        total += part[...].astype(F32)
    out_ref[...] = total.astype(out_ref.dtype)


def update_kernel(matrix, plan_ref, keep_ref, got_ref, m1_ref, m2_ref, *refs):
    out_ref = refs[-1]
    share = keep_ref.shape[1]
    first = plan_ref[1] * share
    for s in range(share):
        g = keep_ref[0, s].astype(F32) + got_ref[0, s].astype(F32)
        first_new = 0.9 * m1_ref[0, s] + 0.1 * g
        second_new = 0.95 * m2_ref[0, s] + 0.05 * g * g
        live = first + s < plan_ref[2 + matrix]
        out_ref[0, s] = jnp.where(live, first_new / (jnp.sqrt(second_new) + EPSILON), 0.0)


def hold_kernel(v_ref, _, out_ref):
    out_ref[...] = v_ref[...]


class Line:
    token = None

    def __call__(self, kernel, name, outs, scratch, operands, plan=(), after=(), specs=None, out_specs=None, cost=COST, **more):
        scalars = [*plan]
        extra = [*after] if self.token is None else [*after, self.token]
        n_in, n_out = len(scalars) + len(operands), len(outs)

        def body(*refs):
            ins, rest = refs[:n_in], refs[n_in + len(extra) :]
            results, token, scratches = rest[:n_out], rest[n_out], rest[n_out + 1 :]
            token[...] = jnp.zeros_like(token)
            kernel(*ins, *results, *scratches)

        *results, self.token = pl.pallas_call(
            body,
            name=name,
            out_shape=[*outs, TOKEN],
            in_specs=[SMEM] * len(scalars) + (specs or [VMEM] * len(operands)) + [VMEM] * len(extra),
            out_specs=[*(out_specs or [VMEM] * n_out), VMEM],
            scratch_shapes=scratch,
            compiler_params=pltpu.CompilerParams(vmem_limit_bytes=VMEM_LIMIT),
            cost_estimate=pl.CostEstimate(flops=cost, bytes_accessed=0, transcendentals=0),
            **more,
        )(*scalars, *operands, *extra)
        return results


def flip(v, shards, bit):
    return lax.ppermute(v, "tensor", [(a, a ^ bit) for a in range(shards)])


def gather_near(v):
    across, beside = flip(v, 4, 2), flip(v, 4, 1)
    return [v, beside, across, flip(across, 4, 1)]


def gather_line(v):
    across = flip(v, 4, 2)
    below = lax.ppermute(v, "tensor", [(a, a + 1) for a in range(3)])
    above = lax.ppermute(v, "tensor", [(a + 1, a) for a in range(3)])
    far = lax.ppermute(across, "tensor", [(2, 3), (1, 0)])
    return [v, below, above, across, far]


def scatter_first(parts):
    return [lax.ppermute(parts[3], "tensor", [(0, 1), (3, 2)]), lax.ppermute(parts[4], "tensor", [(1, 2), (2, 1)])]


def scatter_second(line, parts, came, after=()):
    piece = SHAPE(parts[0].shape, parts[0].dtype)
    own, beside, across = parts[:3]
    across, beside = line(join_kernel, "join", [piece] * 2, [], [across, came[0], beside], (), after)
    return [own, flip(across, 4, 2), flip(beside, 4, 1), *came[1:]]


def core_swap(v, replicas):
    return lax.ppermute(v, "dp", [(a, a ^ 1) for a in range(replicas)])


def axis_swap(v, replicas, step):
    levels = replicas.bit_length() - 2
    pairs = [(a, a ^ (1 << (1 + step if a & 1 else levels - step))) for a in range(replicas)]
    return lax.ppermute(v, "dp", pairs)


def local(replicas, shards, inputs, out_grad, weights, block_index, block_counts, first_moment, second_moment):
    capacity, size = weights.shape[1], weights.shape[2]
    rows, width = inputs.shape
    me = jnp.stack([lax.axis_index("tensor"), lax.axis_index("dp")]).astype(jnp.int32)
    plan = (jnp.concatenate([me, block_counts[0], block_index.reshape(-1)]),)
    features = shards * width // size
    places, share = replicas // 2, capacity // replicas
    levels = places.bit_length() - 1
    held = pltpu.VMEM((shards, rows, width), BF16)
    acc = pltpu.VMEM((HB_DEV + 1, rows, size), F32)
    total = pltpu.VMEM((features + 1, rows, size), F32)
    wide = SHAPE((HB_DEV, rows, size), F32)
    narrow = SHAPE((HB_DEV, rows, size), BF16)
    turned = SHAPE((HB_DEV, size, rows), BF16)
    piece = SHAPE((rows, width), BF16)
    line = Line()
    lined = shards == 4

    def gather(v, form):
        return form(v) if lined else [lax.all_gather(v, "tensor", axis=0)]

    def parts_of(count):
        return [piece] * count if lined else [SHAPE((shards, rows, width), BF16)]

    def grads(matrix, right, left, after=()):
        half = SHAPE((places, share, size, size), BF16)
        name = ("gate_grads", "up_grads", "down_grads")[matrix]
        kernel = functools.partial(grads_kernel, matrix, len(right))
        keep, send = line(kernel, name, [half, half], [held], [*right, left], plan, after)
        return keep, core_swap(send, replicas)

    def fold(keep, got, step, after=()):
        half = SHAPE((keep.shape[0] // 2, *keep.shape[1:]), BF16)
        keep, send = line(fold_kernel, "fold", [half, half], [], [keep, got], (), after)
        return keep, axis_swap(send, replicas, step)

    def update(matrix, keep, got, buffer):
        block = pl.BlockSpec((1, share, size, size), lambda i: (matrix, 0, 0, 0))
        extra = [] if buffer is None else [buffer]
        return line(
            functools.partial(update_kernel, matrix),
            "update",
            [SHAPE(first_moment.shape, F32)],
            [],
            [keep, got, first_moment, second_moment, *extra],
            plan,
            specs=[VMEM, VMEM, block, block] + [ANY] * len(extra),
            out_specs=[block],
            input_output_aliases={5: 0} if extra else {},
            grid=(1,),
        )[0]

    def finish(held_parts):
        return line(sum_kernel, "finish", [piece], [], held_parts)[0]

    def touch(*arrived):
        line(lambda: None, "touch", [], [], [], (), arrived)

    x = gather(inputs, gather_near)
    if lined:
        (order,) = line(
            functools.partial(order_kernel, width // size, capacity), "order",
            [SHAPE((2 * capacity + 2,), jnp.int32)], [], [], plan, out_specs=[SMEM],
        )
    if lined:
        (out_grad,) = line(hold_kernel, "hold", [piece], [], [out_grad, x[2]])
    og = gather(out_grad, gather_line)
    out_parts, in_parts = parts_of(5), parts_of(4)
    hidden, hidden_turned, act, slope, *out_parts = line(
        functools.partial(forward_kernel, len(x), len(out_parts)),
        "forward",
        [narrow, turned, wide, wide, *out_parts],
        [held, acc, acc, total],
        [*x, weights],
        plan,
    )
    if lined:
        out_far = scatter_first(out_parts)
    else:
        outputs = lax.psum_scatter(out_parts[0], "tensor", scatter_dimension=0)
    (x_turned,) = line(
        functools.partial(turn_kernel, len(x)), "turn", [SHAPE((features, size, rows), BF16)], [held], x, plan
    )
    buffer = None
    if lined:
        out_sums = scatter_second(line, out_parts, out_far)
    down = grads(2, og, hidden_turned)
    gate_rows, up_rows = line(
        functools.partial(rows_kernel, len(og)),
        "row_grads",
        [narrow, narrow],
        [held, acc],
        [*og, weights, act, slope],
        plan,
    )
    down = fold(*down, 0)
    if lined:
        part_total = pltpu.VMEM((width // size + 1, rows, size), F32)
        in_operands = [gate_rows, up_rows, weights]
        (in_far,) = line(
            functools.partial(input_part_kernel, True), "input_far", [piece], [part_total], in_operands, (*plan, order)
        )
        in_far = flip(in_far, 4, 1)
    gate = grads(0, [gate_rows], x_turned, out_far[1:] if lined else ())
    if lined:
        in_parts = line(
            functools.partial(input_part_kernel, False), "input_rest", [piece] * 3, [total], in_operands, (*plan, order)
        )
    else:
        in_parts = line(
            functools.partial(input_kernel, 1), "input_grads", in_parts, [total], [gate_rows, up_rows, weights], plan
        )
        input_grad = lax.psum_scatter(in_parts[0], "tensor", scatter_dimension=0)
    for step in range(1, levels):
        down = fold(*down, step)
    if lined:
        outputs = finish(out_sums)
    gate = fold(*gate, 0)
    buffer = update(2, *down, buffer)
    up = grads(1, [up_rows], x_turned)
    if lined:
        in_sums = scatter_second(line, in_parts, [in_far])
    up = fold(*up, 0)
    for step in range(1, levels):
        gate = fold(*gate, step)
    for step in range(1, levels):
        up = fold(*up, step)
    buffer = update(0, *gate, buffer)
    if lined:
        input_grad = finish(in_sums)
    buffer = update(1, *up, buffer)
    return (outputs, input_grad, buffer)


def solution(mesh):
    in_specs = (
        P("dp", "tensor"),
        P("dp", "tensor"),
        P(None, "tensor", None, None),
        P(None, "tensor", None),
        P("tensor", None),
        P(None, ("tensor", "dp"), None, None),
        P(None, ("tensor", "dp"), None, None),
    )
    out_specs = (P("dp", "tensor"), P("dp", "tensor"), P(None, ("tensor", "dp"), None, None))
    body = functools.partial(local, mesh.shape["dp"], mesh.shape["tensor"])
    return jax.shard_map(body, mesh=mesh, in_specs=in_specs, out_specs=out_specs, check_vma=False)
```

```python
import functools
import jax
import jax.numpy as jnp
from jax import lax
from jax.experimental import pallas as pl
from jax.experimental.pallas import tpu as pltpu
from jax.sharding import PartitionSpec as P

HB_DEV = 14
EPSILON = 1e-08
GROUPS = (32, 8)
COST = 2 * 10**10
VMEM_LIMIT = 32 * 1024 * 1024
F32, BF16 = jnp.float32, jnp.bfloat16
SHAPE = jax.ShapeDtypeStruct
SMEM = pl.BlockSpec(memory_space=pltpu.SMEM)
VMEM = pl.BlockSpec(memory_space=pltpu.VMEM)
ANY = pl.BlockSpec(memory_space=pl.ANY)
TOKEN = SHAPE((8, 128), F32)
HEAD = 5


def feature_block(ref, block, size):
    per_shard = ref.shape[2] // size
    start = pl.multiple_of(lax.rem(block, per_shard) * size, size)
    return ref.at[lax.div(block, per_shard), :, pl.ds(start, size)]


def slot_pair(plan_ref, matrix, slot, capacity):
    at = HEAD + (matrix * capacity + slot) * 2
    return plan_ref[at], plan_ref[at + 1]


def each_group(first, last, body):
    large, small = GROUPS

    def run(at, size, count, whole):
        def step(i, carry):
            body([at + i * size + u for u in range(size)], whole)
            return carry

        lax.fori_loop(0, count, step, 0)

    full = lax.div(last - first, large)
    rest = first + full * large
    run(first, large, full, True)
    run(rest, small, lax.div(last - rest + (small - 1), small), False)


def dot(a, b, contract):
    return lax.dot_general(a, b, (contract, ((), ())), preferred_element_type=F32)


def accumulate(plan_ref, matrix, capacity, acc, into, product, order=None, base=0):
    trash = acc.shape[0] - 1
    order_ref, first, last = order or (None, 0, plan_ref[2 + matrix])

    def body(places, whole):
        products, targets = [], []
        for p in places:
            here = p if whole else jnp.minimum(p, last - 1)
            s = here if order is None else order_ref[here]
            pair = slot_pair(plan_ref, matrix, s, capacity)
            target = pair[into] - base
            targets.append(target if whole else jnp.where(p < last, target, trash))
            products.append(product(s, *pair))
        for t, p in zip(targets, products):
            acc[t] += p

    each_group(first, last, body)


def order_kernel(per_shard, capacity, plan_ref, order_ref):
    far = lax.bitwise_xor(plan_ref[0], 3)
    for matrix in (0, 1):

        def is_far(s, matrix=matrix):
            return lax.div(slot_pair(plan_ref, matrix, s, capacity)[0], per_shard) == far

        def count(s, total):
            return total + is_far(s).astype(jnp.int32)

        def put(s, at):
            here, there = at
            found = is_far(s)
            order_ref[matrix * capacity + jnp.where(found, here, there)] = s
            step = found.astype(jnp.int32)
            return here + step, there + 1 - step

        live = plan_ref[2 + matrix]
        total = lax.fori_loop(0, live, count, 0)
        order_ref[2 * capacity + matrix] = total
        lax.fori_loop(0, live, put, (0, total))


def load_shards(pieces, held, me):
    if len(pieces) == 1:
        return pieces[0]
    if len(pieces) == 4:
        for offset, piece in enumerate(pieces):
            held[lax.bitwise_xor(me, offset)] = piece[...]
        return held
    own, below, above, across, far = pieces
    last = held.shape[0] - 1
    held[me] = own[...]
    held[lax.bitwise_xor(me, 2)] = across[...]

    @pl.when(me > 0)
    def _():
        held[me - 1] = below[...]

    @pl.when(me < last)
    def _():
        held[me + 1] = above[...]

    @pl.when((me == 0) | (me == last))
    def _():
        held[last - me] = far[...]

    return held


def store_shards(total, outs, me, per_shard, size):
    if len(outs) == 1:
        places = [(outs[0].at[t], t) for t in range(outs[0].shape[0])]
    elif len(outs) == 4:
        places = [(out, lax.bitwise_xor(me, offset)) for offset, out in enumerate(outs)]
    else:
        last = 3
        own, beside, across, far, middle = outs
        places = [(out, lax.bitwise_xor(me, offset)) for offset, out in enumerate((own, beside, across, far))]
        places.append((middle, last - me))
    for out, t in places:
        for c in range(per_shard):
            out[:, c * size : (c + 1) * size] = total[t * per_shard + c].astype(out.dtype)


def forward_kernel(n_pieces, n_outs, plan_ref, *refs):
    pieces, refs = refs[:n_pieces], refs[n_pieces:]
    w_ref, hidden_ref, turned_ref, act_ref, slope_ref = refs[:5]
    outs, (held, gate, up, total) = refs[5 : 5 + n_outs], refs[5 + n_outs :]
    me = plan_ref[0]
    x_ref = load_shards(pieces, held, me)
    capacity, size = w_ref.shape[1], w_ref.shape[2]
    gate[...] = jnp.zeros_like(gate)
    up[...] = jnp.zeros_like(up)
    total[...] = jnp.zeros_like(total)
    for matrix, acc in ((0, gate), (1, up)):
        accumulate(
            plan_ref, matrix, capacity, acc, 1,
            lambda s, f, h, matrix=matrix: dot(feature_block(x_ref, f, size)[...], w_ref[matrix, s], ((1,), (0,))),
        )
    for h in range(hidden_ref.shape[0]):
        g, u = gate[h], up[h]
        sig = 1.0 / (1.0 + jnp.exp(-g))
        act = g * sig
        act_ref[h] = act
        slope_ref[h] = u * sig * (1.0 + g * (1.0 - sig))
        hidden = (act * u).astype(hidden_ref.dtype)
        hidden_ref[h] = hidden
        turned_ref[h] = hidden.T
    accumulate(
        plan_ref, 2, capacity, total, 0,
        lambda s, f, h: dot(hidden_ref[h], w_ref[2, s], ((1,), (0,))),
    )
    store_shards(total, outs, me, x_ref.shape[2] // size, size)


def turn_kernel(n_pieces, plan_ref, *refs):
    pieces, (turned_ref, held) = refs[:n_pieces], refs[n_pieces:]
    x_ref = load_shards(pieces, held, plan_ref[0])
    size = turned_ref.shape[1]
    per_shard = x_ref.shape[2] // size
    for f in range(turned_ref.shape[0]):
        c = f % per_shard
        turned_ref[f] = x_ref[f // per_shard, :, c * size : (c + 1) * size].T


def rows_kernel(n_pieces, plan_ref, *refs):
    pieces, refs = refs[:n_pieces], refs[n_pieces:]
    w_ref, act_ref, slope_ref, gate_rows_ref, up_rows_ref, held, acc = refs
    og_ref = load_shards(pieces, held, plan_ref[0])
    capacity, size = w_ref.shape[1], w_ref.shape[2]
    acc[...] = jnp.zeros_like(acc)
    accumulate(
        plan_ref, 2, capacity, acc, 1,
        lambda s, f, h: dot(feature_block(og_ref, f, size)[...], w_ref[2, s], ((1,), (1,))),
    )
    for h in range(act_ref.shape[0]):
        gate_rows_ref[h] = (acc[h] * slope_ref[h]).astype(gate_rows_ref.dtype)
        up_rows_ref[h] = (acc[h] * act_ref[h]).astype(up_rows_ref.dtype)


def spread(place, core, places):
    levels = places.bit_length() - 1
    turned = sum(lax.shift_left(lax.bitwise_and(lax.shift_right_logical(place, b), 1), levels - 1 - b) for b in range(levels))
    return 2 * jnp.where(core == 0, place, turned)


def grads_kernel(matrix, n_pieces, plan_ref, *refs):
    pieces, refs = refs[:n_pieces], refs[n_pieces:]
    turned_ref, keep_ref, send_ref, held = refs
    size, share = keep_ref.shape[2], keep_ref.shape[1]
    places = keep_ref.shape[0]
    replica = plan_ref[1]
    right_ref = load_shards(pieces, held, plan_ref[0])
    capacity = 2 * places * share
    count = plan_ref[2 + matrix]

    def one_place(q, carry):
        todo = []
        for out, bit in ((send_ref, 1), (keep_ref, 0)):
            owner = lax.bitwise_xor(replica, bit)
            todo.append((out, lax.bitwise_xor(owner, spread(q, lax.bitwise_and(owner, 1), places)) * share))

        @pl.when(jnp.minimum(todo[0][1], todo[1][1]) < count)
        def _():
            for out, first in todo:
                for s in range(share):
                    f, h = slot_pair(plan_ref, matrix, first + s, capacity)
                    if matrix == 2:
                        left, right = turned_ref[h], feature_block(right_ref, f, size)[...]
                    else:
                        left, right = turned_ref[f], right_ref[h]
                    out[q, s] = dot(left, right, ((1,), (0,))).astype(out.dtype)

        return carry

    lax.fori_loop(0, places, one_place, 0)


def input_kernel(n_outs, plan_ref, gate_rows_ref, up_rows_ref, w_ref, *refs):
    outs, (total,) = refs[:n_outs], refs[n_outs:]
    capacity, size = w_ref.shape[1], w_ref.shape[2]
    total[...] = jnp.zeros_like(total)
    for matrix, rows in ((0, gate_rows_ref), (1, up_rows_ref)):
        accumulate(
            plan_ref, matrix, capacity, total, 0,
            lambda s, f, h, matrix=matrix, rows=rows: dot(rows[h], w_ref[matrix, s], ((1,), (1,))),
        )
    store_shards(total, outs, plan_ref[0], outs[0].shape[-1] // size, size)


def input_part_kernel(is_far, plan_ref, order_ref, gate_rows_ref, up_rows_ref, w_ref, *refs):
    *outs, total = refs
    capacity, size = w_ref.shape[1], w_ref.shape[2]
    per_shard = outs[0].shape[-1] // size
    me = plan_ref[0]
    base = lax.bitwise_xor(me, 3) * per_shard if is_far else 0
    total[...] = jnp.zeros_like(total)
    for matrix, rows in ((0, gate_rows_ref), (1, up_rows_ref)):
        at = matrix * capacity
        cut = at + order_ref[2 * capacity + matrix]
        accumulate(
            plan_ref, matrix, capacity, total, 0,
            lambda s, f, h, matrix=matrix, rows=rows: dot(rows[h], w_ref[matrix, s], ((1,), (1,))),
            (order_ref, at, cut) if is_far else (order_ref, cut, at + plan_ref[2 + matrix]),
            base,
        )
    for offset, out in enumerate(outs):
        first = 0 if is_far else lax.bitwise_xor(me, offset) * per_shard
        for c in range(per_shard):
            out[:, c * size : (c + 1) * size] = total[first + c].astype(out.dtype)


def fold_kernel(keep_ref, got_ref, keep_out, send_out):
    half = keep_out.shape[0]
    keep_out[...] = keep_ref[:half] + got_ref[:half]
    send_out[...] = keep_ref[half:] + got_ref[half:]


def join_kernel(*refs):
    ins, outs = refs[: len(refs) // 2 + 1], refs[len(refs) // 2 + 1 :]
    outs[0][...] = ins[0][...] + ins[1][...]
    for source, out in zip(ins[2:], outs[1:]):
        out[...] = source[...]


def sum_kernel(*refs):
    *parts, out_ref = refs
    total = parts[0][...].astype(F32)
    for part in parts[1:]:
        total += part[...].astype(F32)
    out_ref[...] = total.astype(out_ref.dtype)


def update_kernel(matrix, plan_ref, keep_ref, got_ref, m1_ref, m2_ref, *refs):
    out_ref = refs[-1]
    share = keep_ref.shape[1]
    first = plan_ref[1] * share
    for s in range(share):
        g = keep_ref[0, s].astype(F32) + got_ref[0, s].astype(F32)
        first_new = 0.9 * m1_ref[0, s] + 0.1 * g
        second_new = 0.95 * m2_ref[0, s] + 0.05 * g * g
        live = first + s < plan_ref[2 + matrix]
        out_ref[0, s] = jnp.where(live, first_new / (jnp.sqrt(second_new) + EPSILON), 0.0)


def hold_kernel(v_ref, _, out_ref):
    out_ref[...] = v_ref[...]


class Line:
    token = None

    def __call__(self, kernel, name, outs, scratch, operands, plan=(), after=(), specs=None, out_specs=None, cost=COST, **more):
        scalars = [*plan]
        extra = [*after] if self.token is None else [*after, self.token]
        n_in, n_out = len(scalars) + len(operands), len(outs)

        def body(*refs):
            ins, rest = refs[:n_in], refs[n_in + len(extra) :]
            results, token, scratches = rest[:n_out], rest[n_out], rest[n_out + 1 :]
            token[...] = jnp.zeros_like(token)
            kernel(*ins, *results, *scratches)

        *results, self.token = pl.pallas_call(
            body,
            name=name,
            out_shape=[*outs, TOKEN],
            in_specs=[SMEM] * len(scalars) + (specs or [VMEM] * len(operands)) + [VMEM] * len(extra),
            out_specs=[*(out_specs or [VMEM] * n_out), VMEM],
            scratch_shapes=scratch,
            compiler_params=pltpu.CompilerParams(vmem_limit_bytes=VMEM_LIMIT),
            cost_estimate=pl.CostEstimate(flops=cost, bytes_accessed=0, transcendentals=0),
            **more,
        )(*scalars, *operands, *extra)
        return results


def flip(v, shards, bit):
    return lax.ppermute(v, "tensor", [(a, a ^ bit) for a in range(shards)])


def gather_near(v):
    across, beside = flip(v, 4, 2), flip(v, 4, 1)
    return [v, beside, across, flip(across, 4, 1)]


def gather_line(v):
    across = flip(v, 4, 2)
    below = lax.ppermute(v, "tensor", [(a, a + 1) for a in range(3)])
    above = lax.ppermute(v, "tensor", [(a + 1, a) for a in range(3)])
    far = lax.ppermute(across, "tensor", [(2, 3), (1, 0)])
    return [v, below, above, across, far]


def scatter_first(parts):
    return [lax.ppermute(parts[3], "tensor", [(0, 1), (3, 2)]), lax.ppermute(parts[4], "tensor", [(1, 2), (2, 1)])]


def scatter_second(line, parts, came, after=()):
    piece = SHAPE(parts[0].shape, parts[0].dtype)
    own, beside, across = parts[:3]
    across, beside = line(join_kernel, "join", [piece] * 2, [], [across, came[0], beside], (), after)
    return [own, flip(across, 4, 2), flip(beside, 4, 1), *came[1:]]


def core_swap(v, replicas):
    return lax.ppermute(v, "dp", [(a, a ^ 1) for a in range(replicas)])


def axis_swap(v, replicas, step):
    levels = replicas.bit_length() - 2
    pairs = [(a, a ^ (1 << (1 + step if a & 1 else levels - step))) for a in range(replicas)]
    return lax.ppermute(v, "dp", pairs)


def local(replicas, shards, inputs, out_grad, weights, block_index, block_counts, first_moment, second_moment):
    capacity, size = weights.shape[1], weights.shape[2]
    rows, width = inputs.shape
    me = jnp.stack([lax.axis_index("tensor"), lax.axis_index("dp")]).astype(jnp.int32)
    plan = (jnp.concatenate([me, block_counts[0], block_index.reshape(-1)]),)
    features = shards * width // size
    places, share = replicas // 2, capacity // replicas
    levels = places.bit_length() - 1
    held = pltpu.VMEM((shards, rows, width), BF16)
    acc = pltpu.VMEM((HB_DEV + 1, rows, size), F32)
    total = pltpu.VMEM((features + 1, rows, size), F32)
    wide = SHAPE((HB_DEV, rows, size), F32)
    narrow = SHAPE((HB_DEV, rows, size), BF16)
    turned = SHAPE((HB_DEV, size, rows), BF16)
    piece = SHAPE((rows, width), BF16)
    line = Line()
    lined = shards == 4

    def gather(v, form):
        return form(v) if lined else [lax.all_gather(v, "tensor", axis=0)]

    def parts_of(count):
        return [piece] * count if lined else [SHAPE((shards, rows, width), BF16)]

    def grads(matrix, right, left, after=()):
        half = SHAPE((places, share, size, size), BF16)
        name = ("gate_grads", "up_grads", "down_grads")[matrix]
        kernel = functools.partial(grads_kernel, matrix, len(right))
        keep, send = line(kernel, name, [half, half], [held], [*right, left], plan, after)
        return keep, core_swap(send, replicas)

    def fold(keep, got, step, after=()):
        half = SHAPE((keep.shape[0] // 2, *keep.shape[1:]), BF16)
        keep, send = line(fold_kernel, "fold", [half, half], [], [keep, got], (), after)
        return keep, axis_swap(send, replicas, step)

    def update(matrix, keep, got, buffer):
        block = pl.BlockSpec((1, share, size, size), lambda i: (matrix, 0, 0, 0))
        extra = [] if buffer is None else [buffer]
        return line(
            functools.partial(update_kernel, matrix),
            "update",
            [SHAPE(first_moment.shape, F32)],
            [],
            [keep, got, first_moment, second_moment, *extra],
            plan,
            specs=[VMEM, VMEM, block, block] + [ANY] * len(extra),
            out_specs=[block],
            input_output_aliases={5: 0} if extra else {},
            grid=(1,),
        )[0]

    def finish(held_parts):
        return line(sum_kernel, "finish", [piece], [], held_parts)[0]

    def touch(*arrived):
        line(lambda: None, "touch", [], [], [], (), arrived)

    x = gather(inputs, gather_near)
    if lined:
        (order,) = line(
            functools.partial(order_kernel, width // size, capacity), "order",
            [SHAPE((2 * capacity + 2,), jnp.int32)], [], [], plan, out_specs=[SMEM],
        )
    if lined:
        (out_grad,) = line(hold_kernel, "hold", [piece], [], [out_grad, x[2]])
    og = gather(out_grad, gather_line)
    out_parts, in_parts = parts_of(5), parts_of(4)
    hidden, hidden_turned, act, slope, *out_parts = line(
        functools.partial(forward_kernel, len(x), len(out_parts)),
        "forward",
        [narrow, turned, wide, wide, *out_parts],
        [held, acc, acc, total],
        [*x, weights],
        plan,
    )
    if lined:
        out_far = scatter_first(out_parts)
    else:
        outputs = lax.psum_scatter(out_parts[0], "tensor", scatter_dimension=0)
    (x_turned,) = line(
        functools.partial(turn_kernel, len(x)), "turn", [SHAPE((features, size, rows), BF16)], [held], x, plan
    )
    buffer = None
    if lined:
        out_sums = scatter_second(line, out_parts, out_far)
    down = grads(2, og, hidden_turned)
    gate_rows, up_rows = line(
        functools.partial(rows_kernel, len(og)),
        "row_grads",
        [narrow, narrow],
        [held, acc],
        [*og, weights, act, slope],
        plan,
    )
    down = fold(*down, 0)
    if lined:
        part_total = pltpu.VMEM((width // size + 1, rows, size), F32)
        in_operands = [gate_rows, up_rows, weights]
        (in_far,) = line(
            functools.partial(input_part_kernel, True), "input_far", [piece], [part_total], in_operands, (*plan, order)
        )
        in_far = flip(in_far, 4, 1)
    if lined:
        in_parts = line(
            functools.partial(input_part_kernel, False), "input_rest", [piece] * 3, [total], in_operands, (*plan, order)
        )
    else:
        in_parts = line(
            functools.partial(input_kernel, 1), "input_grads", in_parts, [total], [gate_rows, up_rows, weights], plan
        )
        input_grad = lax.psum_scatter(in_parts[0], "tensor", scatter_dimension=0)
    gate = grads(0, [gate_rows], x_turned, out_far[1:] if lined else ())
    for step in range(1, levels):
        down = fold(*down, step)
    if lined:
        outputs = finish(out_sums)
    gate = fold(*gate, 0)
    up = grads(1, [up_rows], x_turned)
    buffer = update(2, *down, buffer)
    if lined:
        in_sums = scatter_second(line, in_parts, [in_far])
    up = fold(*up, 0)
    for step in range(1, levels):
        gate = fold(*gate, step)
    for step in range(1, levels):
        up = fold(*up, step)
    buffer = update(0, *gate, buffer)
    if lined:
        input_grad = finish(in_sums)
    buffer = update(1, *up, buffer)
    return (outputs, input_grad, buffer)


def solution(mesh):
    in_specs = (
        P("dp", "tensor"),
        P("dp", "tensor"),
        P(None, "tensor", None, None),
        P(None, "tensor", None),
        P("tensor", None),
        P(None, ("tensor", "dp"), None, None),
        P(None, ("tensor", "dp"), None, None),
    )
    out_specs = (P("dp", "tensor"), P("dp", "tensor"), P(None, ("tensor", "dp"), None, None))
    body = functools.partial(local, mesh.shape["dp"], mesh.shape["tensor"])
    return jax.shard_map(body, mesh=mesh, in_specs=in_specs, out_specs=out_specs, check_vma=False)
```

```python
import functools
import jax
import jax.numpy as jnp
from jax import lax
from jax.experimental import pallas as pl
from jax.experimental.pallas import tpu as pltpu
from jax.sharding import PartitionSpec as P

HB_DEV = 14
EPSILON = 1e-08
GROUPS = (32, 16)
COST = 2 * 10**10
VMEM_LIMIT = 32 * 1024 * 1024
F32, BF16 = jnp.float32, jnp.bfloat16
SHAPE = jax.ShapeDtypeStruct
SMEM = pl.BlockSpec(memory_space=pltpu.SMEM)
VMEM = pl.BlockSpec(memory_space=pltpu.VMEM)
ANY = pl.BlockSpec(memory_space=pl.ANY)
TOKEN = SHAPE((8, 128), F32)
HEAD = 5


def feature_block(ref, block, size):
    per_shard = ref.shape[2] // size
    start = pl.multiple_of(lax.rem(block, per_shard) * size, size)
    return ref.at[lax.div(block, per_shard), :, pl.ds(start, size)]


def slot_pair(plan_ref, matrix, slot, capacity):
    at = HEAD + (matrix * capacity + slot) * 2
    return plan_ref[at], plan_ref[at + 1]


def each_group(first, last, body):
    large, small = GROUPS

    def run(at, size, count, whole):
        def step(i, carry):
            body([at + i * size + u for u in range(size)], whole)
            return carry

        lax.fori_loop(0, count, step, 0)

    full = lax.div(last - first, large)
    rest = first + full * large
    run(first, large, full, True)
    run(rest, small, lax.div(last - rest + (small - 1), small), False)


def dot(a, b, contract):
    return lax.dot_general(a, b, (contract, ((), ())), preferred_element_type=F32)


def accumulate(plan_ref, matrix, capacity, acc, into, product, order=None, base=0):
    trash = acc.shape[0] - 1
    order_ref, first, last = order or (None, 0, plan_ref[2 + matrix])

    def body(places, whole):
        products, targets = [], []
        for p in places:
            here = p if whole else jnp.minimum(p, last - 1)
            s = here if order is None else order_ref[here]
            pair = slot_pair(plan_ref, matrix, s, capacity)
            target = pair[into] - base
            targets.append(target if whole else jnp.where(p < last, target, trash))
            products.append(product(s, *pair))
        for t, p in zip(targets, products):
            acc[t] += p

    each_group(first, last, body)


def order_kernel(per_shard, capacity, plan_ref, order_ref):
    far = lax.bitwise_xor(plan_ref[0], 3)
    for matrix in (0, 1):

        def is_far(s, matrix=matrix):
            return lax.div(slot_pair(plan_ref, matrix, s, capacity)[0], per_shard) == far

        def count(s, total):
            return total + is_far(s).astype(jnp.int32)

        def put(s, at):
            here, there = at
            found = is_far(s)
            order_ref[matrix * capacity + jnp.where(found, here, there)] = s
            step = found.astype(jnp.int32)
            return here + step, there + 1 - step

        live = plan_ref[2 + matrix]
        total = lax.fori_loop(0, live, count, 0)
        order_ref[2 * capacity + matrix] = total
        lax.fori_loop(0, live, put, (0, total))


def load_shards(pieces, held, me):
    if len(pieces) == 1:
        return pieces[0]
    if len(pieces) == 4:
        for offset, piece in enumerate(pieces):
            held[lax.bitwise_xor(me, offset)] = piece[...]
        return held
    own, below, above, across, far = pieces
    last = held.shape[0] - 1
    held[me] = own[...]
    held[lax.bitwise_xor(me, 2)] = across[...]

    @pl.when(me > 0)
    def _():
        held[me - 1] = below[...]

    @pl.when(me < last)
    def _():
        held[me + 1] = above[...]

    @pl.when((me == 0) | (me == last))
    def _():
        held[last - me] = far[...]

    return held


def store_shards(total, outs, me, per_shard, size):
    if len(outs) == 1:
        places = [(outs[0].at[t], t) for t in range(outs[0].shape[0])]
    elif len(outs) == 4:
        places = [(out, lax.bitwise_xor(me, offset)) for offset, out in enumerate(outs)]
    else:
        last = 3
        own, beside, across, far, middle = outs
        places = [(out, lax.bitwise_xor(me, offset)) for offset, out in enumerate((own, beside, across, far))]
        places.append((middle, last - me))
    for out, t in places:
        for c in range(per_shard):
            out[:, c * size : (c + 1) * size] = total[t * per_shard + c].astype(out.dtype)


def forward_kernel(n_pieces, n_outs, plan_ref, *refs):
    pieces, refs = refs[:n_pieces], refs[n_pieces:]
    w_ref, hidden_ref, turned_ref, act_ref, slope_ref = refs[:5]
    outs, (held, gate, up, total) = refs[5 : 5 + n_outs], refs[5 + n_outs :]
    me = plan_ref[0]
    x_ref = load_shards(pieces, held, me)
    capacity, size = w_ref.shape[1], w_ref.shape[2]
    gate[...] = jnp.zeros_like(gate)
    up[...] = jnp.zeros_like(up)
    total[...] = jnp.zeros_like(total)
    for matrix, acc in ((0, gate), (1, up)):
        accumulate(
            plan_ref, matrix, capacity, acc, 1,
            lambda s, f, h, matrix=matrix: dot(feature_block(x_ref, f, size)[...], w_ref[matrix, s], ((1,), (0,))),
        )
    for h in range(hidden_ref.shape[0]):
        g, u = gate[h], up[h]
        sig = 1.0 / (1.0 + jnp.exp(-g))
        act = g * sig
        act_ref[h] = act
        slope_ref[h] = u * sig * (1.0 + g * (1.0 - sig))
        hidden = (act * u).astype(hidden_ref.dtype)
        hidden_ref[h] = hidden
        turned_ref[h] = hidden.T
    accumulate(
        plan_ref, 2, capacity, total, 0,
        lambda s, f, h: dot(hidden_ref[h], w_ref[2, s], ((1,), (0,))),
    )
    store_shards(total, outs, me, x_ref.shape[2] // size, size)


def turn_kernel(n_pieces, plan_ref, *refs):
    pieces, (turned_ref, held) = refs[:n_pieces], refs[n_pieces:]
    x_ref = load_shards(pieces, held, plan_ref[0])
    size = turned_ref.shape[1]
    per_shard = x_ref.shape[2] // size
    for f in range(turned_ref.shape[0]):
        c = f % per_shard
        turned_ref[f] = x_ref[f // per_shard, :, c * size : (c + 1) * size].T


def rows_kernel(n_pieces, plan_ref, *refs):
    pieces, refs = refs[:n_pieces], refs[n_pieces:]
    w_ref, act_ref, slope_ref, gate_rows_ref, up_rows_ref, held, acc = refs
    og_ref = load_shards(pieces, held, plan_ref[0])
    capacity, size = w_ref.shape[1], w_ref.shape[2]
    acc[...] = jnp.zeros_like(acc)
    accumulate(
        plan_ref, 2, capacity, acc, 1,
        lambda s, f, h: dot(feature_block(og_ref, f, size)[...], w_ref[2, s], ((1,), (1,))),
    )
    for h in range(act_ref.shape[0]):
        gate_rows_ref[h] = (acc[h] * slope_ref[h]).astype(gate_rows_ref.dtype)
        up_rows_ref[h] = (acc[h] * act_ref[h]).astype(up_rows_ref.dtype)


def spread(place, core, places):
    levels = places.bit_length() - 1
    turned = sum(lax.shift_left(lax.bitwise_and(lax.shift_right_logical(place, b), 1), levels - 1 - b) for b in range(levels))
    return 2 * jnp.where(core == 0, place, turned)


def grads_kernel(matrix, n_pieces, plan_ref, *refs):
    pieces, refs = refs[:n_pieces], refs[n_pieces:]
    turned_ref, keep_ref, send_ref, held = refs
    size, share = keep_ref.shape[2], keep_ref.shape[1]
    places = keep_ref.shape[0]
    replica = plan_ref[1]
    right_ref = load_shards(pieces, held, plan_ref[0])
    capacity = 2 * places * share
    count = plan_ref[2 + matrix]

    def one_place(q, carry):
        todo = []
        for out, bit in ((send_ref, 1), (keep_ref, 0)):
            owner = lax.bitwise_xor(replica, bit)
            todo.append((out, lax.bitwise_xor(owner, spread(q, lax.bitwise_and(owner, 1), places)) * share))

        @pl.when(jnp.minimum(todo[0][1], todo[1][1]) < count)
        def _():
            for out, first in todo:
                for s in range(share):
                    f, h = slot_pair(plan_ref, matrix, first + s, capacity)
                    if matrix == 2:
                        left, right = turned_ref[h], feature_block(right_ref, f, size)[...]
                    else:
                        left, right = turned_ref[f], right_ref[h]
                    out[q, s] = dot(left, right, ((1,), (0,))).astype(out.dtype)

        return carry

    lax.fori_loop(0, places, one_place, 0)


def input_kernel(n_outs, plan_ref, gate_rows_ref, up_rows_ref, w_ref, *refs):
    outs, (total,) = refs[:n_outs], refs[n_outs:]
    capacity, size = w_ref.shape[1], w_ref.shape[2]
    total[...] = jnp.zeros_like(total)
    for matrix, rows in ((0, gate_rows_ref), (1, up_rows_ref)):
        accumulate(
            plan_ref, matrix, capacity, total, 0,
            lambda s, f, h, matrix=matrix, rows=rows: dot(rows[h], w_ref[matrix, s], ((1,), (1,))),
        )
    store_shards(total, outs, plan_ref[0], outs[0].shape[-1] // size, size)


def input_part_kernel(is_far, plan_ref, order_ref, gate_rows_ref, up_rows_ref, w_ref, *refs):
    *outs, total = refs
    capacity, size = w_ref.shape[1], w_ref.shape[2]
    per_shard = outs[0].shape[-1] // size
    me = plan_ref[0]
    base = lax.bitwise_xor(me, 3) * per_shard if is_far else 0
    total[...] = jnp.zeros_like(total)
    for matrix, rows in ((0, gate_rows_ref), (1, up_rows_ref)):
        at = matrix * capacity
        cut = at + order_ref[2 * capacity + matrix]
        accumulate(
            plan_ref, matrix, capacity, total, 0,
            lambda s, f, h, matrix=matrix, rows=rows: dot(rows[h], w_ref[matrix, s], ((1,), (1,))),
            (order_ref, at, cut) if is_far else (order_ref, cut, at + plan_ref[2 + matrix]),
            base,
        )
    for offset, out in enumerate(outs):
        first = 0 if is_far else lax.bitwise_xor(me, offset) * per_shard
        for c in range(per_shard):
            out[:, c * size : (c + 1) * size] = total[first + c].astype(out.dtype)


def fold_kernel(keep_ref, got_ref, keep_out, send_out):
    half = keep_out.shape[0]
    keep_out[...] = keep_ref[:half] + got_ref[:half]
    send_out[...] = keep_ref[half:] + got_ref[half:]


def join_kernel(*refs):
    ins, outs = refs[: len(refs) // 2 + 1], refs[len(refs) // 2 + 1 :]
    outs[0][...] = ins[0][...] + ins[1][...]
    for source, out in zip(ins[2:], outs[1:]):
        out[...] = source[...]


def sum_kernel(*refs):
    *parts, out_ref = refs
    total = parts[0][...].astype(F32)
    for part in parts[1:]:
        total += part[...].astype(F32)
    out_ref[...] = total.astype(out_ref.dtype)


def update_kernel(matrix, plan_ref, keep_ref, got_ref, m1_ref, m2_ref, *refs):
    out_ref = refs[-1]
    share = keep_ref.shape[1]
    first = plan_ref[1] * share
    for s in range(share):
        g = keep_ref[0, s].astype(F32) + got_ref[0, s].astype(F32)
        first_new = 0.9 * m1_ref[0, s] + 0.1 * g
        second_new = 0.95 * m2_ref[0, s] + 0.05 * g * g
        live = first + s < plan_ref[2 + matrix]
        out_ref[0, s] = jnp.where(live, first_new / (jnp.sqrt(second_new) + EPSILON), 0.0)


def hold_kernel(v_ref, _, out_ref):
    out_ref[...] = v_ref[...]


class Line:
    token = None

    def __call__(self, kernel, name, outs, scratch, operands, plan=(), after=(), specs=None, out_specs=None, cost=COST, **more):
        scalars = [*plan]
        extra = [*after] if self.token is None else [*after, self.token]
        n_in, n_out = len(scalars) + len(operands), len(outs)

        def body(*refs):
            ins, rest = refs[:n_in], refs[n_in + len(extra) :]
            results, token, scratches = rest[:n_out], rest[n_out], rest[n_out + 1 :]
            token[...] = jnp.zeros_like(token)
            kernel(*ins, *results, *scratches)

        *results, self.token = pl.pallas_call(
            body,
            name=name,
            out_shape=[*outs, TOKEN],
            in_specs=[SMEM] * len(scalars) + (specs or [VMEM] * len(operands)) + [VMEM] * len(extra),
            out_specs=[*(out_specs or [VMEM] * n_out), VMEM],
            scratch_shapes=scratch,
            compiler_params=pltpu.CompilerParams(vmem_limit_bytes=VMEM_LIMIT),
            cost_estimate=pl.CostEstimate(flops=cost, bytes_accessed=0, transcendentals=0),
            **more,
        )(*scalars, *operands, *extra)
        return results


def flip(v, shards, bit):
    return lax.ppermute(v, "tensor", [(a, a ^ bit) for a in range(shards)])


def gather_near(v):
    across, beside = flip(v, 4, 2), flip(v, 4, 1)
    return [v, beside, across, flip(across, 4, 1)]


def gather_line(v):
    across = flip(v, 4, 2)
    below = lax.ppermute(v, "tensor", [(a, a + 1) for a in range(3)])
    above = lax.ppermute(v, "tensor", [(a + 1, a) for a in range(3)])
    far = lax.ppermute(across, "tensor", [(2, 3), (1, 0)])
    return [v, below, above, across, far]


def scatter_first(parts):
    return [lax.ppermute(parts[3], "tensor", [(0, 1), (3, 2)]), lax.ppermute(parts[4], "tensor", [(1, 2), (2, 1)])]


def scatter_second(line, parts, came, after=()):
    piece = SHAPE(parts[0].shape, parts[0].dtype)
    own, beside, across = parts[:3]
    across, beside = line(join_kernel, "join", [piece] * 2, [], [across, came[0], beside], (), after)
    return [own, flip(across, 4, 2), flip(beside, 4, 1), *came[1:]]


def core_swap(v, replicas):
    return lax.ppermute(v, "dp", [(a, a ^ 1) for a in range(replicas)])


def axis_swap(v, replicas, step):
    levels = replicas.bit_length() - 2
    pairs = [(a, a ^ (1 << (1 + step if a & 1 else levels - step))) for a in range(replicas)]
    return lax.ppermute(v, "dp", pairs)


def local(replicas, shards, inputs, out_grad, weights, block_index, block_counts, first_moment, second_moment):
    capacity, size = weights.shape[1], weights.shape[2]
    rows, width = inputs.shape
    me = jnp.stack([lax.axis_index("tensor"), lax.axis_index("dp")]).astype(jnp.int32)
    plan = (jnp.concatenate([me, block_counts[0], block_index.reshape(-1)]),)
    features = shards * width // size
    places, share = replicas // 2, capacity // replicas
    levels = places.bit_length() - 1
    held = pltpu.VMEM((shards, rows, width), BF16)
    acc = pltpu.VMEM((HB_DEV + 1, rows, size), F32)
    total = pltpu.VMEM((features + 1, rows, size), F32)
    wide = SHAPE((HB_DEV, rows, size), F32)
    narrow = SHAPE((HB_DEV, rows, size), BF16)
    turned = SHAPE((HB_DEV, size, rows), BF16)
    piece = SHAPE((rows, width), BF16)
    line = Line()
    lined = shards == 4

    def gather(v, form):
        return form(v) if lined else [lax.all_gather(v, "tensor", axis=0)]

    def parts_of(count):
        return [piece] * count if lined else [SHAPE((shards, rows, width), BF16)]

    def grads(matrix, right, left, after=()):
        half = SHAPE((places, share, size, size), BF16)
        name = ("gate_grads", "up_grads", "down_grads")[matrix]
        kernel = functools.partial(grads_kernel, matrix, len(right))
        keep, send = line(kernel, name, [half, half], [held], [*right, left], plan, after)
        return keep, core_swap(send, replicas)

    def fold(keep, got, step, after=()):
        half = SHAPE((keep.shape[0] // 2, *keep.shape[1:]), BF16)
        keep, send = line(fold_kernel, "fold", [half, half], [], [keep, got], (), after)
        return keep, axis_swap(send, replicas, step)

    def update(matrix, keep, got, buffer):
        block = pl.BlockSpec((1, share, size, size), lambda i: (matrix, 0, 0, 0))
        extra = [] if buffer is None else [buffer]
        return line(
            functools.partial(update_kernel, matrix),
            "update",
            [SHAPE(first_moment.shape, F32)],
            [],
            [keep, got, first_moment, second_moment, *extra],
            plan,
            specs=[VMEM, VMEM, block, block] + [ANY] * len(extra),
            out_specs=[block],
            input_output_aliases={5: 0} if extra else {},
            grid=(1,),
        )[0]

    def finish(held_parts):
        return line(sum_kernel, "finish", [piece], [], held_parts)[0]

    def touch(*arrived):
        line(lambda: None, "touch", [], [], [], (), arrived)

    x = gather(inputs, gather_near)
    if lined:
        (order,) = line(
            functools.partial(order_kernel, width // size, capacity), "order",
            [SHAPE((2 * capacity + 2,), jnp.int32)], [], [], plan, out_specs=[SMEM],
        )
    if lined:
        (out_grad,) = line(hold_kernel, "hold", [piece], [], [out_grad, x[2]])
    og = gather(out_grad, gather_line)
    out_parts, in_parts = parts_of(5), parts_of(4)
    hidden, hidden_turned, act, slope, *out_parts = line(
        functools.partial(forward_kernel, len(x), len(out_parts)),
        "forward",
        [narrow, turned, wide, wide, *out_parts],
        [held, acc, acc, total],
        [*x, weights],
        plan,
    )
    if lined:
        out_far = scatter_first(out_parts)
    else:
        outputs = lax.psum_scatter(out_parts[0], "tensor", scatter_dimension=0)
    (x_turned,) = line(
        functools.partial(turn_kernel, len(x)), "turn", [SHAPE((features, size, rows), BF16)], [held], x, plan
    )
    buffer = None
    if lined:
        out_sums = scatter_second(line, out_parts, out_far)
    down = grads(2, og, hidden_turned)
    gate_rows, up_rows = line(
        functools.partial(rows_kernel, len(og)),
        "row_grads",
        [narrow, narrow],
        [held, acc],
        [*og, weights, act, slope],
        plan,
    )
    down = fold(*down, 0)
    if lined:
        part_total = pltpu.VMEM((width // size + 1, rows, size), F32)
        in_operands = [gate_rows, up_rows, weights]
        (in_far,) = line(
            functools.partial(input_part_kernel, True), "input_far", [piece], [part_total], in_operands, (*plan, order)
        )
        in_far = flip(in_far, 4, 1)
    if lined:
        in_parts = line(
            functools.partial(input_part_kernel, False), "input_rest", [piece] * 3, [total], in_operands, (*plan, order)
        )
    else:
        in_parts = line(
            functools.partial(input_kernel, 1), "input_grads", in_parts, [total], [gate_rows, up_rows, weights], plan
        )
        input_grad = lax.psum_scatter(in_parts[0], "tensor", scatter_dimension=0)
    gate = grads(0, [gate_rows], x_turned, out_far[1:] if lined else ())
    for step in range(1, levels):
        down = fold(*down, step)
    if lined:
        outputs = finish(out_sums)
    gate = fold(*gate, 0)
    up = grads(1, [up_rows], x_turned)
    buffer = update(2, *down, buffer)
    if lined:
        in_sums = scatter_second(line, in_parts, [in_far])
    up = fold(*up, 0)
    for step in range(1, levels):
        gate = fold(*gate, step)
    for step in range(1, levels):
        up = fold(*up, step)
    buffer = update(0, *gate, buffer)
    if lined:
        input_grad = finish(in_sums)
    buffer = update(1, *up, buffer)
    return (outputs, input_grad, buffer)


def solution(mesh):
    in_specs = (
        P("dp", "tensor"),
        P("dp", "tensor"),
        P(None, "tensor", None, None),
        P(None, "tensor", None),
        P("tensor", None),
        P(None, ("tensor", "dp"), None, None),
        P(None, ("tensor", "dp"), None, None),
    )
    out_specs = (P("dp", "tensor"), P("dp", "tensor"), P(None, ("tensor", "dp"), None, None))
    body = functools.partial(local, mesh.shape["dp"], mesh.shape["tensor"])
    return jax.shard_map(body, mesh=mesh, in_specs=in_specs, out_specs=out_specs, check_vma=False)
```

```python
import functools
import jax
import jax.numpy as jnp
from jax import lax
from jax.experimental import pallas as pl
from jax.experimental.pallas import tpu as pltpu
from jax.sharding import PartitionSpec as P

HB_DEV = 14
EPSILON = 1e-08
GROUPS = (32, 8)
COST = 2 * 10**10
VMEM_LIMIT = 32 * 1024 * 1024
F32, BF16 = jnp.float32, jnp.bfloat16
SHAPE = jax.ShapeDtypeStruct
SMEM = pl.BlockSpec(memory_space=pltpu.SMEM)
VMEM = pl.BlockSpec(memory_space=pltpu.VMEM)
ANY = pl.BlockSpec(memory_space=pl.ANY)
TOKEN = SHAPE((8, 128), F32)
HEAD = 5


def feature_block(ref, block, size):
    per_shard = ref.shape[2] // size
    start = pl.multiple_of(lax.rem(block, per_shard) * size, size)
    return ref.at[lax.div(block, per_shard), :, pl.ds(start, size)]


def slot_pair(plan_ref, matrix, slot, capacity):
    at = HEAD + (matrix * capacity + slot) * 2
    return plan_ref[at], plan_ref[at + 1]


def each_group(first, last, body):
    large, small = GROUPS

    def run(at, size, count, whole):
        def step(i, carry):
            body([at + i * size + u for u in range(size)], whole)
            return carry

        lax.fori_loop(0, count, step, 0)

    full = lax.div(last - first, large)
    rest = first + full * large
    run(first, large, full, True)
    run(rest, small, lax.div(last - rest + (small - 1), small), False)


def dot(a, b, contract):
    return lax.dot_general(a, b, (contract, ((), ())), preferred_element_type=F32)


def accumulate(plan_ref, matrix, capacity, acc, into, product, order=None, base=0):
    trash = acc.shape[0] - 1
    order_ref, first, last = order or (None, 0, plan_ref[2 + matrix])

    def body(places, whole):
        products, targets = [], []
        for p in places:
            here = p if whole else jnp.minimum(p, last - 1)
            s = here if order is None else order_ref[here]
            pair = slot_pair(plan_ref, matrix, s, capacity)
            target = pair[into] - base
            targets.append(target if whole else jnp.where(p < last, target, trash))
            products.append(product(s, *pair))
        for t, p in zip(targets, products):
            acc[t] += p

    each_group(first, last, body)


def order_kernel(per_shard, capacity, plan_ref, order_ref):
    far = lax.bitwise_xor(plan_ref[0], 3)
    for matrix in (0, 1):

        def is_far(s, matrix=matrix):
            return lax.div(slot_pair(plan_ref, matrix, s, capacity)[0], per_shard) == far

        def count(s, total):
            return total + is_far(s).astype(jnp.int32)

        def put(s, at):
            here, there = at
            found = is_far(s)
            order_ref[matrix * capacity + jnp.where(found, here, there)] = s
            step = found.astype(jnp.int32)
            return here + step, there + 1 - step

        live = plan_ref[2 + matrix]
        total = lax.fori_loop(0, live, count, 0)
        order_ref[2 * capacity + matrix] = total
        lax.fori_loop(0, live, put, (0, total))


def load_shards(pieces, held, me):
    if len(pieces) == 1:
        return pieces[0]
    if len(pieces) == 4:
        for offset, piece in enumerate(pieces):
            held[lax.bitwise_xor(me, offset)] = piece[...]
        return held
    own, below, above, across, far = pieces
    last = held.shape[0] - 1
    held[me] = own[...]
    held[lax.bitwise_xor(me, 2)] = across[...]

    @pl.when(me > 0)
    def _():
        held[me - 1] = below[...]

    @pl.when(me < last)
    def _():
        held[me + 1] = above[...]

    @pl.when((me == 0) | (me == last))
    def _():
        held[last - me] = far[...]

    return held


def store_shards(total, outs, me, per_shard, size):
    if len(outs) == 1:
        places = [(outs[0].at[t], t) for t in range(outs[0].shape[0])]
    elif len(outs) == 4:
        places = [(out, lax.bitwise_xor(me, offset)) for offset, out in enumerate(outs)]
    else:
        last = 3
        own, beside, across, far, middle = outs
        places = [(out, lax.bitwise_xor(me, offset)) for offset, out in enumerate((own, beside, across, far))]
        places.append((middle, last - me))
    for out, t in places:
        for c in range(per_shard):
            out[:, c * size : (c + 1) * size] = total[t * per_shard + c].astype(out.dtype)


def forward_kernel(n_pieces, n_outs, plan_ref, *refs):
    pieces, refs = refs[:n_pieces], refs[n_pieces:]
    w_ref, hidden_ref, turned_ref, act_ref, slope_ref = refs[:5]
    outs, (held, gate, up, total) = refs[5 : 5 + n_outs], refs[5 + n_outs :]
    me = plan_ref[0]
    x_ref = load_shards(pieces, held, me)
    capacity, size = w_ref.shape[1], w_ref.shape[2]
    gate[...] = jnp.zeros_like(gate)
    up[...] = jnp.zeros_like(up)
    total[...] = jnp.zeros_like(total)
    for matrix, acc in ((0, gate), (1, up)):
        accumulate(
            plan_ref, matrix, capacity, acc, 1,
            lambda s, f, h, matrix=matrix: dot(feature_block(x_ref, f, size)[...], w_ref[matrix, s], ((1,), (0,))),
        )
    for h in range(hidden_ref.shape[0]):
        g, u = gate[h], up[h]
        sig = 1.0 / (1.0 + jnp.exp(-g))
        act = g * sig
        act_ref[h] = act
        slope_ref[h] = u * sig * (1.0 + g * (1.0 - sig))
        hidden = (act * u).astype(hidden_ref.dtype)
        hidden_ref[h] = hidden
        turned_ref[h] = hidden.T
    accumulate(
        plan_ref, 2, capacity, total, 0,
        lambda s, f, h: dot(hidden_ref[h], w_ref[2, s], ((1,), (0,))),
    )
    store_shards(total, outs, me, x_ref.shape[2] // size, size)


def turn_kernel(n_pieces, plan_ref, *refs):
    pieces, (turned_ref, held) = refs[:n_pieces], refs[n_pieces:]
    x_ref = load_shards(pieces, held, plan_ref[0])
    size = turned_ref.shape[1]
    per_shard = x_ref.shape[2] // size
    for f in range(turned_ref.shape[0]):
        c = f % per_shard
        turned_ref[f] = x_ref[f // per_shard, :, c * size : (c + 1) * size].T


def rows_kernel(n_pieces, plan_ref, *refs):
    pieces, refs = refs[:n_pieces], refs[n_pieces:]
    w_ref, act_ref, slope_ref, gate_rows_ref, up_rows_ref, held, acc = refs
    og_ref = load_shards(pieces, held, plan_ref[0])
    capacity, size = w_ref.shape[1], w_ref.shape[2]
    acc[...] = jnp.zeros_like(acc)
    accumulate(
        plan_ref, 2, capacity, acc, 1,
        lambda s, f, h: dot(feature_block(og_ref, f, size)[...], w_ref[2, s], ((1,), (1,))),
    )
    for h in range(act_ref.shape[0]):
        gate_rows_ref[h] = (acc[h] * slope_ref[h]).astype(gate_rows_ref.dtype)
        up_rows_ref[h] = (acc[h] * act_ref[h]).astype(up_rows_ref.dtype)


def spread(place, core, places):
    levels = places.bit_length() - 1
    turned = sum(lax.shift_left(lax.bitwise_and(lax.shift_right_logical(place, b), 1), levels - 1 - b) for b in range(levels))
    return 2 * jnp.where(core == 0, place, turned)


def grads_kernel(matrix, n_pieces, plan_ref, *refs):
    pieces, refs = refs[:n_pieces], refs[n_pieces:]
    turned_ref, keep_ref, send_ref, held = refs
    size, share = keep_ref.shape[2], keep_ref.shape[1]
    places = keep_ref.shape[0]
    replica = plan_ref[1]
    right_ref = load_shards(pieces, held, plan_ref[0])
    capacity = 2 * places * share
    count = plan_ref[2 + matrix]

    def one_place(q, carry):
        todo = []
        for out, bit in ((send_ref, 1), (keep_ref, 0)):
            owner = lax.bitwise_xor(replica, bit)
            todo.append((out, lax.bitwise_xor(owner, spread(q, lax.bitwise_and(owner, 1), places)) * share))

        @pl.when(jnp.minimum(todo[0][1], todo[1][1]) < count)
        def _():
            for out, first in todo:
                for s in range(share):
                    f, h = slot_pair(plan_ref, matrix, first + s, capacity)
                    if matrix == 2:
                        left, right = turned_ref[h], feature_block(right_ref, f, size)[...]
                    else:
                        left, right = turned_ref[f], right_ref[h]
                    out[q, s] = dot(left, right, ((1,), (0,))).astype(out.dtype)

        return carry

    lax.fori_loop(0, places, one_place, 0)


def input_kernel(n_outs, plan_ref, gate_rows_ref, up_rows_ref, w_ref, *refs):
    outs, (total,) = refs[:n_outs], refs[n_outs:]
    capacity, size = w_ref.shape[1], w_ref.shape[2]
    total[...] = jnp.zeros_like(total)
    for matrix, rows in ((0, gate_rows_ref), (1, up_rows_ref)):
        accumulate(
            plan_ref, matrix, capacity, total, 0,
            lambda s, f, h, matrix=matrix, rows=rows: dot(rows[h], w_ref[matrix, s], ((1,), (1,))),
        )
    store_shards(total, outs, plan_ref[0], outs[0].shape[-1] // size, size)


def input_part_kernel(is_far, plan_ref, order_ref, gate_rows_ref, up_rows_ref, w_ref, *refs):
    *outs, total = refs
    capacity, size = w_ref.shape[1], w_ref.shape[2]
    per_shard = outs[0].shape[-1] // size
    me = plan_ref[0]
    base = lax.bitwise_xor(me, 3) * per_shard if is_far else 0
    total[...] = jnp.zeros_like(total)
    for matrix, rows in ((0, gate_rows_ref), (1, up_rows_ref)):
        at = matrix * capacity
        cut = at + order_ref[2 * capacity + matrix]
        accumulate(
            plan_ref, matrix, capacity, total, 0,
            lambda s, f, h, matrix=matrix, rows=rows: dot(rows[h], w_ref[matrix, s], ((1,), (1,))),
            (order_ref, at, cut) if is_far else (order_ref, cut, at + plan_ref[2 + matrix]),
            base,
        )
    for offset, out in enumerate(outs):
        first = 0 if is_far else lax.bitwise_xor(me, offset) * per_shard
        for c in range(per_shard):
            out[:, c * size : (c + 1) * size] = total[first + c].astype(out.dtype)


def fold_kernel(keep_ref, got_ref, keep_out, send_out):
    half = keep_out.shape[0]
    keep_out[...] = keep_ref[:half] + got_ref[:half]
    send_out[...] = keep_ref[half:] + got_ref[half:]


def join_kernel(*refs):
    ins, outs = refs[: len(refs) // 2 + 1], refs[len(refs) // 2 + 1 :]
    outs[0][...] = ins[0][...] + ins[1][...]
    for source, out in zip(ins[2:], outs[1:]):
        out[...] = source[...]


def sum_kernel(*refs):
    *parts, out_ref = refs
    total = parts[0][...].astype(F32)
    for part in parts[1:]:
        total += part[...].astype(F32)
    out_ref[...] = total.astype(out_ref.dtype)


def update_kernel(matrix, plan_ref, keep_ref, got_ref, m1_ref, m2_ref, *refs):
    out_ref = refs[-1]
    share = keep_ref.shape[1]
    first = plan_ref[1] * share
    for s in range(share):
        g = keep_ref[0, s].astype(F32) + got_ref[0, s].astype(F32)
        first_new = 0.9 * m1_ref[0, s] + 0.1 * g
        second_new = 0.95 * m2_ref[0, s] + 0.05 * g * g
        live = first + s < plan_ref[2 + matrix]
        out_ref[0, s] = jnp.where(live, first_new / (jnp.sqrt(second_new) + EPSILON), 0.0)


def hold_kernel(v_ref, _, out_ref):
    out_ref[...] = v_ref[...]


class Line:
    token = None

    def __call__(self, kernel, name, outs, scratch, operands, plan=(), after=(), specs=None, out_specs=None, cost=COST, **more):
        scalars = [*plan]
        extra = [*after] if self.token is None else [*after, self.token]
        n_in, n_out = len(scalars) + len(operands), len(outs)

        def body(*refs):
            ins, rest = refs[:n_in], refs[n_in + len(extra) :]
            results, token, scratches = rest[:n_out], rest[n_out], rest[n_out + 1 :]
            token[...] = jnp.zeros_like(token)
            kernel(*ins, *results, *scratches)

        *results, self.token = pl.pallas_call(
            body,
            name=name,
            out_shape=[*outs, TOKEN],
            in_specs=[SMEM] * len(scalars) + (specs or [VMEM] * len(operands)) + [VMEM] * len(extra),
            out_specs=[*(out_specs or [VMEM] * n_out), VMEM],
            scratch_shapes=scratch,
            compiler_params=pltpu.CompilerParams(vmem_limit_bytes=VMEM_LIMIT),
            cost_estimate=pl.CostEstimate(flops=cost, bytes_accessed=0, transcendentals=0),
            **more,
        )(*scalars, *operands, *extra)
        return results


def flip(v, shards, bit):
    return lax.ppermute(v, "tensor", [(a, a ^ bit) for a in range(shards)])


def gather_near(v):
    across, beside = flip(v, 4, 2), flip(v, 4, 1)
    return [v, beside, across, flip(across, 4, 1)]


def gather_line(v):
    across = flip(v, 4, 2)
    below = lax.ppermute(v, "tensor", [(a, a + 1) for a in range(3)])
    above = lax.ppermute(v, "tensor", [(a + 1, a) for a in range(3)])
    far = lax.ppermute(across, "tensor", [(2, 3), (1, 0)])
    return [v, below, above, across, far]


def scatter_first(parts):
    return [lax.ppermute(parts[3], "tensor", [(0, 1), (3, 2)]), lax.ppermute(parts[4], "tensor", [(1, 2), (2, 1)])]


def scatter_second(line, parts, came, after=()):
    piece = SHAPE(parts[0].shape, parts[0].dtype)
    own, beside, across = parts[:3]
    across, beside = line(join_kernel, "join", [piece] * 2, [], [across, came[0], beside], (), after)
    return [own, flip(across, 4, 2), flip(beside, 4, 1), *came[1:]]


def core_swap(v, replicas):
    return lax.ppermute(v, "dp", [(a, a ^ 1) for a in range(replicas)])


def axis_swap(v, replicas, step):
    levels = replicas.bit_length() - 2
    pairs = [(a, a ^ (1 << (1 + step if a & 1 else levels - step))) for a in range(replicas)]
    return lax.ppermute(v, "dp", pairs)


def local(replicas, shards, inputs, out_grad, weights, block_index, block_counts, first_moment, second_moment):
    capacity, size = weights.shape[1], weights.shape[2]
    rows, width = inputs.shape
    me = jnp.stack([lax.axis_index("tensor"), lax.axis_index("dp")]).astype(jnp.int32)
    plan = (jnp.concatenate([me, block_counts[0], block_index.reshape(-1)]),)
    features = shards * width // size
    places, share = replicas // 2, capacity // replicas
    levels = places.bit_length() - 1
    held = pltpu.VMEM((shards, rows, width), BF16)
    acc = pltpu.VMEM((HB_DEV + 1, rows, size), F32)
    total = pltpu.VMEM((features + 1, rows, size), F32)
    wide = SHAPE((HB_DEV, rows, size), F32)
    narrow = SHAPE((HB_DEV, rows, size), BF16)
    turned = SHAPE((HB_DEV, size, rows), BF16)
    piece = SHAPE((rows, width), BF16)
    line = Line()
    lined = shards == 4

    def gather(v, form):
        return form(v) if lined else [lax.all_gather(v, "tensor", axis=0)]

    def parts_of(count):
        return [piece] * count if lined else [SHAPE((shards, rows, width), BF16)]

    def grads(matrix, right, left, after=()):
        half = SHAPE((places, share, size, size), BF16)
        name = ("gate_grads", "up_grads", "down_grads")[matrix]
        kernel = functools.partial(grads_kernel, matrix, len(right))
        keep, send = line(kernel, name, [half, half], [held], [*right, left], plan, after)
        return keep, core_swap(send, replicas)

    def fold(keep, got, step, after=()):
        half = SHAPE((keep.shape[0] // 2, *keep.shape[1:]), BF16)
        keep, send = line(fold_kernel, "fold", [half, half], [], [keep, got], (), after)
        return keep, axis_swap(send, replicas, step)

    def update(matrix, keep, got, buffer):
        block = pl.BlockSpec((1, share, size, size), lambda i: (matrix, 0, 0, 0))
        extra = [] if buffer is None else [buffer]
        return line(
            functools.partial(update_kernel, matrix),
            "update",
            [SHAPE(first_moment.shape, F32)],
            [],
            [keep, got, first_moment, second_moment, *extra],
            plan,
            specs=[VMEM, VMEM, block, block] + [ANY] * len(extra),
            out_specs=[block],
            input_output_aliases={5: 0} if extra else {},
            grid=(1,),
        )[0]

    def finish(held_parts):
        return line(sum_kernel, "finish", [piece], [], held_parts)[0]

    def touch(*arrived):
        line(lambda: None, "touch", [], [], [], (), arrived)

    x = gather(inputs, gather_near)
    if lined:
        (order,) = line(
            functools.partial(order_kernel, width // size, capacity), "order",
            [SHAPE((2 * capacity + 2,), jnp.int32)], [], [], plan, out_specs=[SMEM],
        )
    if lined:
        (out_grad,) = line(hold_kernel, "hold", [piece], [], [out_grad, x[2]])
    og = gather(out_grad, gather_line)
    out_parts, in_parts = parts_of(5), parts_of(4)
    hidden, hidden_turned, act, slope, *out_parts = line(
        functools.partial(forward_kernel, len(x), len(out_parts)),
        "forward",
        [narrow, turned, wide, wide, *out_parts],
        [held, acc, acc, total],
        [*x, weights],
        plan,
    )
    if lined:
        out_far = scatter_first(out_parts)
    else:
        outputs = lax.psum_scatter(out_parts[0], "tensor", scatter_dimension=0)
    (x_turned,) = line(
        functools.partial(turn_kernel, len(x)), "turn", [SHAPE((features, size, rows), BF16)], [held], x, plan
    )
    buffer = None
    if lined:
        out_sums = scatter_second(line, out_parts, out_far)
    down = grads(2, og, hidden_turned)
    gate_rows, up_rows = line(
        functools.partial(rows_kernel, len(og)),
        "row_grads",
        [narrow, narrow],
        [held, acc],
        [*og, weights, act, slope],
        plan,
    )
    down = fold(*down, 0)
    if lined:
        part_total = pltpu.VMEM((width // size + 1, rows, size), F32)
        in_operands = [gate_rows, up_rows, weights]
        (in_far,) = line(
            functools.partial(input_part_kernel, True), "input_far", [piece], [part_total], in_operands, (*plan, order)
        )
        in_far = flip(in_far, 4, 1)
    gate = grads(0, [gate_rows], x_turned, out_far[1:] if lined else ())
    if lined:
        in_parts = line(
            functools.partial(input_part_kernel, False), "input_rest", [piece] * 3, [total], in_operands, (*plan, order)
        )
    else:
        in_parts = line(
            functools.partial(input_kernel, 1), "input_grads", in_parts, [total], [gate_rows, up_rows, weights], plan
        )
        input_grad = lax.psum_scatter(in_parts[0], "tensor", scatter_dimension=0)
    for step in range(1, levels):
        down = fold(*down, step)
    if lined:
        outputs = finish(out_sums)
    gate = fold(*gate, 0)
    up = grads(1, [up_rows], x_turned)
    buffer = update(2, *down, buffer)
    if lined:
        in_sums = scatter_second(line, in_parts, [in_far])
    up = fold(*up, 0)
    for step in range(1, levels):
        gate = fold(*gate, step)
    for step in range(1, levels):
        up = fold(*up, step)
    buffer = update(0, *gate, buffer)
    if lined:
        input_grad = finish(in_sums)
    buffer = update(1, *up, buffer)
    return (outputs, input_grad, buffer)


def solution(mesh):
    in_specs = (
        P("dp", "tensor"),
        P("dp", "tensor"),
        P(None, "tensor", None, None),
        P(None, "tensor", None),
        P("tensor", None),
        P(None, ("tensor", "dp"), None, None),
        P(None, ("tensor", "dp"), None, None),
    )
    out_specs = (P("dp", "tensor"), P("dp", "tensor"), P(None, ("tensor", "dp"), None, None))
    body = functools.partial(local, mesh.shape["dp"], mesh.shape["tensor"])
    return jax.shard_map(body, mesh=mesh, in_specs=in_specs, out_specs=out_specs, check_vma=False)
```
